32 devices in a mesh: pipe: 2 (over x), dp: 16 (over z, y, core).
Axes of the slice: x: 2, y: 2, z: 4, core: 2. Of those that a mesh axis runs over, the one named last changes fastest.
Arguments:
- inputs: bfloat16 [64, 256, 768], P('dp'), may hold values from -6 to 6
- cotangent: bfloat16 [64, 256, 768], P('dp'), may hold values from -6 to 6
- lengths: int32 [64], P('dp'), may hold values from 128 to 256, as said below
- norm1_gain: float32 [2, 768], P('pipe'), may hold values from 0.5 to 1.5
- norm1_bias: float32 [2, 768], P('pipe'), may hold values from -1 to 1
- qkv_weight: bfloat16 [2, 768, 2304], P('pipe'), may hold values from -0.21875 to 0.21875
- qkv_bias: float32 [2, 2304], P('pipe'), may hold values from -1 to 1
- dense_weight: bfloat16 [2, 768, 768], P('pipe'), may hold values from -1.25 to 1.25
- dense_bias: float32 [2, 768], P('pipe'), may hold values from -1 to 1
- norm2_gain: float32 [2, 768], P('pipe'), may hold values from 0.5 to 1.5
- norm2_bias: float32 [2, 768], P('pipe'), may hold values from -1 to 1
- fc_in_weight: bfloat16 [2, 768, 3072], P('pipe'), may hold values from -0.21875 to 0.21875
- fc_in_bias: float32 [2, 3072], P('pipe'), may hold values from -1 to 1
- fc_out_weight: bfloat16 [2, 3072, 768], P('pipe'), may hold values from -0.109375 to 0.109375
- fc_out_bias: float32 [2, 768], P('pipe'), may hold values from -1 to 1
Outputs:
- layer_outputs: bfloat16 [2, 64, 256, 768], P('pipe', 'dp')
- input_grads: bfloat16 [2, 64, 256, 768], P('pipe', 'dp')
- grad_norm1_gain: float32 [2, 768], P('pipe')
- grad_norm1_bias: float32 [2, 768], P('pipe')
- grad_qkv_weight: float32 [2, 768, 2304], P('pipe')
- grad_qkv_bias: float32 [2, 2304], P('pipe')
- grad_dense_weight: float32 [2, 768, 768], P('pipe')
- grad_dense_bias: float32 [2, 768], P('pipe')
- grad_norm2_gain: float32 [2, 768], P('pipe')
- grad_norm2_bias: float32 [2, 768], P('pipe')
- grad_fc_in_weight: float32 [2, 768, 3072], P('pipe')
- grad_fc_in_bias: float32 [2, 3072], P('pipe')
- grad_fc_out_weight: float32 [2, 3072, 768], P('pipe')
- grad_fc_out_bias: float32 [2, 768], P('pipe')
- example_norms: float32 [64], P('dp')
The draws below stay inside these ranges and needn't reach their ends.
Inputs may be any that keep to these rules, and one draw needn't show every extreme that they name: `lengths`: each sequence has between 128 and 256 tokens; in every draw some sequence has exactly 256.
All inputs are finite; a program needn't handle non-finite values.
Results may differ from the reference program's by a relative error of at most 0.017.
Values may be sent and summed in bfloat16 or wider, within the bound.
A program may use at most 256 MiB of HBM per device.

```python
import jax
import jax.numpy as jnp
from jax import lax

D = 768
HEADS = 12
HEAD = 64
ROT = 16
FF = 3072
LAYERS = 2
SEQ = 256
MIN_LEN = 128
EXAMPLES = 64


def draw_lengths(key, part):
    key = jax.random.fold_in(key, 11)
    key_base, key_top = jax.random.split(key)
    spread = jax.random.randint(key_base, (EXAMPLES,), 0, 1024)
    span = SEQ - MIN_LEN
    lengths = MIN_LEN + span * spread * spread // (1024 * 1024)
    chosen = jax.random.randint(key_top, (), 0, EXAMPLES)
    return jnp.where(jnp.arange(EXAMPLES) == chosen, SEQ, lengths).astype(jnp.int32)


def shard_levels(own_key, dims, shards, smallest, largest):
    level, own = 1.0, jax.random.fold_in(own_key, 6)
    for dim, shards_of in shards:
        heights = jnp.exp(jax.random.uniform(jax.random.fold_in(own, dim), (shards_of,), jnp.float32, smallest / len(shards), largest / len(shards)))
        level = level * jnp.repeat(heights, dims[dim] // shards_of).reshape([-1 if axis == dim else 1 for axis in range(len(dims))])
    return level


def centred(own_key, shape, width, bound, shards=(), held_as=jnp.bfloat16):
    values = jax.random.normal(own_key, shape, jnp.float32) * width
    if len(shards) > 0:
        values = shard_levels(own_key, shape, shards, -0.22, 0.18) * values
    return jnp.clip(values, min=-bound, max=bound).astype(held_as)


def setup_inputs(seed: int = 0) -> dict:
    seeds = jax.random.split(jax.random.key(seed), 16)
    return {
        "inputs": centred(seeds[0], (EXAMPLES, SEQ, D), 1.0, 6.0, ((0, 16),)),
        "cotangent": centred(seeds[1], (EXAMPLES, SEQ, D), 1.0, 6.0, ((0, 16),)),
        "lengths": draw_lengths(jax.random.fold_in(seeds[15], 71), 0),
        "norm1_gain": jnp.clip(1.0 + 0.1 * jax.random.normal(seeds[3], (LAYERS, D), jnp.float32), 0.5, 1.5),
        "norm1_bias": centred(seeds[4], (LAYERS, D), 0.2, 1.0, ((0, 2),), jnp.float32),
        "qkv_weight": centred(seeds[5], (LAYERS, D, 3 * D), D ** -0.5, 0.21875, ((0, 2),)),
        "qkv_bias": centred(seeds[6], (LAYERS, 3 * D), 0.2, 1.0, ((0, 2),), jnp.float32),
        "dense_weight": centred(seeds[7], (LAYERS, D, D), (D // 32) ** -0.5, 1.25, ((0, 2),)),
        "dense_bias": centred(seeds[8], (LAYERS, D), 0.2, 1.0, ((0, 2),), jnp.float32),
        "norm2_gain": jnp.clip(1.0 + 0.1 * jax.random.normal(seeds[9], (LAYERS, D), jnp.float32), 0.5, 1.5),
        "norm2_bias": centred(seeds[10], (LAYERS, D), 0.2, 1.0, ((0, 2),), jnp.float32),
        "fc_in_weight": centred(seeds[11], (LAYERS, D, FF), D ** -0.5, 0.21875, ((0, 2),)),
        "fc_in_bias": centred(seeds[12], (LAYERS, FF), 0.2, 1.0, ((0, 2),), jnp.float32),
        "fc_out_weight": centred(seeds[13], (LAYERS, FF, D), FF ** -0.5, 0.109375, ((0, 2),)),
        "fc_out_bias": centred(seeds[14], (LAYERS, D), 0.2, 1.0, ((0, 2),), jnp.float32),
    }


HIGH = lax.Precision.HIGHEST
NEG_FILL = -1e+30

@jax.custom_vjp
def low(v):
    return lax.optimization_barrier(v.astype(jnp.bfloat16)).astype(jnp.float32)

@jax.custom_vjp
def low_back(v):
    return v

def low_keep(v):
    return (low(v), None)

def low_pass(kept, grad):
    return (grad,)

def back_keep(v):
    return (v, None)

def back_low(kept, grad):
    return (low(grad),)
low.defvjp(low_keep, low_pass)
low_back.defvjp(back_keep, back_low)

def norm_rows(values, gain, shift):
    center = values - lax.optimization_barrier(jnp.mean(values, axis=-1, keepdims=True))
    spread = lax.optimization_barrier(jnp.mean(center * center, axis=-1, keepdims=True))
    return center * lax.rsqrt(spread + 1e-05) * gain + shift

def rotary_tables(seq_len):
    half = ROT // 2
    freq = jnp.power(10000.0, -(2.0 * jnp.arange(half, dtype=jnp.float32)) / ROT)
    angle = jnp.arange(seq_len, dtype=jnp.float32)[:, None] * freq[None, :]
    return (jnp.cos(angle)[:, None, :], jnp.sin(angle)[:, None, :])

def rotate(values, cosine, sine):
    half = ROT // 2
    first = values[..., :half]
    second = values[..., half:ROT]
    return jnp.concatenate([first * cosine - second * sine, second * cosine + first * sine, values[..., ROT:]], axis=-1)

def layer(inp, params, length):
    gain1, shift1, w_qkv, b_qkv, w_dense, b_dense, gain2, shift2, w_in, b_in, w_out, b_out = params
    seq_len = inp.shape[0]
    cosine, sine = rotary_tables(seq_len)
    normed1 = low(norm_rows(inp, gain1, shift1))
    mixed = low_back(jnp.dot(normed1, w_qkv, precision=HIGH) + b_qkv).reshape(seq_len, 3, HEADS, HEAD)
    query = low(rotate(mixed[:, 0], cosine, sine))
    key_rot = low(rotate(mixed[:, 1], cosine, sine))
    value = low(mixed[:, 2])
    scores = low_back(jnp.einsum('qhd,khd->hqk', query, key_rot, precision=HIGH) * HEAD ** (-0.5))
    positions = jnp.arange(seq_len)
    allowed = (positions[None, :] <= positions[:, None]) & (positions[None, :] < length)
    probs = low(jax.nn.softmax(jnp.where(allowed[None], scores, NEG_FILL), axis=-1))
    context = low(low_back(jnp.einsum('hqk,khd->qhd', probs, value, precision=HIGH).reshape(seq_len, D)))
    attended = jnp.dot(context, w_dense, precision=HIGH) + b_dense
    normed2 = low(norm_rows(inp, gain2, shift2))
    hidden = low_back(jnp.dot(normed2, w_in, precision=HIGH) + b_in)
    activated = low(jax.nn.gelu(hidden, approximate=False))
    return inp + attended + jnp.dot(activated, w_out, precision=HIGH) + b_out

def reference(inputs, cotangent, lengths, norm1_gain, norm1_bias, qkv_weight, qkv_bias, dense_weight, dense_bias, norm2_gain, norm2_bias, fc_in_weight, fc_in_bias, fc_out_weight, fc_out_bias):
    stacked = tuple((w.astype(jnp.float32) for w in (norm1_gain, norm1_bias, qkv_weight, qkv_bias, dense_weight, dense_bias, norm2_gain, norm2_bias, fc_in_weight, fc_in_bias, fc_out_weight, fc_out_bias)))
    first_layer = tuple((w[0] for w in stacked))
    second_layer = tuple((w[1] for w in stacked))
    positions = jnp.arange(SEQ)

    def one(totals, item):
        tokens, cot, length = item
        mask = (positions < length).astype(jnp.float32)[:, None]

        def both(inp, params0, params1, offset):
            out0 = layer(inp, params0, length)
            handed = low_back(low(out0)) + offset
            return (layer(handed, params1, length), out0)
        offset0 = jnp.zeros((SEQ, D), jnp.float32)
        out1, pull, out0 = jax.vjp(both, tokens.astype(jnp.float32), first_layer, second_layer, offset0, has_aux=True)
        grad_x, grads0, grads1, grad_mid = pull(cot.astype(jnp.float32) * mask)
        paired = tuple((jnp.stack([a, b]) for a, b in zip(grads0, grads1)))
        total = jnp.float32(0.0)
        for leaf in paired:
            total = total + jnp.sum(leaf * leaf)
        totals = tuple((a + b for a, b in zip(totals, paired)))
        outs = jnp.stack([out0, out1]).astype(jnp.bfloat16)
        grads_in = jnp.stack([grad_x, grad_mid]).astype(jnp.bfloat16)
        return (totals, (outs, grads_in, total))
    start = tuple((jnp.zeros_like(w) for w in stacked))
    totals, (outs, grads_in, norms) = lax.scan(one, start, (inputs, cotangent, lengths))
    outs = jnp.transpose(outs, (1, 0, 2, 3))
    grads_in = jnp.transpose(grads_in, (1, 0, 2, 3))
    return (outs, grads_in, totals[0], totals[1], totals[2], totals[3], totals[4], totals[5], totals[6], totals[7], totals[8], totals[9], totals[10], totals[11], norms)
```

```python
import functools

import jax
import jax.numpy as jnp
import numpy as np
from jax import lax
from jax.experimental import pallas as pl
from jax.experimental.pallas import tpu as pltpu
from jax.sharding import PartitionSpec as P

HEADS = 12
HEAD = 64
ROT = 16
EPSILON = 1e-05
NEG_FILL = -1e30
INV_ROOT_TWO = 0.7071067811865476
INV_ROOT_TWO_PI = 0.3989422804014327
MESH = pl.DeviceIdType.MESH
F32 = jnp.float32
BF16 = jnp.bfloat16


def dot_nn(a, b):
    return jnp.dot(a, b, preferred_element_type=F32)


def dot_nt(a, b):
    return lax.dot_general(a, b, (((1,), (1,)), ((), ())), preferred_element_type=F32)


def dot_tn(a, b):
    return lax.dot_general(a, b, (((0,), (0,)), ((), ())), preferred_element_type=F32)


def rotary_tables(seq):
    half = ROT // 2
    freq = 10000.0 ** (-2.0 * np.arange(half) / ROT)
    angle = np.arange(seq)[:, None] * freq[None, :]
    cosine, sine = np.cos(angle), np.sin(angle)
    own = np.ones((seq, HEAD))
    up = np.zeros((seq, HEAD))
    down = np.zeros((seq, HEAD))
    own[:, :half] = cosine
    own[:, half:ROT] = cosine
    up[:, half:ROT] = sine
    down[:, :half] = -sine
    tables = np.stack([np.concatenate([t, t], axis=1) for t in (own, up, down)])
    return tables.astype(np.float32)


def section_kernel(
    n_mb,
    lens,
    inputs,
    cot,
    g1,
    b1,
    wqkv,
    bqkv,
    wd,
    bd,
    g2,
    b2,
    wi,
    bi,
    wo,
    bo,
    tables,
    out_y,
    out_dx,
    a_hbm,
    b_hbm,
    small,
    wqkv_v,
    wd_v,
    wi_v,
    wo_v,
    xb,
    av,
    bv,
    pb,
    yb,
    dxb,
    acc,
    dctx_v,
    bias_v,
    wsem,
    insem,
    cotsem,
    ysem,
    dxsem,
    asem,
    bsem,
    fsend,
    frecv,
    bsend,
    brecv,
):
    section = lax.axis_index("pipe")
    first = section == 0
    last = section == 1
    peer = 1 - section
    seq, d = xb.shape[1], xb.shape[2]
    pairs = d // 128

    wcopies = [
        pltpu.make_async_copy(src.at[0], dst, wsem.at[k])
        for k, (src, dst) in enumerate(((wqkv, wqkv_v), (wd, wd_v), (wi, wi_v), (wo, wo_v)))
    ]

    @pl.when(first)
    def _():
        pltpu.make_async_copy(inputs, xb, insem).start()

    for c in wcopies:
        c.start()

    @pl.when(last)
    def _():
        pltpu.make_async_copy(cot, bv.at[4], cotsem).start()

    barrier = pltpu.get_barrier_semaphore()
    pl.semaphore_signal(barrier, inc=1, device_id={"pipe": peer}, device_id_type=MESH)
    pl.semaphore_wait(barrier, 1)

    def fcopy(i):
        return pltpu.make_async_remote_copy(
            src_ref=yb.at[i],
            dst_ref=xb.at[i],
            send_sem=fsend.at[i],
            recv_sem=frecv.at[i],
            device_id={"pipe": peer},
            device_id_type=MESH,
        )

    def bcopy(i):
        return pltpu.make_async_remote_copy(
            src_ref=dxb.at[i],
            dst_ref=bv.at[4, i],
            send_sem=bsend.at[i],
            recv_sem=brecv.at[i],
            device_id={"pipe": peer},
            device_id_type=MESH,
        )

    lane = lax.broadcasted_iota(jnp.int32, (seq, 128), 1)
    lower = lane < HEAD

    def pick(value, a):
        return jnp.where(lower if a == 0 else jnp.logical_not(lower), value, jnp.zeros_like(value))

    def rotate(w, sign):
        return (
            w * tables[0]
            + sign * (pltpu.roll(w, ROT // 2, 1) * tables[1] + pltpu.roll(w, 128 - ROT // 2, 1) * tables[2])
        )

    def unit_of(i):
        x = xb[i].astype(F32)
        center = x - jnp.mean(x, axis=-1, keepdims=True)
        inverse = lax.rsqrt(jnp.mean(center * center, axis=-1, keepdims=True) + EPSILON)
        return x, center * inverse, inverse

    def forward(i, carry):
        @pl.when(last)
        def _():
            fcopy(i).wait_recv()

        x, unit, inverse = unit_of(i)
        a1 = (unit * g1[...] + b1[...]).astype(BF16)
        a2 = (unit * g2[...] + b2[...]).astype(BF16)
        av[5, i] = a1
        av[0, i] = a2

        @pl.when(i == 0)
        def _():
            wcopies[0].wait()

        for t in range(3):
            mixed = dot_nn(a1, wqkv_v[:, t * d : (t + 1) * d]) + bqkv[:, t * d : (t + 1) * d]
            if t == 2:
                bv[5 + t, i] = mixed.astype(BF16)
            else:
                for hp in range(pairs):
                    w = rotate(mixed[:, hp * 128 : (hp + 1) * 128], 1.0)
                    if t == 0:
                        w = w * HEAD ** (-0.5)
                    bv[5 + t, i, :, hp * 128 : (hp + 1) * 128] = w.astype(BF16)

        key = lax.broadcasted_iota(jnp.int32, (seq, seq), 0)
        query = lax.broadcasted_iota(jnp.int32, (seq, seq), 1)
        bias_v[...] = jnp.where((key <= query) & (key < lens[i]), 0.0, NEG_FILL)

        def attend(hp, carry):
            cols = pl.ds(pl.multiple_of(hp * 128, 128), 128)
            qp, kp, vp = bv[5, i, :, cols], bv[6, i, :, cols], bv[7, i, :, cols]
            ctx = None
            for a in range(2):
                scores = dot_nt(pick(kp, a), qp) + bias_v[...]
                expo = jnp.exp(scores - jnp.max(scores, axis=0, keepdims=True))
                probs = (expo * (1.0 / jnp.sum(expo, axis=0, keepdims=True))).astype(BF16)
                pb[i, 2 * hp + a] = probs
                part = dot_tn(probs, pick(vp, a))
                ctx = part if ctx is None else ctx + part
            av[6, i, :, cols] = ctx.astype(BF16)
            return carry

        lax.fori_loop(0, pairs, attend, 0)

        @pl.when(i == 0)
        def _():
            for k in (1, 2, 3):
                wcopies[k].wait()

        acc[...] = x + dot_nn(av[6, i], wd_v[...]) + bd[...] + bo[...]

        def feed(j, carry):
            cols = pl.ds(pl.multiple_of(j * d, 128), d)
            hidden = dot_nn(av[0, i], wi_v[:, cols]) + bi[:, cols]
            gate = 0.5 * (1.0 + lax.erf(hidden * INV_ROOT_TWO))
            act = (hidden * gate).astype(BF16)
            av[1 + j, i] = act
            bv[j, i] = (gate + hidden * jnp.exp(-0.5 * hidden * hidden) * INV_ROOT_TWO_PI).astype(BF16)
            acc[...] += dot_nn(act, wo_v[pl.ds(pl.multiple_of(j * d, 128), d), :])
            return carry

        lax.fori_loop(0, 4, feed, 0)
        yb[i] = acc[...].astype(BF16)

        @pl.when(first)
        def _():
            fcopy(i).start()

        pltpu.make_async_copy(yb.at[i], out_y.at[0, i], ysem.at[i]).start()
        for k in range(7):
            pltpu.make_async_copy(av.at[k, i], a_hbm.at[k, i], asem.at[k, i]).start()
        return carry

    def backward(i, carry):
        @pl.when(first)
        def _():
            bcopy(i).wait_recv()

        @pl.when(last)
        def _():
            row = lax.broadcasted_iota(jnp.int32, (seq, d), 0)
            value = bv[4, i].astype(F32)
            bv[4, i] = jnp.where(row < lens[i], value, 0.0).astype(BF16)

        gy = bv[4, i]
        small[i, 7:8, :] = jnp.sum(gy.astype(F32), axis=0, keepdims=True)
        acc[...] = jnp.zeros_like(acc)

        def feed(j, carry):
            cols = pl.ds(pl.multiple_of(j * d, 128), d)
            dact = dot_nt(bv[4, i], wo_v[pl.ds(pl.multiple_of(j * d, 128), d), :])
            dh = (dact * bv[j, i].astype(F32)).astype(BF16)
            bv[j, i] = dh
            small[i, pl.ds(8 + j, 1), :] = jnp.sum(dh.astype(F32), axis=0, keepdims=True)
            acc[...] += dot_nt(dh, wi_v[:, cols])
            return carry

        lax.fori_loop(0, 4, feed, 0)
        dctx_v[...] = dot_nt(gy, wd_v[...]).astype(BF16)

        def attend(hp, carry):
            cols = pl.ds(pl.multiple_of(hp * 128, 128), 128)
            qp, kp, vp = bv[5, i, :, cols], bv[6, i, :, cols], bv[7, i, :, cols]
            dop = dctx_v[:, cols]
            dq = dk = dv = None
            for a in range(2):
                probs = pb[i, 2 * hp + a]
                pf = probs.astype(F32)
                dprob = dot_nt(pick(vp, a), dop)
                prod = dprob * pf
                ds = (prod - pf * jnp.sum(prod, axis=0, keepdims=True)).astype(BF16)
                dv_a = dot_nn(probs, pick(dop, a))
                dk_a = dot_nn(ds, pick(qp, a))
                dq_a = dot_tn(ds, pick(kp, a))
                dv = dv_a if dv is None else dv + dv_a
                dk = dk_a if dk is None else dk + dk_a
                dq = dq_a if dq is None else dq + dq_a
            for t, w in ((0, rotate(dq * HEAD ** (-0.5), -1.0)), (1, rotate(dk, -1.0)), (2, dv)):
                w = w.astype(BF16)
                bv[5 + t, i, :, cols] = w
                small[i, 4 + t : 5 + t, cols] = jnp.sum(w.astype(F32), axis=0, keepdims=True)
            return carry

        lax.fori_loop(0, pairs, attend, 0)
        da1 = dot_nt(bv[5, i], wqkv_v[:, 0:d])
        da1 = da1 + dot_nt(bv[6, i], wqkv_v[:, d : 2 * d])
        da1 = da1 + dot_nt(bv[7, i], wqkv_v[:, 2 * d : 3 * d])
        da2 = acc[...]
        x, unit, inverse = unit_of(i)
        small[i, 0:1, :] = jnp.sum(da1 * unit, axis=0, keepdims=True)
        small[i, 1:2, :] = jnp.sum(da1, axis=0, keepdims=True)
        small[i, 2:3, :] = jnp.sum(da2 * unit, axis=0, keepdims=True)
        small[i, 3:4, :] = jnp.sum(da2, axis=0, keepdims=True)
        scaled = da1 * g1[...] + da2 * g2[...]
        mean_g = jnp.mean(scaled, axis=-1, keepdims=True)
        mean_gn = jnp.mean(scaled * unit, axis=-1, keepdims=True)
        dx = bv[4, i].astype(F32) + inverse * (scaled - mean_g - unit * mean_gn)
        dxb[i] = dx.astype(BF16)

        @pl.when(last)
        def _():
            bcopy(i).start()

        pltpu.make_async_copy(dxb.at[i], out_dx.at[0, i], dxsem.at[i]).start()
        for k in range(8):
            pltpu.make_async_copy(bv.at[k, i], b_hbm.at[k, i], bsem.at[k, i]).start()
        return carry

    @pl.when(first)
    def _():
        pltpu.make_async_copy(inputs, xb, insem).wait()

    lax.fori_loop(0, n_mb, forward, 0)

    @pl.when(last)
    def _():
        pltpu.make_async_copy(cot, bv.at[4], cotsem).wait()

    lax.fori_loop(0, n_mb, backward, 0)

    def drain(i, carry):
        @pl.when(first)
        def _():
            fcopy(i).wait_send()

        @pl.when(last)
        def _():
            bcopy(i).wait_send()

        pltpu.make_async_copy(yb.at[i], out_y.at[0, i], ysem.at[i]).wait()
        pltpu.make_async_copy(dxb.at[i], out_dx.at[0, i], dxsem.at[i]).wait()
        for k in range(7):
            pltpu.make_async_copy(av.at[k, i], a_hbm.at[k, i], asem.at[k, i]).wait()
        for k in range(8):
            pltpu.make_async_copy(bv.at[k, i], b_hbm.at[k, i], bsem.at[k, i]).wait()
        return carry

    lax.fori_loop(0, n_mb, drain, 0)


def section_call(lens, inputs, cot, params, tables):
    n_mb, seq, d = inputs.shape
    g1, b1, wqkv, bqkv, wd, bd, g2, b2, wi, bi, wo, bo = params
    ff = wi.shape[2]
    vmem = pl.BlockSpec(memory_space=pltpu.VMEM)
    smem = pl.BlockSpec(memory_space=pltpu.SMEM)
    hbm = pl.BlockSpec(memory_space=pl.ANY)
    dma = pltpu.SemaphoreType.DMA
    flops = n_mb * 2 * seq * (3 * d * d + d * d + 2 * d * ff) * 2
    return pl.pallas_call(
        functools.partial(section_kernel, n_mb),
        out_shape=(
            jax.ShapeDtypeStruct((1, n_mb, seq, d), BF16),
            jax.ShapeDtypeStruct((1, n_mb, seq, d), BF16),
            jax.ShapeDtypeStruct((7, n_mb, seq, d), BF16),
            jax.ShapeDtypeStruct((8, n_mb, seq, d), BF16),
            jax.ShapeDtypeStruct((n_mb, 16, d), F32),
        ),
        in_specs=[smem, hbm, hbm, vmem, vmem, hbm, vmem, hbm, vmem, vmem, vmem, hbm, vmem, hbm, vmem, vmem],
        out_specs=(hbm, hbm, hbm, hbm, vmem),
        scratch_shapes=[
            pltpu.VMEM((d, 3 * d), BF16),
            pltpu.VMEM((d, d), BF16),
            pltpu.VMEM((d, ff), BF16),
            pltpu.VMEM((ff, d), BF16),
            pltpu.VMEM((n_mb, seq, d), BF16),
            pltpu.VMEM((7, n_mb, seq, d), BF16),
            pltpu.VMEM((8, n_mb, seq, d), BF16),
            pltpu.VMEM((n_mb, HEADS, seq, seq), BF16),
            pltpu.VMEM((n_mb, seq, d), BF16),
            pltpu.VMEM((n_mb, seq, d), BF16),
            pltpu.VMEM((seq, d), F32),
            pltpu.VMEM((seq, d), BF16),
            pltpu.VMEM((seq, seq), F32),
            dma((4,)),
            dma,
            dma,
            dma((n_mb,)),
            dma((n_mb,)),
            dma((7, n_mb)),
            dma((8, n_mb)),
            dma((n_mb,)),
            dma((n_mb,)),
            dma((n_mb,)),
            dma((n_mb,)),
        ],
        compiler_params=pltpu.CompilerParams(
            collective_id=0, has_side_effects=True, vmem_limit_bytes=62 * 2**20
        ),
        cost_estimate=pl.CostEstimate(flops=flops, bytes_accessed=40 * 2**20, transcendentals=0),
    )(lens, inputs, cot, g1, b1, wqkv, bqkv, wd, bd, g2, b2, wi, bi, wo, bo, tables)


def a_index(b):
    return jnp.where(b < 4, 0, jnp.where(b < 8, b - 3, jnp.where(b < 11, 5, 6)))


def b_index(b):
    return jnp.where(b < 4, b, jnp.where(b < 8, 4, jnp.where(b < 11, b - 3, 4)))


def weight_kernel(a_ref, b_ref, p_ref, nrm_ref):
    n_mb, seq, d = a_ref.shape[1:]

    @pl.when(pl.program_id(0) == 0)
    def _():
        nrm_ref[...] = jnp.zeros_like(nrm_ref)

    step = 256
    for c in range(d // step):
        cols = slice(c * step, (c + 1) * step)
        total = None
        for m in range(n_mb):
            grad = dot_tn(a_ref[0, m], b_ref[0, m, :, cols])
            squares = jnp.sum((grad * grad).reshape(d // 8, 8, step), axis=0)
            nrm_ref[m] += squares[:, :128] + squares[:, 128:]
            total = grad if total is None else total + grad
        p_ref[0, :, cols] = total.astype(BF16)


def weight_call(a, b):
    n_mb, seq, d = a.shape[1:]
    return pl.pallas_call(
        weight_kernel,
        grid=(12,),
        out_shape=(
            jax.ShapeDtypeStruct((12, d, d), BF16),
            jax.ShapeDtypeStruct((n_mb, 8, 128), F32),
        ),
        in_specs=[
            pl.BlockSpec((1, n_mb, seq, d), lambda g: (a_index(g), 0, 0, 0)),
            pl.BlockSpec((1, n_mb, seq, d), lambda g: (b_index(g), 0, 0, 0)),
        ],
        out_specs=(
            pl.BlockSpec((1, d, d), lambda g: (g, 0, 0)),
            pl.BlockSpec((n_mb, 8, 128), lambda g: (0, 0, 0)),
        ),
        compiler_params=pltpu.CompilerParams(vmem_limit_bytes=48 * 2**20),
        cost_estimate=pl.CostEstimate(
            flops=12 * 2 * n_mb * seq * d * d, bytes_accessed=40 * 2**20, transcendentals=0
        ),
    )(a, b)


def on_device(inputs, cotangent, lengths, *params):
    n_mb, seq, d = inputs.shape
    tables = jnp.asarray(rotary_tables(seq))
    out_y, out_dx, a, b, small = section_call(lengths, inputs, cotangent, params, tables)
    partial, nrm = weight_call(a, b)
    small = small[:, :12]
    weight = jnp.ones((12, 1), F32).at[7].set(2.0)
    norms = jnp.sum(nrm, axis=(1, 2)) + jnp.sum(small * small * weight, axis=(1, 2))
    norms = lax.psum(norms, "pipe")
    summed = lax.psum(partial, "dp").astype(F32)
    vectors = lax.psum(jnp.sum(small, axis=0), "dp")
    rows = [vectors[k : k + 1] for k in range(12)]
    w_in = jnp.concatenate([summed[k] for k in range(4)], axis=1)[None]
    w_out = summed[4:8].reshape(1, 4 * d, d)
    w_qkv = jnp.concatenate([summed[8 + k] for k in range(3)], axis=1)[None]
    w_dense = summed[11:12]
    return (
        out_y,
        out_dx,
        rows[0],
        rows[1],
        w_qkv,
        vectors[4:7].reshape(1, 3 * d),
        w_dense,
        rows[7],
        rows[2],
        rows[3],
        w_in,
        vectors[8:12].reshape(1, 4 * d),
        w_out,
        rows[7],
        norms,
    )


def solution(mesh):
    matrix, vector = P("pipe", None, None), P("pipe", None)
    weights = (vector, vector, matrix, vector, matrix, vector) * 2
    tokens = P("dp", None, None)
    return jax.shard_map(
        on_device,
        mesh=mesh,
        in_specs=(tokens, tokens, P("dp")) + weights,
        out_specs=(P("pipe", "dp", None, None),) * 2 + weights + (P("dp"),),
        check_vma=False,
    )
```

```python
import functools

import jax
import jax.numpy as jnp
import numpy as np
from jax import lax
from jax.experimental import pallas as pl
from jax.experimental.pallas import tpu as pltpu
from jax.sharding import PartitionSpec as P

HEADS = 12
HEAD = 64
ROT = 16
EPSILON = 1e-05
NEG_FILL = -1e30
INV_ROOT_TWO = 0.7071067811865476
INV_ROOT_TWO_PI = 0.3989422804014327
MESH = pl.DeviceIdType.MESH
F32 = jnp.float32
BF16 = jnp.bfloat16


def dot_nn(a, b):
    return jnp.dot(a, b, preferred_element_type=F32)


def dot_nt(a, b):
    return lax.dot_general(a, b, (((1,), (1,)), ((), ())), preferred_element_type=F32)


def dot_tn(a, b):
    return lax.dot_general(a, b, (((0,), (0,)), ((), ())), preferred_element_type=F32)


def rotary_tables(seq):
    half = ROT // 2
    freq = 10000.0 ** (-2.0 * np.arange(half) / ROT)
    angle = np.arange(seq)[:, None] * freq[None, :]
    cosine, sine = np.cos(angle), np.sin(angle)
    own = np.ones((seq, HEAD))
    up = np.zeros((seq, HEAD))
    down = np.zeros((seq, HEAD))
    own[:, :half] = cosine
    own[:, half:ROT] = cosine
    up[:, half:ROT] = sine
    down[:, :half] = -sine
    tables = np.stack([np.concatenate([t, t], axis=1) for t in (own, up, down)])
    return tables.astype(np.float32)


def section_kernel(
    n_mb,
    lens,
    inputs,
    cot,
    g1,
    b1,
    wqkv,
    bqkv,
    wd,
    bd,
    g2,
    b2,
    wi,
    bi,
    wo,
    bo,
    tables,
    out_y,
    out_dx,
    a_hbm,
    b_hbm,
    small,
    wqkv_v,
    wd_v,
    wi_v,
    wo_v,
    xb,
    av,
    bv,
    pb,
    yb,
    dxb,
    acc,
    dctx_v,
    bias_v,
    wsem,
    insem,
    cotsem,
    ysem,
    dxsem,
    asem,
    bsem,
    fsend,
    frecv,
    bsend,
    brecv,
):
    section = lax.axis_index("pipe")
    first = section == 0
    last = section == 1
    peer = 1 - section
    seq, d = xb.shape[1], xb.shape[2]
    pairs = d // 128

    wcopies = [
        pltpu.make_async_copy(src.at[0], dst, wsem.at[k])
        for k, (src, dst) in enumerate(((wqkv, wqkv_v), (wd, wd_v), (wi, wi_v), (wo, wo_v)))
    ]

    @pl.when(first)
    def _():
        pltpu.make_async_copy(inputs, xb, insem).start()

    for c in wcopies:
        c.start()

    @pl.when(last)
    def _():
        pltpu.make_async_copy(cot, bv.at[4], cotsem).start()

    barrier = pltpu.get_barrier_semaphore()
    pl.semaphore_signal(barrier, inc=1, device_id={"pipe": peer}, device_id_type=MESH)
    pl.semaphore_wait(barrier, 1)

    def fcopy(i):
        return pltpu.make_async_remote_copy(
            src_ref=yb.at[i],
            dst_ref=xb.at[i],
            send_sem=fsend.at[i],
            recv_sem=frecv.at[i],
            device_id={"pipe": peer},
            device_id_type=MESH,
        )

    def bcopy(i):
        return pltpu.make_async_remote_copy(
            src_ref=dxb.at[i],
            dst_ref=bv.at[4, i],
            send_sem=bsend.at[i],
            recv_sem=brecv.at[i],
            device_id={"pipe": peer},
            device_id_type=MESH,
        )

    lane = lax.broadcasted_iota(jnp.int32, (seq, 128), 1)
    lower = lane < HEAD

    def pick(value, a):
        return jnp.where(lower if a == 0 else jnp.logical_not(lower), value, jnp.zeros_like(value))

    def rotate(w, sign):
        return (
            w * tables[0]
            + sign * (pltpu.roll(w, ROT // 2, 1) * tables[1] + pltpu.roll(w, 128 - ROT // 2, 1) * tables[2])
        )

    def unit_of(i):
        x = xb[i].astype(F32)
        center = x - jnp.mean(x, axis=-1, keepdims=True)
        inverse = lax.rsqrt(jnp.mean(center * center, axis=-1, keepdims=True) + EPSILON)
        return x, center * inverse, inverse

    def forward(i, carry):
        @pl.when(last)
        def _():
            fcopy(i).wait_recv()

        x, unit, inverse = unit_of(i)
        a1 = (unit * g1[...] + b1[...]).astype(BF16)
        a2 = (unit * g2[...] + b2[...]).astype(BF16)
        av[5, i] = a1
        av[0, i] = a2

        @pl.when(i == 0)
        def _():
            wcopies[0].wait()

        for t in range(3):
            mixed = dot_nn(a1, wqkv_v[:, t * d : (t + 1) * d]) + bqkv[:, t * d : (t + 1) * d]
            if t == 2:
                bv[5 + t, i] = mixed.astype(BF16)
            else:
                for hp in range(pairs):
                    w = rotate(mixed[:, hp * 128 : (hp + 1) * 128], 1.0)
                    if t == 0:
                        w = w * HEAD ** (-0.5)
                    bv[5 + t, i, :, hp * 128 : (hp + 1) * 128] = w.astype(BF16)

        key = lax.broadcasted_iota(jnp.int32, (seq, seq), 0)
        query = lax.broadcasted_iota(jnp.int32, (seq, seq), 1)
        bias_v[...] = jnp.where((key <= query) & (key < lens[i]), 0.0, NEG_FILL)

        def attend(hp, carry):
            cols = pl.ds(pl.multiple_of(hp * 128, 128), 128)
            qp, kp, vp = bv[5, i, :, cols], bv[6, i, :, cols], bv[7, i, :, cols]
            ctx = None
            for a in range(2):
                scores = dot_nt(pick(kp, a), qp) + bias_v[...]
                expo = jnp.exp(scores - jnp.max(scores, axis=0, keepdims=True))
                probs = (expo * (1.0 / jnp.sum(expo, axis=0, keepdims=True))).astype(BF16)
                pb[i, 2 * hp + a] = probs
                part = dot_tn(probs, pick(vp, a))
                ctx = part if ctx is None else ctx + part
            av[6, i, :, cols] = ctx.astype(BF16)
            return carry

        lax.fori_loop(0, pairs, attend, 0)

        @pl.when(i == 0)
        def _():
            for k in (1, 2, 3):
                wcopies[k].wait()

        acc[...] = x + dot_nn(av[6, i], wd_v[...]) + bd[...] + bo[...]

        def feed(j, carry):
            cols = pl.ds(pl.multiple_of(j * d, 128), d)
            hidden = dot_nn(av[0, i], wi_v[:, cols]) + bi[:, cols]
            gate = 0.5 * (1.0 + lax.erf(hidden * INV_ROOT_TWO))
            act = (hidden * gate).astype(BF16)
            av[1 + j, i] = act
            bv[j, i] = (gate + hidden * jnp.exp(-0.5 * hidden * hidden) * INV_ROOT_TWO_PI).astype(BF16)
            acc[...] += dot_nn(act, wo_v[pl.ds(pl.multiple_of(j * d, 128), d), :])
            return carry

        lax.fori_loop(0, 4, feed, 0)
        yb[i] = acc[...].astype(BF16)

        @pl.when(first)
        def _():
            fcopy(i).start()

        pltpu.make_async_copy(yb.at[i], out_y.at[0, i], ysem.at[i]).start()
        for k in range(7):
            pltpu.make_async_copy(av.at[k, i], a_hbm.at[k, i], asem.at[k, i]).start()
        return carry

    def backward(i, carry):
        @pl.when(first)
        def _():
            bcopy(i).wait_recv()

        @pl.when(last)
        def _():
            row = lax.broadcasted_iota(jnp.int32, (seq, d), 0)
            value = bv[4, i].astype(F32)
            bv[4, i] = jnp.where(row < lens[i], value, 0.0).astype(BF16)

        gy = bv[4, i]
        small[i, 7:8, :] = jnp.sum(gy.astype(F32), axis=0, keepdims=True)
        acc[...] = jnp.zeros_like(acc)

        def feed(j, carry):
            cols = pl.ds(pl.multiple_of(j * d, 128), d)
            dact = dot_nt(bv[4, i], wo_v[pl.ds(pl.multiple_of(j * d, 128), d), :])
            dh = (dact * bv[j, i].astype(F32)).astype(BF16)
            bv[j, i] = dh
            small[i, pl.ds(8 + j, 1), :] = jnp.sum(dh.astype(F32), axis=0, keepdims=True)
            acc[...] += dot_nt(dh, wi_v[:, cols])
            return carry

        lax.fori_loop(0, 4, feed, 0)
        dctx_v[...] = dot_nt(gy, wd_v[...]).astype(BF16)

        def attend(hp, carry):
            cols = pl.ds(pl.multiple_of(hp * 128, 128), 128)
            qp, kp, vp = bv[5, i, :, cols], bv[6, i, :, cols], bv[7, i, :, cols]
            dop = dctx_v[:, cols]
            dq = dk = dv = None
            for a in range(2):
                probs = pb[i, 2 * hp + a]
                pf = probs.astype(F32)
                dprob = dot_nt(pick(vp, a), dop)
                prod = dprob * pf
                ds = (prod - pf * jnp.sum(prod, axis=0, keepdims=True)).astype(BF16)
                dv_a = dot_nn(probs, pick(dop, a))
                dk_a = dot_nn(ds, pick(qp, a))
                dq_a = dot_tn(ds, pick(kp, a))
                dv = dv_a if dv is None else dv + dv_a
                dk = dk_a if dk is None else dk + dk_a
                dq = dq_a if dq is None else dq + dq_a
            for t, w in ((0, rotate(dq * HEAD ** (-0.5), -1.0)), (1, rotate(dk, -1.0)), (2, dv)):
                w = w.astype(BF16)
                bv[5 + t, i, :, cols] = w
                small[i, 4 + t : 5 + t, cols] = jnp.sum(w.astype(F32), axis=0, keepdims=True)
            return carry

        lax.fori_loop(0, pairs, attend, 0)
        da1 = dot_nt(bv[5, i], wqkv_v[:, 0:d])
        da1 = da1 + dot_nt(bv[6, i], wqkv_v[:, d : 2 * d])
        da1 = da1 + dot_nt(bv[7, i], wqkv_v[:, 2 * d : 3 * d])
        da2 = acc[...]
        x, unit, inverse = unit_of(i)
        small[i, 0:1, :] = jnp.sum(da1 * unit, axis=0, keepdims=True)
        small[i, 1:2, :] = jnp.sum(da1, axis=0, keepdims=True)
        small[i, 2:3, :] = jnp.sum(da2 * unit, axis=0, keepdims=True)
        small[i, 3:4, :] = jnp.sum(da2, axis=0, keepdims=True)
        scaled = da1 * g1[...] + da2 * g2[...]
        mean_g = jnp.mean(scaled, axis=-1, keepdims=True)
        mean_gn = jnp.mean(scaled * unit, axis=-1, keepdims=True)
        dx = bv[4, i].astype(F32) + inverse * (scaled - mean_g - unit * mean_gn)
        dxb[i] = dx.astype(BF16)

        @pl.when(last)
        def _():
            bcopy(i).start()

        pltpu.make_async_copy(dxb.at[i], out_dx.at[0, i], dxsem.at[i]).start()
        for k in range(8):
            pltpu.make_async_copy(bv.at[k, i], b_hbm.at[k, i], bsem.at[k, i]).start()
        return carry

    @pl.when(first)
    def _():
        pltpu.make_async_copy(inputs, xb, insem).wait()

    lax.fori_loop(0, n_mb, forward, 0)

    @pl.when(last)
    def _():
        pltpu.make_async_copy(cot, bv.at[4], cotsem).wait()

    lax.fori_loop(0, n_mb, backward, 0)

    def drain(i, carry):
        @pl.when(first)
        def _():
            fcopy(i).wait_send()

        @pl.when(last)
        def _():
            bcopy(i).wait_send()

        pltpu.make_async_copy(yb.at[i], out_y.at[0, i], ysem.at[i]).wait()
        pltpu.make_async_copy(dxb.at[i], out_dx.at[0, i], dxsem.at[i]).wait()
        for k in range(7):
            pltpu.make_async_copy(av.at[k, i], a_hbm.at[k, i], asem.at[k, i]).wait()
        for k in range(8):
            pltpu.make_async_copy(bv.at[k, i], b_hbm.at[k, i], bsem.at[k, i]).wait()
        return carry

    lax.fori_loop(0, n_mb, drain, 0)


def section_call(lens, inputs, cot, params, tables):
    n_mb, seq, d = inputs.shape
    g1, b1, wqkv, bqkv, wd, bd, g2, b2, wi, bi, wo, bo = params
    ff = wi.shape[2]
    vmem = pl.BlockSpec(memory_space=pltpu.VMEM)
    smem = pl.BlockSpec(memory_space=pltpu.SMEM)
    hbm = pl.BlockSpec(memory_space=pl.ANY)
    dma = pltpu.SemaphoreType.DMA
    flops = n_mb * 2 * seq * (3 * d * d + d * d + 2 * d * ff) * 2
    return pl.pallas_call(
        functools.partial(section_kernel, n_mb),
        out_shape=(
            jax.ShapeDtypeStruct((1, n_mb, seq, d), BF16),
            jax.ShapeDtypeStruct((1, n_mb, seq, d), BF16),
            jax.ShapeDtypeStruct((7, n_mb, seq, d), BF16),
            jax.ShapeDtypeStruct((8, n_mb, seq, d), BF16),
            jax.ShapeDtypeStruct((n_mb, 16, d), F32),
        ),
        in_specs=[smem, hbm, hbm, vmem, vmem, hbm, vmem, hbm, vmem, vmem, vmem, hbm, vmem, hbm, vmem, vmem],
        out_specs=(hbm, hbm, hbm, hbm, vmem),
        scratch_shapes=[
            pltpu.VMEM((d, 3 * d), BF16),
            pltpu.VMEM((d, d), BF16),
            pltpu.VMEM((d, ff), BF16),
            pltpu.VMEM((ff, d), BF16),
            pltpu.VMEM((n_mb, seq, d), BF16),
            pltpu.VMEM((7, n_mb, seq, d), BF16),
            pltpu.VMEM((8, n_mb, seq, d), BF16),
            pltpu.VMEM((n_mb, HEADS, seq, seq), BF16),
            pltpu.VMEM((n_mb, seq, d), BF16),
            pltpu.VMEM((n_mb, seq, d), BF16),
            pltpu.VMEM((seq, d), F32),
            pltpu.VMEM((seq, d), BF16),
            pltpu.VMEM((seq, seq), F32),
            dma((4,)),
            dma,
            dma,
            dma((n_mb,)),
            dma((n_mb,)),
            dma((7, n_mb)),
            dma((8, n_mb)),
            dma((n_mb,)),
            dma((n_mb,)),
            dma((n_mb,)),
            dma((n_mb,)),
        ],
        compiler_params=pltpu.CompilerParams(
            collective_id=0, has_side_effects=True, vmem_limit_bytes=62 * 2**20
        ),
        cost_estimate=pl.CostEstimate(flops=flops, bytes_accessed=40 * 2**20, transcendentals=0),
    )(lens, inputs, cot, g1, b1, wqkv, bqkv, wd, bd, g2, b2, wi, bi, wo, bo, tables)


PIECES = 4


def a_index(b):
    g = b // 4
    return g * (2 - g) * (b - 3) + (g * (g - 1) // 2) * 5 + b // 11


def b_index(b):
    g = b // 4
    middle, late = g * (2 - g), g * (g - 1) // 2
    return (1 - middle - late) * b + middle * 4 + late * (b - 3) - (b // 11) * 4


def gradient_kernel(
    nb,
    a_hbm,
    b_hbm,
    small,
    out_in,
    out_out,
    out_qkv,
    out_dense,
    out_vec,
    out_nrm,
    abuf,
    bbuf,
    own,
    csend,
    crecv,
    fin,
    yred,
    leafy,
    leafz,
    midy,
    midz,
    yz,
    vec,
    vrecv,
    nrm,
    nrecv,
    absem,
    outsem,
    s_core,
    r_core,
    s_yred,
    r_yred,
    s_leafy,
    r_leafy,
    s_leafz,
    r_leafz,
    s_midy,
    r_midy,
    s_midz,
    r_midz,
    s_yz,
    r_yz,
    s_toty,
    r_toty,
    s_boty,
    r_boty,
    s_totz,
    r_totz,
    s_lz,
    r_lz,
    s_ag,
    r_ag,
    s_vec,
    r_vec,
    s_nrm,
    r_nrm,
):
    n_mb, seq, d = abuf.shape[1:]
    pipe = lax.axis_index("pipe")
    me = lax.axis_index("dp")
    group, inner = me // 16, me % 16
    z, y, core = inner // 4, (inner // 2) % 2, inner % 2
    mid = (z // 2 + z % 2) == 1
    leaf = jnp.logical_not(mid)

    def at(z_, y_, core_):
        return {"dp": group * 16 + (z_ * 2 + y_) * 2 + core_}

    core_peer = at(z, y, 1 - core)
    y_peer = at(z, 1 - y, core)
    near = at(z + 1 - 2 * (z % 2), y, core)
    across = at(3 - z, y, core)
    pipe_peer = {"pipe": 1 - pipe}
    zi = z // 2
    y_mine, y_other = y, 1 - y
    z_mine, z_other = 2 + zi, 3 - zi
    half = core * PIECES

    def remote(src, dst, send, recv, device):
        return pltpu.make_async_remote_copy(
            src_ref=src, dst_ref=dst, send_sem=send, recv_sem=recv, device_id=device, device_id_type=MESH
        )

    def c_core(b):
        return remote(csend.at[b % 2], crecv.at[b], s_core.at[b % 2], r_core.at[b], core_peer)

    def c_yred(b):
        return remote(own.at[b, y_other], yred.at[b], s_yred.at[b], r_yred.at[b], y_peer)

    def c_leafy(b):
        return remote(own.at[b, y_mine], leafy.at[b], s_leafy.at[b], r_leafy.at[b], near)

    def c_leafz(b):
        return remote(own.at[b, pl.ds(2, 2)], leafz.at[b], s_leafz.at[b], r_leafz.at[b], near)

    def c_midy(b):
        return remote(own.at[b, y_mine], midy.at[b], s_midy.at[b], r_midy.at[b], across)

    def c_midz(b):
        return remote(own.at[b, z_other], midz.at[b], s_midz.at[b], r_midz.at[b], across)

    def c_yz(b):
        return remote(own.at[b, z_mine], yz.at[b], s_yz.at[b], r_yz.at[b], y_peer)

    def piece(b, k):
        return fin.at[b, half + k]

    def c_toty(b):
        return remote(piece(b, y_mine), piece(b, y_mine), s_toty.at[b], r_toty.at[b], near)

    def c_boty(b):
        return remote(piece(b, y_mine), piece(b, y_mine), s_boty.at[b], r_boty.at[b], y_peer)

    def c_totz(b):
        return remote(piece(b, z_mine), piece(b, z_mine), s_totz.at[b], r_totz.at[b], across)

    def c_lz(b, which):
        k = z_mine if which == 0 else z_other
        return remote(piece(b, k), piece(b, k), s_lz.at[which, b], r_lz.at[which, b], near)

    def c_ag(b, k):
        return remote(piece(b, k), piece(b, k), s_ag.at[k, b], r_ag.at[k, b], core_peer)

    vec_to = (core_peer, y_peer, near, across, near)

    def c_vec(h):
        return remote(vec.at[h], vrecv.at[h], s_vec.at[h], r_vec.at[h], vec_to[h])

    def c_nrm():
        return remote(nrm, nrecv, s_nrm, r_nrm, pipe_peer)

    def c_load(b, which):
        slot = b % 2
        if which == 0:
            return pltpu.make_async_copy(a_hbm.at[a_index(b)], abuf.at[slot], absem.at[0, slot])
        return pltpu.make_async_copy(b_hbm.at[b_index(b)], bbuf.at[slot], absem.at[1, slot])

    def add(*values):
        total = values[0].astype(F32)
        for v in values[1:]:
            total = total + v.astype(F32)
        return total

    for which in range(2):
        c_load(0, which).start()

    barrier = pltpu.get_barrier_semaphore()
    for device in (core_peer, y_peer, near, pipe_peer):
        pl.semaphore_signal(barrier, inc=1, device_id=device, device_id_type=MESH)

    @pl.when(mid)
    def _():
        pl.semaphore_signal(barrier, inc=1, device_id=across, device_id_type=MESH)
        pl.semaphore_wait(barrier, 5)

    @pl.when(leaf)
    def _():
        pl.semaphore_wait(barrier, 4)

    row = lax.broadcasted_iota(jnp.int32, (16, d), 0)
    total = None
    for m in range(n_mb):
        value = jnp.where(row < 12, small[m], 0.0)
        squares = value * value * jnp.where(row == 7, 2.0, 1.0)
        folded = squares[:8] + squares[8:]
        nrm[m] = sum(folded[:, k * 128 : (k + 1) * 128] for k in range(d // 128))
        total = value if total is None else total + value
    vec[0] = total
    c_vec(0).start()

    def weight_block(b):
        slot = b % 2
        for which in range(2):
            c_load(b, which).wait()

        @pl.when(b + 1 < nb)
        def _():
            for which in range(2):
                c_load(b + 1, which).start()

        @pl.when(b >= 2)
        def _():
            c_core(b - 2).wait_send()

        step = 256
        for c in range(d // step):
            cols = slice(c * step, (c + 1) * step)
            total = None
            for m in range(n_mb):
                grad = dot_tn(abuf[slot, m], bbuf[slot, m, :, cols])
                squares = jnp.sum((grad * grad).reshape(d // 8, 8, step), axis=0)
                nrm[m] += squares[:, :128] + squares[:, 128:]
                total = grad if total is None else total + grad
            total = total.astype(BF16).reshape(2, PIECES, d // 8, step)

            @pl.when(core == 0)
            def _():
                own[b, :, :, cols] = total[0]
                csend[slot, :, :, cols] = total[1]

            @pl.when(core == 1)
            def _():
                own[b, :, :, cols] = total[1]
                csend[slot, :, :, cols] = total[0]

        c_core(b).start()

    def lag1(b):
        c_core(b).wait_recv()
        for k in range(PIECES):
            own[b, k] = add(own[b, k], crecv[b, k]).astype(BF16)
        c_yred(b).start()

        @pl.when(leaf)
        def _():
            c_leafz(b).start()

    def lag2(b):
        @pl.when(mid)
        def _():
            c_leafz(b).wait_recv()
            for k in range(2):
                own[b, 2 + k] = add(own[b, 2 + k], leafz[b, k]).astype(BF16)
            c_midz(b).start()

        c_yred(b).wait_recv()
        own[b, y_mine] = add(own[b, y_mine], yred[b]).astype(BF16)

        @pl.when(leaf)
        def _():
            c_leafy(b).start()

    def lag3(b):
        @pl.when(mid)
        def _():
            c_midz(b).wait_recv()
            own[b, z_mine] = add(own[b, z_mine], midz[b]).astype(BF16)
            c_yz(b).start()
            c_leafy(b).wait_recv()
            own[b, y_mine] = add(own[b, y_mine], leafy[b]).astype(BF16)
            c_midy(b).start()

    def lag4(b):
        @pl.when(mid)
        def _():
            c_yz(b).wait_recv()
            fin[b, half + z_mine] = add(own[b, z_mine], yz[b]).astype(BF16)
            c_totz(b).start()
            c_lz(b, 0).start()
            c_ag(b, z_mine).start()
            c_midy(b).wait_recv()
            fin[b, half + y_mine] = add(own[b, y_mine], midy[b]).astype(BF16)
            c_toty(b).start()
            c_boty(b).start()
            c_ag(b, y_mine).start()

    def lag5(b):
        @pl.when(mid)
        def _():
            c_totz(b).wait_recv()
            c_lz(b, 1).start()
            c_ag(b, z_other).start()
            c_boty(b).wait_recv()
            c_ag(b, y_other).start()

        @pl.when(leaf)
        def _():
            c_toty(b).wait_recv()
            c_boty(b).start()
            c_ag(b, y_mine).start()
            c_lz(b, 0).wait_recv()
            c_ag(b, z_mine).start()

    def lag6(b):
        @pl.when(leaf)
        def _():
            c_boty(b).wait_recv()
            c_ag(b, y_other).start()
            c_lz(b, 1).wait_recv()
            c_ag(b, z_other).start()

    def out_copies(b, act):
        @pl.when(b // 4 == 0)
        def _():
            cols = pl.ds(pl.multiple_of(b * d, 128), d)
            act(pltpu.make_async_copy(fin.at[b], out_in.at[:, :, cols], outsem.at[b]))

        @pl.when(b // 4 == 1)
        def _():
            act(pltpu.make_async_copy(fin.at[b], out_out.at[b - 4], outsem.at[b]))

        @pl.when((b // 4 == 2) & (b < 11))
        def _():
            cols = pl.ds(pl.multiple_of((b - 8) * d, 128), d)
            act(pltpu.make_async_copy(fin.at[b], out_qkv.at[:, :, cols], outsem.at[b]))

        @pl.when(b == 11)
        def _():
            act(pltpu.make_async_copy(fin.at[b], out_dense, outsem.at[b]))

    def lag7(b):
        for k in range(PIECES):
            c_ag(b, k).wait_recv()
        out_copies(b, lambda c: c.start())

    def vector_steps(t):
        @pl.when(t == 1)
        def _():
            c_vec(0).wait_recv()
            vec[1] = vec[0] + vrecv[0]
            c_vec(1).start()

        @pl.when(t == 2)
        def _():
            c_vec(1).wait_recv()
            vec[2] = vec[1] + vrecv[1]

            @pl.when(leaf)
            def _():
                c_vec(2).start()

        @pl.when((t == 3) & mid)
        def _():
            c_vec(2).wait_recv()
            vec[3] = vec[2] + vrecv[2]
            c_vec(3).start()

        @pl.when((t == 4) & mid)
        def _():
            c_vec(3).wait_recv()
            vec[4] = vec[3] + vrecv[3]
            c_vec(4).start()
            out_vec[...] = vec[4]

        @pl.when((t == 5) & leaf)
        def _():
            c_vec(4).wait_recv()
            out_vec[...] = vrecv[4]

        @pl.when(t == nb)
        def _():
            c_nrm().start()

    stages = (weight_block, lag1, lag2, lag3, lag4, lag5, lag6, lag7)

    def step(t, carry):
        for lag, stage in enumerate(stages):

            @pl.when((t >= lag) & (t - lag < nb))
            def _(lag=lag, stage=stage):
                stage(t - lag)

        vector_steps(t)
        return carry

    lax.fori_loop(0, nb + len(stages) - 1, step, 0)

    c_nrm().wait_recv()
    out_nrm[...] = nrm[...] + nrecv[...]
    c_nrm().wait_send()
    c_vec(0).wait_send()
    c_vec(1).wait_send()
    c_core(nb - 2).wait_send()
    c_core(nb - 1).wait_send()

    @pl.when(leaf)
    def _():
        c_vec(2).wait_send()

    @pl.when(mid)
    def _():
        c_vec(3).wait_send()
        c_vec(4).wait_send()

    def drain(b, carry):
        c_yred(b).wait_send()
        c_boty(b).wait_send()
        for k in range(PIECES):
            c_ag(b, k).wait_send()

        @pl.when(leaf)
        def _():
            c_leafy(b).wait_send()
            c_leafz(b).wait_send()

        @pl.when(mid)
        def _():
            c_midy(b).wait_send()
            c_midz(b).wait_send()
            c_yz(b).wait_send()
            c_toty(b).wait_send()
            c_totz(b).wait_send()
            c_lz(b, 0).wait_send()
            c_lz(b, 1).wait_send()

        out_copies(b, lambda c: c.wait())
        return carry

    lax.fori_loop(0, nb, drain, 0)


def gradient_call(a, b, small):
    n_mb, seq, d = a.shape[1:]
    nb = 12
    rows = d // 8
    vmem = pl.BlockSpec(memory_space=pltpu.VMEM)
    hbm = pl.BlockSpec(memory_space=pl.ANY)
    dma = pltpu.SemaphoreType.DMA

    def wide(columns):
        return jax.ShapeDtypeStruct((8, rows, columns), BF16)

    def slots(*lead):
        return pltpu.VMEM(lead + (rows, d), BF16)

    return pl.pallas_call(
        functools.partial(gradient_kernel, nb),
        out_shape=(
            wide(4 * d),
            jax.ShapeDtypeStruct((4, 8, rows, d), BF16),
            wide(3 * d),
            wide(d),
            jax.ShapeDtypeStruct((16, d), F32),
            jax.ShapeDtypeStruct((n_mb, 8, 128), F32),
        ),
        in_specs=[hbm, hbm, vmem],
        out_specs=(hbm, hbm, hbm, hbm, vmem, vmem),
        scratch_shapes=[
            pltpu.VMEM((2, n_mb, seq, d), BF16),
            pltpu.VMEM((2, n_mb, seq, d), BF16),
            slots(nb, PIECES),
            slots(2, PIECES),
            slots(nb, PIECES),
            slots(nb, 2 * PIECES),
            slots(nb),
            slots(nb),
            slots(nb, 2),
            slots(nb),
            slots(nb),
            slots(nb),
            pltpu.VMEM((5, 16, d), F32),
            pltpu.VMEM((5, 16, d), F32),
            pltpu.VMEM((n_mb, 8, 128), F32),
            pltpu.VMEM((n_mb, 8, 128), F32),
            dma((2, 2)),
            dma((nb,)),
            dma((2,)),
            dma((nb,)),
        ]
        + [dma((nb,)) for _ in range(18)]
        + [dma((2, nb)), dma((2, nb)), dma((PIECES, nb)), dma((PIECES, nb)), dma((5,)), dma((5,)), dma, dma],
        compiler_params=pltpu.CompilerParams(
            collective_id=1, has_side_effects=True, vmem_limit_bytes=62 * 2**20
        ),
        cost_estimate=pl.CostEstimate(
            flops=nb * 2 * n_mb * seq * d * d, bytes_accessed=64 * 2**20, transcendentals=0
        ),
    )(a, b, small)


def on_device(size, inputs, cotangent, lengths, *params):
    n_mb, seq, d = inputs.shape
    tables = jnp.asarray(rotary_tables(seq))
    out_y, out_dx, a, b, small = section_call(lengths, inputs, cotangent, params, tables)
    w_in, w_out, w_qkv, w_dense, vectors, nrm = gradient_call(a, b, small)
    sums = [w_in, w_out, w_qkv, w_dense, vectors]
    if size > 16:
        groups = [[g * 16 + r for g in range(size // 16)] for r in range(16)]
        sums = [lax.psum(v, "dp", axis_index_groups=groups) for v in sums]
    w_in, w_out, w_qkv, w_dense, vectors = [v.astype(F32) for v in sums]
    norms = jnp.sum(nrm, axis=(1, 2))
    rows = [vectors[k : k + 1] for k in range(12)]
    return (
        out_y,
        out_dx,
        rows[0],
        rows[1],
        w_qkv.reshape(1, d, 3 * d),
        vectors[4:7].reshape(1, 3 * d),
        w_dense.reshape(1, d, d),
        rows[7],
        rows[2],
        rows[3],
        w_in.reshape(1, d, 4 * d),
        vectors[8:12].reshape(1, 4 * d),
        w_out.reshape(1, 4 * d, d),
        rows[7],
        norms,
    )


def solution(mesh):
    matrix, vector = P("pipe", None, None), P("pipe", None)
    weights = (vector, vector, matrix, vector, matrix, vector) * 2
    tokens = P("dp", None, None)
    return jax.shard_map(
        functools.partial(on_device, mesh.shape["dp"]),
        mesh=mesh,
        in_specs=(tokens, tokens, P("dp")) + weights,
        out_specs=(P("pipe", "dp", None, None),) * 2 + weights + (P("dp"),),
        check_vma=False,
    )
```

```python
import functools

import jax
import jax.numpy as jnp
import numpy as np
from jax import lax
from jax.experimental import pallas as pl
from jax.experimental.pallas import tpu as pltpu
from jax.sharding import PartitionSpec as P

HEADS = 12
HEAD = 64
ROT = 16
EPSILON = 1e-05
NEG_FILL = -1e30
INV_ROOT_TWO = 0.7071067811865476
INV_ROOT_TWO_PI = 0.3989422804014327
MESH = pl.DeviceIdType.MESH
F32 = jnp.float32
BF16 = jnp.bfloat16


def dot_nn(a, b):
    return jnp.dot(a, b, preferred_element_type=F32)


def dot_nt(a, b):
    return lax.dot_general(a, b, (((1,), (1,)), ((), ())), preferred_element_type=F32)


def dot_tn(a, b):
    return lax.dot_general(a, b, (((0,), (0,)), ((), ())), preferred_element_type=F32)


def rotary_tables(seq):
    half = ROT // 2
    freq = 10000.0 ** (-2.0 * np.arange(half) / ROT)
    angle = np.arange(seq)[:, None] * freq[None, :]
    cosine, sine = np.cos(angle), np.sin(angle)
    own = np.ones((seq, HEAD))
    up = np.zeros((seq, HEAD))
    down = np.zeros((seq, HEAD))
    own[:, :half] = cosine
    own[:, half:ROT] = cosine
    up[:, half:ROT] = sine
    down[:, :half] = -sine
    tables = np.stack([np.concatenate([t, t], axis=1) for t in (own, up, down)])
    return tables.astype(np.float32)


def section_kernel(
    n_mb,
    lens,
    inputs,
    cot,
    g1,
    b1,
    wqkv,
    bqkv,
    wd,
    bd,
    g2,
    b2,
    wi,
    bi,
    wo,
    bo,
    tables,
    out_y,
    out_dx,
    a_hbm,
    b_hbm,
    small,
    wqkv_v,
    wd_v,
    wi_v,
    wo_v,
    xb,
    av,
    bv,
    pb,
    yb,
    dxb,
    acc,
    dctx_v,
    bias_v,
    wsem,
    insem,
    cotsem,
    ysem,
    dxsem,
    asem,
    bsem,
    fsend,
    frecv,
    bsend,
    brecv,
):
    section = lax.axis_index("pipe")
    first = section == 0
    last = section == 1
    peer = 1 - section
    seq, d = xb.shape[1], xb.shape[2]
    pairs = d // 128

    wcopies = [
        pltpu.make_async_copy(src.at[0], dst, wsem.at[k])
        for k, (src, dst) in enumerate(((wqkv, wqkv_v), (wd, wd_v), (wi, wi_v), (wo, wo_v)))
    ]

    @pl.when(first)
    def _():
        pltpu.make_async_copy(inputs, xb, insem).start()

    for c in wcopies:
        c.start()

    @pl.when(last)
    def _():
        pltpu.make_async_copy(cot, bv.at[4], cotsem).start()

    barrier = pltpu.get_barrier_semaphore()
    pl.semaphore_signal(barrier, inc=1, device_id={"pipe": peer}, device_id_type=MESH)
    pl.semaphore_wait(barrier, 1)

    def fcopy(i):
        return pltpu.make_async_remote_copy(
            src_ref=yb.at[i],
            dst_ref=xb.at[i],
            send_sem=fsend.at[i],
            recv_sem=frecv.at[i],
            device_id={"pipe": peer},
            device_id_type=MESH,
        )

    def bcopy(i):
        return pltpu.make_async_remote_copy(
            src_ref=dxb.at[i],
            dst_ref=bv.at[4, i],
            send_sem=bsend.at[i],
            recv_sem=brecv.at[i],
            device_id={"pipe": peer},
            device_id_type=MESH,
        )

    lane = lax.broadcasted_iota(jnp.int32, (seq, 128), 1)
    lower = lane < HEAD

    def pick(value, a):
        return jnp.where(lower if a == 0 else jnp.logical_not(lower), value, jnp.zeros_like(value))

    def rotate(w, sign):
        return (
            w * tables[0]
            + sign * (pltpu.roll(w, ROT // 2, 1) * tables[1] + pltpu.roll(w, 128 - ROT // 2, 1) * tables[2])
        )

    def unit_of(i):
        x = xb[i].astype(F32)
        center = x - jnp.mean(x, axis=-1, keepdims=True)
        inverse = lax.rsqrt(jnp.mean(center * center, axis=-1, keepdims=True) + EPSILON)
        return x, center * inverse, inverse

    def both_parts(attend, feed):
        for k in range(pairs):
            attend(k)
        for k in range(4):
            feed(k)

    def forward(i):
        @pl.when(last)
        def _():
            fcopy(i).wait_recv()

        x, unit, inverse = unit_of(i)
        a1 = (unit * g1[...] + b1[...]).astype(BF16)
        a2 = (unit * g2[...] + b2[...]).astype(BF16)
        av[5, i] = a1
        av[0, i] = a2

        @pl.when(i == 0)
        def _():
            wcopies[0].wait()

        for t in (2, 1, 0):
            mixed = dot_nn(a1, wqkv_v[:, t * d : (t + 1) * d]) + bqkv[:, t * d : (t + 1) * d]
            if t == 2:
                bv[5 + t, i] = mixed.astype(BF16)
            else:
                for hp in range(pairs):
                    w = rotate(mixed[:, hp * 128 : (hp + 1) * 128], 1.0)
                    if t == 0:
                        w = w * HEAD ** (-0.5)
                    bv[5 + t, i, :, hp * 128 : (hp + 1) * 128] = w.astype(BF16)

        key = lax.broadcasted_iota(jnp.int32, (seq, seq), 0)
        query = lax.broadcasted_iota(jnp.int32, (seq, seq), 1)
        bias_v[...] = jnp.where((key <= query) & (key < lens[i]), 0.0, NEG_FILL)

        def attend(hp):
            cols = slice(hp * 128, (hp + 1) * 128)
            qp, kp, vp = bv[5, i, :, cols], bv[6, i, :, cols], bv[7, i, :, cols]
            ctx = None
            for a in range(2):
                scores = dot_nt(pick(kp, a), qp) + bias_v[...]
                expo = jnp.exp(scores - jnp.max(scores, axis=0, keepdims=True))
                probs = (expo * (1.0 / jnp.sum(expo, axis=0, keepdims=True))).astype(BF16)
                pb[i, 2 * hp + a] = probs
                part = dot_tn(probs, pick(vp, a))
                ctx = part if ctx is None else ctx + part
            av[6, i, :, cols] = ctx.astype(BF16)

        @pl.when(i == 0)
        def _():
            for k in (1, 2, 3):
                wcopies[k].wait()

        acc[...] = xb[i].astype(F32) + bd[...] + bo[...]

        def feed(j):
            cols = slice(j * d, (j + 1) * d)
            hidden = dot_nn(av[0, i], wi_v[:, cols]) + bi[:, cols]
            gate = 0.5 * (1.0 + lax.erf(hidden * INV_ROOT_TWO))
            act = (hidden * gate).astype(BF16)
            av[1 + j, i] = act
            bv[j, i] = (gate + hidden * jnp.exp(-0.5 * hidden * hidden) * INV_ROOT_TWO_PI).astype(BF16)
            acc[...] += dot_nn(act, wo_v[j * d : (j + 1) * d, :])

        both_parts(attend, feed)
        yb[i] = (acc[...] + dot_nn(av[6, i], wd_v[...])).astype(BF16)

        @pl.when(first)
        def _():
            fcopy(i).start()

        pltpu.make_async_copy(yb.at[i], out_y.at[0, i], ysem.at[i]).start()
        for k in range(7):
            pltpu.make_async_copy(av.at[k, i], a_hbm.at[k, i], asem.at[k, i]).start()

    def backward(i):
        @pl.when(first)
        def _():
            bcopy(i).wait_recv()

        @pl.when(last)
        def _():
            row = lax.broadcasted_iota(jnp.int32, (seq, d), 0)
            value = bv[4, i].astype(F32)
            bv[4, i] = jnp.where(row < lens[i], value, 0.0).astype(BF16)

        gy = bv[4, i]
        small[i, 7:8, :] = jnp.sum(gy.astype(F32), axis=0, keepdims=True)
        acc[...] = jnp.zeros_like(acc)

        def feed(j):
            cols = slice(j * d, (j + 1) * d)
            dact = dot_nt(bv[4, i], wo_v[j * d : (j + 1) * d, :])
            dh = (dact * bv[j, i].astype(F32)).astype(BF16)
            bv[j, i] = dh
            small[i, 8 + j : 9 + j, :] = jnp.sum(dh.astype(F32), axis=0, keepdims=True)
            acc[...] += dot_nt(dh, wi_v[:, cols])

        dctx_v[...] = dot_nt(gy, wd_v[...]).astype(BF16)

        def attend(hp):
            cols = slice(hp * 128, (hp + 1) * 128)
            qp, kp, vp = bv[5, i, :, cols], bv[6, i, :, cols], bv[7, i, :, cols]
            dop = dctx_v[:, cols]
            dq = dk = dv = None
            for a in range(2):
                probs = pb[i, 2 * hp + a]
                pf = probs.astype(F32)
                dprob = dot_nt(pick(vp, a), dop)
                prod = dprob * pf
                ds = (prod - pf * jnp.sum(prod, axis=0, keepdims=True)).astype(BF16)
                dv_a = dot_nn(probs, pick(dop, a))
                dk_a = dot_nn(ds, pick(qp, a))
                dq_a = dot_tn(ds, pick(kp, a))
                dv = dv_a if dv is None else dv + dv_a
                dk = dk_a if dk is None else dk + dk_a
                dq = dq_a if dq is None else dq + dq_a
            for t, w in ((0, rotate(dq * HEAD ** (-0.5), -1.0)), (1, rotate(dk, -1.0)), (2, dv)):
                w = w.astype(BF16)
                bv[5 + t, i, :, cols] = w
                small[i, 4 + t : 5 + t, cols] = jnp.sum(w.astype(F32), axis=0, keepdims=True)

        both_parts(attend, feed)
        da1 = dot_nt(bv[5, i], wqkv_v[:, 0:d])
        da1 = da1 + dot_nt(bv[6, i], wqkv_v[:, d : 2 * d])
        da1 = da1 + dot_nt(bv[7, i], wqkv_v[:, 2 * d : 3 * d])
        da2 = acc[...]
        x, unit, inverse = unit_of(i)
        small[i, 0:1, :] = jnp.sum(da1 * unit, axis=0, keepdims=True)
        small[i, 1:2, :] = jnp.sum(da1, axis=0, keepdims=True)
        small[i, 2:3, :] = jnp.sum(da2 * unit, axis=0, keepdims=True)
        small[i, 3:4, :] = jnp.sum(da2, axis=0, keepdims=True)
        scaled = da1 * g1[...] + da2 * g2[...]
        mean_g = jnp.mean(scaled, axis=-1, keepdims=True)
        mean_gn = jnp.mean(scaled * unit, axis=-1, keepdims=True)
        dx = bv[4, i].astype(F32) + inverse * (scaled - mean_g - unit * mean_gn)
        dxb[i] = dx.astype(BF16)

        @pl.when(last)
        def _():
            bcopy(i).start()

        pltpu.make_async_copy(dxb.at[i], out_dx.at[0, i], dxsem.at[i]).start()
        for k in range(8):
            pltpu.make_async_copy(bv.at[k, i], b_hbm.at[k, i], bsem.at[k, i]).start()

    @pl.when(first)
    def _():
        pltpu.make_async_copy(inputs, xb, insem).wait()

    @pl.when(last)
    def _():
        pltpu.make_async_copy(cot, bv.at[4], cotsem).wait()

    def tick(step, carry):
        phase = section * (step % 2) + (1 - section) * (step // n_mb)
        mb = section * (step // 2) + (1 - section) * (step % n_mb)

        @pl.when(phase == 0)
        def _():
            forward(mb)

        @pl.when(phase == 1)
        def _():
            backward(mb)

        return carry

    lax.fori_loop(0, 2 * n_mb, tick, 0)

    def drain(i, carry):
        @pl.when(first)
        def _():
            fcopy(i).wait_send()

        @pl.when(last)
        def _():
            bcopy(i).wait_send()

        pltpu.make_async_copy(yb.at[i], out_y.at[0, i], ysem.at[i]).wait()
        pltpu.make_async_copy(dxb.at[i], out_dx.at[0, i], dxsem.at[i]).wait()
        for k in range(7):
            pltpu.make_async_copy(av.at[k, i], a_hbm.at[k, i], asem.at[k, i]).wait()
        for k in range(8):
            pltpu.make_async_copy(bv.at[k, i], b_hbm.at[k, i], bsem.at[k, i]).wait()
        return carry

    lax.fori_loop(0, n_mb, drain, 0)


def section_call(lens, inputs, cot, params, tables):
    n_mb, seq, d = inputs.shape
    g1, b1, wqkv, bqkv, wd, bd, g2, b2, wi, bi, wo, bo = params
    ff = wi.shape[2]
    vmem = pl.BlockSpec(memory_space=pltpu.VMEM)
    smem = pl.BlockSpec(memory_space=pltpu.SMEM)
    hbm = pl.BlockSpec(memory_space=pl.ANY)
    dma = pltpu.SemaphoreType.DMA
    flops = n_mb * 2 * seq * (3 * d * d + d * d + 2 * d * ff) * 2
    return pl.pallas_call(
        functools.partial(section_kernel, n_mb),
        out_shape=(
            jax.ShapeDtypeStruct((1, n_mb, seq, d), BF16),
            jax.ShapeDtypeStruct((1, n_mb, seq, d), BF16),
            jax.ShapeDtypeStruct((7, n_mb, seq, d), BF16),
            jax.ShapeDtypeStruct((8, n_mb, seq, d), BF16),
            jax.ShapeDtypeStruct((n_mb, 16, d), F32),
        ),
        in_specs=[smem, hbm, hbm, vmem, vmem, hbm, vmem, hbm, vmem, vmem, vmem, hbm, vmem, hbm, vmem, vmem],
        out_specs=(hbm, hbm, hbm, hbm, vmem),
        scratch_shapes=[
            pltpu.VMEM((d, 3 * d), BF16),
            pltpu.VMEM((d, d), BF16),
            pltpu.VMEM((d, ff), BF16),
            pltpu.VMEM((ff, d), BF16),
            pltpu.VMEM((n_mb, seq, d), BF16),
            pltpu.VMEM((7, n_mb, seq, d), BF16),
            pltpu.VMEM((8, n_mb, seq, d), BF16),
            pltpu.VMEM((n_mb, HEADS, seq, seq), BF16),
            pltpu.VMEM((n_mb, seq, d), BF16),
            pltpu.VMEM((n_mb, seq, d), BF16),
            pltpu.VMEM((seq, d), F32),
            pltpu.VMEM((seq, d), BF16),
            pltpu.VMEM((seq, seq), F32),
            dma((4,)),
            dma,
            dma,
            dma((n_mb,)),
            dma((n_mb,)),
            dma((7, n_mb)),
            dma((8, n_mb)),
            dma((n_mb,)),
            dma((n_mb,)),
            dma((n_mb,)),
            dma((n_mb,)),
        ],
        compiler_params=pltpu.CompilerParams(
            collective_id=0, has_side_effects=True, vmem_limit_bytes=62 * 2**20
        ),
        cost_estimate=pl.CostEstimate(flops=flops, bytes_accessed=40 * 2**20, transcendentals=0),
    )(lens, inputs, cot, g1, b1, wqkv, bqkv, wd, bd, g2, b2, wi, bi, wo, bo, tables)


PIECES = 4
SPLITS = 2


def a_index(b):
    g = b // 4
    return g * (2 - g) * (b - 3) + (g * (g - 1) // 2) * 5 + b // 11


def b_index(b):
    g = b // 4
    middle, late = g * (2 - g), g * (g - 1) // 2
    return (1 - middle - late) * b + middle * 4 + late * (b - 3) - (b // 11) * 4


def gradient_kernel(
    nb,
    a_hbm,
    b_hbm,
    small,
    out_in,
    out_out,
    out_qkv,
    out_dense,
    out_vec,
    out_nrm,
    abuf,
    bbuf,
    own,
    csend,
    crecv,
    fin,
    yred,
    leafy,
    leafz,
    midy,
    midz,
    yz,
    vec,
    vrecv,
    nrm,
    nrecv,
    absem,
    outsem,
    s_core,
    r_core,
    s_yred,
    r_yred,
    s_leafy,
    r_leafy,
    s_leafz,
    r_leafz,
    s_midy,
    r_midy,
    s_midz,
    r_midz,
    s_yz,
    r_yz,
    s_toty,
    r_toty,
    s_boty,
    r_boty,
    s_totz,
    r_totz,
    s_lz,
    r_lz,
    s_ag,
    r_ag,
    s_vec,
    r_vec,
    s_nrm,
    r_nrm,
):
    n_mb, seq, d = abuf.shape[1:]
    pipe = lax.axis_index("pipe")
    me = lax.axis_index("dp")
    group, inner = me // 16, me % 16
    z, y, core = inner // 4, (inner // 2) % 2, inner % 2
    mid = (z // 2 + z % 2) == 1
    leaf = jnp.logical_not(mid)

    def at(z_, y_, core_):
        return {"dp": group * 16 + (z_ * 2 + y_) * 2 + core_}

    core_peer = at(z, y, 1 - core)
    y_peer = at(z, 1 - y, core)
    near = at(z + 1 - 2 * (z % 2), y, core)
    across = at(3 - z, y, core)
    pipe_peer = {"pipe": 1 - pipe}
    zi = z // 2
    y_mine, y_other = y, 1 - y
    z_mine, z_other = 2 + zi, 3 - zi
    half = core * PIECES

    def remote(src, dst, send, recv, device):
        return pltpu.make_async_remote_copy(
            src_ref=src, dst_ref=dst, send_sem=send, recv_sem=recv, device_id=device, device_id_type=MESH
        )

    def c_core(b):
        return remote(csend.at[b % 2], crecv.at[b], s_core.at[b % 2], r_core.at[b], core_peer)

    def c_yred(b):
        return remote(own.at[b, y_other], yred.at[b], s_yred.at[b], r_yred.at[b], y_peer)

    def c_leafy(b):
        return remote(own.at[b, y_mine], leafy.at[b], s_leafy.at[b], r_leafy.at[b], near)

    def c_leafz(b):
        return remote(own.at[b, pl.ds(2, 2)], leafz.at[b], s_leafz.at[b], r_leafz.at[b], near)

    def c_midy(b):
        return remote(own.at[b, y_mine], midy.at[b], s_midy.at[b], r_midy.at[b], across)

    def c_midz(b):
        return remote(own.at[b, z_other], midz.at[b], s_midz.at[b], r_midz.at[b], across)

    def c_yz(b):
        return remote(own.at[b, z_mine], yz.at[b], s_yz.at[b], r_yz.at[b], y_peer)

    def piece(b, k):
        return fin.at[b, half + k]

    def c_toty(b):
        return remote(piece(b, y_mine), piece(b, y_mine), s_toty.at[b], r_toty.at[b], near)

    def c_boty(b):
        return remote(piece(b, y_mine), piece(b, y_mine), s_boty.at[b], r_boty.at[b], y_peer)

    def c_totz(b):
        return remote(piece(b, z_mine), piece(b, z_mine), s_totz.at[b], r_totz.at[b], across)

    def c_lz(b, which):
        k = z_mine if which == 0 else z_other
        return remote(piece(b, k), piece(b, k), s_lz.at[which, b], r_lz.at[which, b], near)

    def c_ag(b, k):
        return remote(piece(b, k), piece(b, k), s_ag.at[k, b], r_ag.at[k, b], core_peer)

    vec_to = (core_peer, y_peer, near, across, near)

    def c_vec(h):
        return remote(vec.at[h], vrecv.at[h], s_vec.at[h], r_vec.at[h], vec_to[h])

    def c_nrm():
        return remote(nrm, nrecv, s_nrm, r_nrm, pipe_peer)

    def c_load(w, which):
        slot = w % 2
        if which == 0:
            return pltpu.make_async_copy(a_hbm.at[a_index(w)], abuf.at[slot], absem.at[0, slot])
        return pltpu.make_async_copy(b_hbm.at[b_index(w)], bbuf.at[slot], absem.at[1, slot])

    def add(*values):
        total = values[0].astype(F32)
        for v in values[1:]:
            total = total + v.astype(F32)
        return total

    for which in range(2):
        c_load(0, which).start()

    barrier = pltpu.get_barrier_semaphore()
    for device in (core_peer, y_peer, near, pipe_peer):
        pl.semaphore_signal(barrier, inc=1, device_id=device, device_id_type=MESH)

    @pl.when(mid)
    def _():
        pl.semaphore_signal(barrier, inc=1, device_id=across, device_id_type=MESH)
        pl.semaphore_wait(barrier, 5)

    @pl.when(leaf)
    def _():
        pl.semaphore_wait(barrier, 4)

    row = lax.broadcasted_iota(jnp.int32, (16, d), 0)
    total = None
    for m in range(n_mb):
        value = jnp.where(row < 12, small[m], 0.0)
        squares = value * value * jnp.where(row == 7, 2.0, 1.0)
        folded = squares[:8] + squares[8:]
        nrm[m] = sum(folded[:, k * 128 : (k + 1) * 128] for k in range(d // 128))
        total = value if total is None else total + value
    vec[0] = total
    c_vec(0).start()

    def weight_block(b):
        slot = b % 2
        w, part = b // SPLITS, b % SPLITS
        wslot = w % 2

        @pl.when(part == 0)
        def _():
            for which in range(2):
                c_load(w, which).wait()

        @pl.when((part == 0) & (w + 1 < nb // SPLITS))
        def _():
            for which in range(2):
                c_load(w + 1, which).start()

        @pl.when(b >= 2)
        def _():
            c_core(b - 2).wait_send()

        step = 256
        lhs = pl.ds(pl.multiple_of(part * (d // SPLITS), 128), d // SPLITS)
        for c in range(d // step):
            cols = slice(c * step, (c + 1) * step)
            total = None
            for m in range(n_mb):
                grad = dot_tn(abuf[wslot, m, :, lhs], bbuf[wslot, m, :, cols])
                squares = jnp.sum((grad * grad).reshape(-1, 8, step), axis=0)
                nrm[m] += squares[:, :128] + squares[:, 128:]
                total = grad if total is None else total + grad
            total = total.astype(BF16).reshape(2, PIECES, -1, step)

            @pl.when(core == 0)
            def _():
                own[b, :, :, cols] = total[0]
                csend[slot, :, :, cols] = total[1]

            @pl.when(core == 1)
            def _():
                own[b, :, :, cols] = total[1]
                csend[slot, :, :, cols] = total[0]

        c_core(b).start()

    def lag1(b):
        c_core(b).wait_recv()
        for k in range(PIECES):
            own[b, k] = add(own[b, k], crecv[b, k]).astype(BF16)
        c_yred(b).start()

        @pl.when(leaf)
        def _():
            c_leafz(b).start()

    def lag2(b):
        @pl.when(mid)
        def _():
            c_leafz(b).wait_recv()
            for k in range(2):
                own[b, 2 + k] = add(own[b, 2 + k], leafz[b, k]).astype(BF16)
            c_midz(b).start()

        c_yred(b).wait_recv()
        own[b, y_mine] = add(own[b, y_mine], yred[b]).astype(BF16)

        @pl.when(leaf)
        def _():
            c_leafy(b).start()

    def lag3(b):
        @pl.when(mid)
        def _():
            c_midz(b).wait_recv()
            own[b, z_mine] = add(own[b, z_mine], midz[b]).astype(BF16)
            c_yz(b).start()
            c_leafy(b).wait_recv()
            own[b, y_mine] = add(own[b, y_mine], leafy[b]).astype(BF16)
            c_midy(b).start()

    def lag4(b):
        @pl.when(mid)
        def _():
            c_yz(b).wait_recv()
            fin[b, half + z_mine] = add(own[b, z_mine], yz[b]).astype(BF16)
            c_totz(b).start()
            c_lz(b, 0).start()
            c_ag(b, z_mine).start()
            c_midy(b).wait_recv()
            fin[b, half + y_mine] = add(own[b, y_mine], midy[b]).astype(BF16)
            c_toty(b).start()
            c_boty(b).start()
            c_ag(b, y_mine).start()

    def lag5(b):
        @pl.when(mid)
        def _():
            c_totz(b).wait_recv()
            c_lz(b, 1).start()
            c_ag(b, z_other).start()
            c_boty(b).wait_recv()
            c_ag(b, y_other).start()

        @pl.when(leaf)
        def _():
            c_toty(b).wait_recv()
            c_boty(b).start()
            c_ag(b, y_mine).start()
            c_lz(b, 0).wait_recv()
            c_ag(b, z_mine).start()

    def lag6(b):
        @pl.when(leaf)
        def _():
            c_boty(b).wait_recv()
            c_ag(b, y_other).start()
            c_lz(b, 1).wait_recv()
            c_ag(b, z_other).start()

    def out_copies(b, act):
        w = b // SPLITS
        rows = pl.ds((b % SPLITS) * 2 * PIECES, 2 * PIECES)

        @pl.when(w // 4 == 0)
        def _():
            cols = pl.ds(pl.multiple_of(w * d, 128), d)
            act(pltpu.make_async_copy(fin.at[b], out_in.at[rows, :, cols], outsem.at[b]))

        @pl.when(w // 4 == 1)
        def _():
            act(pltpu.make_async_copy(fin.at[b], out_out.at[w - 4, rows], outsem.at[b]))

        @pl.when((w // 4 == 2) & (w < 11))
        def _():
            cols = pl.ds(pl.multiple_of((w - 8) * d, 128), d)
            act(pltpu.make_async_copy(fin.at[b], out_qkv.at[rows, :, cols], outsem.at[b]))

        @pl.when(w == 11)
        def _():
            act(pltpu.make_async_copy(fin.at[b], out_dense.at[rows], outsem.at[b]))

    def lag7(b):
        for k in range(PIECES):
            c_ag(b, k).wait_recv()
        out_copies(b, lambda c: c.start())

    def vector_steps(t):
        @pl.when(t == 1)
        def _():
            c_vec(0).wait_recv()
            vec[1] = vec[0] + vrecv[0]
            c_vec(1).start()

        @pl.when(t == 2)
        def _():
            c_vec(1).wait_recv()
            vec[2] = vec[1] + vrecv[1]

            @pl.when(leaf)
            def _():
                c_vec(2).start()

        @pl.when((t == 3) & mid)
        def _():
            c_vec(2).wait_recv()
            vec[3] = vec[2] + vrecv[2]
            c_vec(3).start()

        @pl.when((t == 4) & mid)
        def _():
            c_vec(3).wait_recv()
            vec[4] = vec[3] + vrecv[3]
            c_vec(4).start()
            out_vec[...] = vec[4]

        @pl.when((t == 5) & leaf)
        def _():
            c_vec(4).wait_recv()
            out_vec[...] = vrecv[4]

        @pl.when(t == nb)
        def _():
            c_nrm().start()

    stages = (weight_block, lag1, lag2, lag3, lag4, lag5, lag6, lag7)

    def step(t, carry):
        for lag, stage in enumerate(stages):

            @pl.when((t >= lag) & (t - lag < nb))
            def _(lag=lag, stage=stage):
                stage(t - lag)

        vector_steps(t)
        return carry

    lax.fori_loop(0, nb + len(stages) - 1, step, 0)

    c_nrm().wait_recv()
    out_nrm[...] = nrm[...] + nrecv[...]
    c_nrm().wait_send()
    c_vec(0).wait_send()
    c_vec(1).wait_send()
    c_core(nb - 2).wait_send()
    c_core(nb - 1).wait_send()

    @pl.when(leaf)
    def _():
        c_vec(2).wait_send()

    @pl.when(mid)
    def _():
        c_vec(3).wait_send()
        c_vec(4).wait_send()

    def drain(b, carry):
        c_yred(b).wait_send()
        c_boty(b).wait_send()
        for k in range(PIECES):
            c_ag(b, k).wait_send()

        @pl.when(leaf)
        def _():
            c_leafy(b).wait_send()
            c_leafz(b).wait_send()

        @pl.when(mid)
        def _():
            c_midy(b).wait_send()
            c_midz(b).wait_send()
            c_yz(b).wait_send()
            c_toty(b).wait_send()
            c_totz(b).wait_send()
            c_lz(b, 0).wait_send()
            c_lz(b, 1).wait_send()

        out_copies(b, lambda c: c.wait())
        return carry

    lax.fori_loop(0, nb, drain, 0)


def gradient_call(a, b, small):
    n_mb, seq, d = a.shape[1:]
    nb = 12 * SPLITS
    lead = 2 * PIECES * SPLITS
    rows = d // lead
    vmem = pl.BlockSpec(memory_space=pltpu.VMEM)
    hbm = pl.BlockSpec(memory_space=pl.ANY)
    dma = pltpu.SemaphoreType.DMA

    def wide(columns):
        return jax.ShapeDtypeStruct((lead, rows, columns), BF16)

    def slots(*lead):
        return pltpu.VMEM(lead + (rows, d), BF16)

    return pl.pallas_call(
        functools.partial(gradient_kernel, nb),
        out_shape=(
            wide(4 * d),
            jax.ShapeDtypeStruct((4, lead, rows, d), BF16),
            wide(3 * d),
            wide(d),
            jax.ShapeDtypeStruct((16, d), F32),
            jax.ShapeDtypeStruct((n_mb, 8, 128), F32),
        ),
        in_specs=[hbm, hbm, vmem],
        out_specs=(hbm, hbm, hbm, hbm, vmem, vmem),
        scratch_shapes=[
            pltpu.VMEM((2, n_mb, seq, d), BF16),
            pltpu.VMEM((2, n_mb, seq, d), BF16),
            slots(nb, PIECES),
            slots(2, PIECES),
            slots(nb, PIECES),
            slots(nb, 2 * PIECES),
            slots(nb),
            slots(nb),
            slots(nb, 2),
            slots(nb),
            slots(nb),
            slots(nb),
            pltpu.VMEM((5, 16, d), F32),
            pltpu.VMEM((5, 16, d), F32),
            pltpu.VMEM((n_mb, 8, 128), F32),
            pltpu.VMEM((n_mb, 8, 128), F32),
            dma((2, 2)),
            dma((nb,)),
            dma((2,)),
            dma((nb,)),
        ]
        + [dma((nb,)) for _ in range(18)]
        + [dma((2, nb)), dma((2, nb)), dma((PIECES, nb)), dma((PIECES, nb)), dma((5,)), dma((5,)), dma, dma],
        compiler_params=pltpu.CompilerParams(
            collective_id=1, has_side_effects=True, vmem_limit_bytes=62 * 2**20
        ),
        cost_estimate=pl.CostEstimate(
            flops=24 * n_mb * seq * d * d, bytes_accessed=64 * 2**20, transcendentals=0
        ),
    )(a, b, small)


def on_device(size, inputs, cotangent, lengths, *params):
    n_mb, seq, d = inputs.shape
    tables = jnp.asarray(rotary_tables(seq))
    out_y, out_dx, a, b, small = section_call(lengths, inputs, cotangent, params, tables)
    w_in, w_out, w_qkv, w_dense, vectors, nrm = gradient_call(a, b, small)
    sums = [w_in, w_out, w_qkv, w_dense, vectors]
    if size > 16:
        groups = [[g * 16 + r for g in range(size // 16)] for r in range(16)]
        sums = [lax.psum(v, "dp", axis_index_groups=groups) for v in sums]
    w_in, w_out, w_qkv, w_dense, vectors = [v.astype(F32) for v in sums]
    norms = jnp.sum(nrm, axis=(1, 2))
    rows = [vectors[k : k + 1] for k in range(12)]
    return (
        out_y,
        out_dx,
        rows[0],
        rows[1],
        w_qkv.reshape(1, d, 3 * d),
        vectors[4:7].reshape(1, 3 * d),
        w_dense.reshape(1, d, d),
        rows[7],
        rows[2],
        rows[3],
        w_in.reshape(1, d, 4 * d),
        vectors[8:12].reshape(1, 4 * d),
        w_out.reshape(1, 4 * d, d),
        rows[7],
        norms,
    )


def solution(mesh):
    matrix, vector = P("pipe", None, None), P("pipe", None)
    weights = (vector, vector, matrix, vector, matrix, vector) * 2
    tokens = P("dp", None, None)
    return jax.shard_map(
        functools.partial(on_device, mesh.shape["dp"]),
        mesh=mesh,
        in_specs=(tokens, tokens, P("dp")) + weights,
        out_specs=(P("pipe", "dp", None, None),) * 2 + weights + (P("dp"),),
        check_vma=False,
    )
```

```python
import functools

import jax
import jax.numpy as jnp
import numpy as np
from jax import lax
from jax.experimental import pallas as pl
from jax.experimental.pallas import tpu as pltpu
from jax.sharding import PartitionSpec as P

HEADS = 12
HEAD = 64
ROT = 16
EPSILON = 1e-05
NEG_FILL = -1e30
INV_ROOT_TWO = 0.7071067811865476
INV_ROOT_TWO_PI = 0.3989422804014327
MESH = pl.DeviceIdType.MESH
F32 = jnp.float32
BF16 = jnp.bfloat16


def dot_nn(a, b):
    return jnp.dot(a, b, preferred_element_type=F32)


def dot_nt(a, b):
    return lax.dot_general(a, b, (((1,), (1,)), ((), ())), preferred_element_type=F32)


def dot_tn(a, b):
    return lax.dot_general(a, b, (((0,), (0,)), ((), ())), preferred_element_type=F32)


def rotary_tables(seq):
    half = ROT // 2
    freq = 10000.0 ** (-2.0 * np.arange(half) / ROT)
    angle = np.arange(seq)[:, None] * freq[None, :]
    cosine, sine = np.cos(angle), np.sin(angle)
    own = np.ones((seq, HEAD))
    up = np.zeros((seq, HEAD))
    down = np.zeros((seq, HEAD))
    own[:, :half] = cosine
    own[:, half:ROT] = cosine
    up[:, half:ROT] = sine
    down[:, :half] = -sine
    tables = np.stack([np.concatenate([t, t], axis=1) for t in (own, up, down)])
    return tables.astype(np.float32)


def section_kernel(
    n_mb,
    lens,
    inputs,
    cot,
    g1,
    b1,
    wqkv,
    bqkv,
    wd,
    bd,
    g2,
    b2,
    wi,
    bi,
    wo,
    bo,
    tables,
    out_y,
    out_dx,
    a_hbm,
    b_hbm,
    small,
    wqkv_v,
    wd_v,
    wi_v,
    wo_v,
    xb,
    av,
    bv,
    pb,
    yb,
    dxb,
    acc,
    dctx_v,
    bias_v,
    wsem,
    insem,
    cotsem,
    ysem,
    dxsem,
    asem,
    bsem,
    fsend,
    frecv,
    bsend,
    brecv,
):
    section = lax.axis_index("pipe")
    first = section == 0
    last = section == 1
    peer = 1 - section
    seq, d = xb.shape[1], xb.shape[2]
    pairs = d // 128

    wcopies = [
        pltpu.make_async_copy(src.at[0], dst, wsem.at[k])
        for k, (src, dst) in enumerate(((wqkv, wqkv_v), (wd, wd_v), (wi, wi_v), (wo, wo_v)))
    ]

    @pl.when(first)
    def _():
        pltpu.make_async_copy(inputs, xb, insem).start()

    for c in wcopies:
        c.start()

    @pl.when(last)
    def _():
        pltpu.make_async_copy(cot, bv.at[4], cotsem).start()

    barrier = pltpu.get_barrier_semaphore()
    pl.semaphore_signal(barrier, inc=1, device_id={"pipe": peer}, device_id_type=MESH)
    pl.semaphore_wait(barrier, 1)

    def fcopy(i):
        return pltpu.make_async_remote_copy(
            src_ref=yb.at[i],
            dst_ref=xb.at[i],
            send_sem=fsend.at[i],
            recv_sem=frecv.at[i],
            device_id={"pipe": peer},
            device_id_type=MESH,
        )

    def bcopy(i):
        return pltpu.make_async_remote_copy(
            src_ref=dxb.at[i],
            dst_ref=bv.at[4, i],
            send_sem=bsend.at[i],
            recv_sem=brecv.at[i],
            device_id={"pipe": peer},
            device_id_type=MESH,
        )

    lane = lax.broadcasted_iota(jnp.int32, (seq, 128), 1)
    lower = lane < HEAD

    def pick(value, a):
        return jnp.where(lower if a == 0 else jnp.logical_not(lower), value, jnp.zeros_like(value))

    def rotate(w, sign):
        return (
            w * tables[0]
            + sign * (pltpu.roll(w, ROT // 2, 1) * tables[1] + pltpu.roll(w, 128 - ROT // 2, 1) * tables[2])
        )

    def unit_of(i):
        x = xb[i].astype(F32)
        center = x - jnp.mean(x, axis=-1, keepdims=True)
        inverse = lax.rsqrt(jnp.mean(center * center, axis=-1, keepdims=True) + EPSILON)
        return x, center * inverse, inverse

    def pair_columns(h):
        return slice((h // 2) * 128, (h // 2 + 1) * 128)

    def pipelined(stages, count, extra):
        for t in range(count + max(lag for lag, _ in stages)):
            for run in extra.get(t, ()):
                run()
            for lag, stage in stages:
                if 0 <= t - lag < count:
                    stage(t - lag)

    def feed_slots(feed_in, feed_mid, feed_out):
        slots = {}
        for k in range(6):
            runs = []
            for lag, stage in ((2, feed_out), (1, feed_mid), (0, feed_in)):
                if 0 <= k - lag < 4:
                    runs.append(functools.partial(stage, k - lag))
            slots[(5 * k) // 2] = runs
        return slots

    def forward(i):
        @pl.when(last)
        def _():
            fcopy(i).wait_recv()

        x, unit, inverse = unit_of(i)
        a1 = (unit * g1[...] + b1[...]).astype(BF16)
        a2 = (unit * g2[...] + b2[...]).astype(BF16)
        av[5, i] = a1
        av[0, i] = a2

        @pl.when(i == 0)
        def _():
            wcopies[0].wait()

        mixed = {}

        def project(t):
            mixed[t] = dot_nn(a1, wqkv_v[:, t * d : (t + 1) * d]) + bqkv[:, t * d : (t + 1) * d]

        def settle(t):
            if t == 2:
                bv[7, i] = mixed[2].astype(BF16)
                return
            for hp in range(pairs):
                w = rotate(mixed[t][:, hp * 128 : (hp + 1) * 128], 1.0)
                if t == 0:
                    w = w * HEAD ** (-0.5)
                bv[5 + t, i, :, hp * 128 : (hp + 1) * 128] = w.astype(BF16)

        pipelined(((0, project), (1, settle)), 3, {})
        key = lax.broadcasted_iota(jnp.int32, (seq, seq), 0)
        query = lax.broadcasted_iota(jnp.int32, (seq, seq), 1)
        bias_v[...] = jnp.where((key <= query) & (key < lens[i]), 0.0, NEG_FILL)

        @pl.when(i == 0)
        def _():
            for k in (1, 2, 3):
                wcopies[k].wait()

        acc[...] = xb[i].astype(F32) + bd[...] + bo[...]
        scores, probs, parts, hidden = {}, {}, {}, {}

        def head_scores(h):
            cols = pair_columns(h)
            scores[h] = dot_nt(pick(bv[6, i, :, cols], h % 2), bv[5, i, :, cols])

        def head_softmax(h):
            value = scores.pop(h) + bias_v[...]
            expo = jnp.exp(value - jnp.max(value, axis=0, keepdims=True))
            probs[h] = (expo * (1.0 / jnp.sum(expo, axis=0, keepdims=True))).astype(BF16)
            pb[i, h] = probs[h]

        def head_context(h):
            cols = pair_columns(h)
            parts[h] = dot_tn(probs.pop(h), pick(bv[7, i, :, cols], h % 2))
            if h % 2 == 1:
                av[6, i, :, cols] = (parts.pop(h - 1) + parts.pop(h)).astype(BF16)

        def feed_in(j):
            cols = slice(j * d, (j + 1) * d)
            hidden[j] = dot_nn(av[0, i], wi_v[:, cols]) + bi[:, cols]

        def feed_gate(j):
            value = hidden.pop(j)
            gate = 0.5 * (1.0 + lax.erf(value * INV_ROOT_TWO))
            av[1 + j, i] = (value * gate).astype(BF16)
            bv[j, i] = (gate + value * jnp.exp(-0.5 * value * value) * INV_ROOT_TWO_PI).astype(BF16)

        def feed_out(j):
            acc[...] += dot_nn(av[1 + j, i], wo_v[j * d : (j + 1) * d, :])

        pipelined(
            ((0, head_scores), (2, head_softmax), (3, head_context)),
            HEADS,
            feed_slots(feed_in, feed_gate, feed_out),
        )
        yb[i] = (acc[...] + dot_nn(av[6, i], wd_v[...])).astype(BF16)

        @pl.when(first)
        def _():
            fcopy(i).start()

        pltpu.make_async_copy(yb.at[i], out_y.at[0, i], ysem.at[i]).start()
        for k in range(7):
            pltpu.make_async_copy(av.at[k, i], a_hbm.at[k, i], asem.at[k, i]).start()

    def backward(i):
        @pl.when(first)
        def _():
            bcopy(i).wait_recv()

        @pl.when(last)
        def _():
            row = lax.broadcasted_iota(jnp.int32, (seq, d), 0)
            value = bv[4, i].astype(F32)
            bv[4, i] = jnp.where(row < lens[i], value, 0.0).astype(BF16)

        gy = bv[4, i]
        small[i, 7:8, :] = jnp.sum(gy.astype(F32), axis=0, keepdims=True)
        acc[...] = jnp.zeros_like(acc)

        dctx_v[...] = dot_nt(gy, wd_v[...]).astype(BF16)
        dact, dprob, ds, dmix = {}, {}, {}, {}

        def feed_in(j):
            dact[j] = dot_nt(bv[4, i], wo_v[j * d : (j + 1) * d, :])

        def feed_slope(j):
            dh = (dact.pop(j) * bv[j, i].astype(F32)).astype(BF16)
            bv[j, i] = dh
            small[i, 8 + j : 9 + j, :] = jnp.sum(dh.astype(F32), axis=0, keepdims=True)

        def feed_out(j):
            acc[...] += dot_nt(bv[j, i], wi_v[:, j * d : (j + 1) * d])

        def head_dprob(h):
            cols = pair_columns(h)
            dprob[h] = dot_nt(pick(bv[7, i, :, cols], h % 2), dctx_v[:, cols])

        def head_dscores(h):
            pf = pb[i, h].astype(F32)
            prod = dprob.pop(h) * pf
            ds[h] = (prod - pf * jnp.sum(prod, axis=0, keepdims=True)).astype(BF16)

        def head_products(h):
            cols = pair_columns(h)
            value = ds.pop(h)
            dv = dot_nn(pb[i, h], pick(dctx_v[:, cols], h % 2))
            dk = dot_nn(value, pick(bv[5, i, :, cols], h % 2))
            dq = dot_tn(value, pick(bv[6, i, :, cols], h % 2))
            dmix[h] = (dq, dk, dv)

        def pair_settle(h):
            if h % 2 == 0:
                return
            cols = pair_columns(h)
            dq, dk, dv = [p + q for p, q in zip(dmix.pop(h - 1), dmix.pop(h))]
            for t, w in ((0, rotate(dq * HEAD ** (-0.5), -1.0)), (1, rotate(dk, -1.0)), (2, dv)):
                w = w.astype(BF16)
                bv[5 + t, i, :, cols] = w
                small[i, 4 + t : 5 + t, cols] = jnp.sum(w.astype(F32), axis=0, keepdims=True)

        pipelined(
            ((0, head_dprob), (2, head_dscores), (3, head_products), (4, pair_settle)),
            HEADS,
            feed_slots(feed_in, feed_slope, feed_out),
        )
        da1 = dot_nt(bv[5, i], wqkv_v[:, 0:d])
        da1 = da1 + dot_nt(bv[6, i], wqkv_v[:, d : 2 * d])
        da1 = da1 + dot_nt(bv[7, i], wqkv_v[:, 2 * d : 3 * d])
        da2 = acc[...]
        x, unit, inverse = unit_of(i)
        small[i, 0:1, :] = jnp.sum(da1 * unit, axis=0, keepdims=True)
        small[i, 1:2, :] = jnp.sum(da1, axis=0, keepdims=True)
        small[i, 2:3, :] = jnp.sum(da2 * unit, axis=0, keepdims=True)
        small[i, 3:4, :] = jnp.sum(da2, axis=0, keepdims=True)
        scaled = da1 * g1[...] + da2 * g2[...]
        mean_g = jnp.mean(scaled, axis=-1, keepdims=True)
        mean_gn = jnp.mean(scaled * unit, axis=-1, keepdims=True)
        dx = bv[4, i].astype(F32) + inverse * (scaled - mean_g - unit * mean_gn)
        dxb[i] = dx.astype(BF16)

        @pl.when(last)
        def _():
            bcopy(i).start()

        pltpu.make_async_copy(dxb.at[i], out_dx.at[0, i], dxsem.at[i]).start()
        for k in range(8):
            pltpu.make_async_copy(bv.at[k, i], b_hbm.at[k, i], bsem.at[k, i]).start()

    @pl.when(first)
    def _():
        pltpu.make_async_copy(inputs, xb, insem).wait()

    @pl.when(last)
    def _():
        pltpu.make_async_copy(cot, bv.at[4], cotsem).wait()

    def tick(step, carry):
        phase = section * (step % 2) + (1 - section) * (step // n_mb)
        mb = section * (step // 2) + (1 - section) * (step % n_mb)

        @pl.when(phase == 0)
        def _():
            forward(mb)

        @pl.when(phase == 1)
        def _():
            backward(mb)

        return carry

    lax.fori_loop(0, 2 * n_mb, tick, 0)

    def drain(i, carry):
        @pl.when(first)
        def _():
            fcopy(i).wait_send()

        @pl.when(last)
        def _():
            bcopy(i).wait_send()

        pltpu.make_async_copy(yb.at[i], out_y.at[0, i], ysem.at[i]).wait()
        pltpu.make_async_copy(dxb.at[i], out_dx.at[0, i], dxsem.at[i]).wait()
        for k in range(7):
            pltpu.make_async_copy(av.at[k, i], a_hbm.at[k, i], asem.at[k, i]).wait()
        for k in range(8):
            pltpu.make_async_copy(bv.at[k, i], b_hbm.at[k, i], bsem.at[k, i]).wait()
        return carry

    lax.fori_loop(0, n_mb, drain, 0)


def section_call(lens, inputs, cot, params, tables):
    n_mb, seq, d = inputs.shape
    g1, b1, wqkv, bqkv, wd, bd, g2, b2, wi, bi, wo, bo = params
    ff = wi.shape[2]
    vmem = pl.BlockSpec(memory_space=pltpu.VMEM)
    smem = pl.BlockSpec(memory_space=pltpu.SMEM)
    hbm = pl.BlockSpec(memory_space=pl.ANY)
    dma = pltpu.SemaphoreType.DMA
    flops = n_mb * 2 * seq * (3 * d * d + d * d + 2 * d * ff) * 2
    return pl.pallas_call(
        functools.partial(section_kernel, n_mb),
        out_shape=(
            jax.ShapeDtypeStruct((1, n_mb, seq, d), BF16),
            jax.ShapeDtypeStruct((1, n_mb, seq, d), BF16),
            jax.ShapeDtypeStruct((7, n_mb, seq, d), BF16),
            jax.ShapeDtypeStruct((8, n_mb, seq, d), BF16),
            jax.ShapeDtypeStruct((n_mb, 16, d), F32),
        ),
        in_specs=[smem, hbm, hbm, vmem, vmem, hbm, vmem, hbm, vmem, vmem, vmem, hbm, vmem, hbm, vmem, vmem],
        out_specs=(hbm, hbm, hbm, hbm, vmem),
        scratch_shapes=[
            pltpu.VMEM((d, 3 * d), BF16),
            pltpu.VMEM((d, d), BF16),
            pltpu.VMEM((d, ff), BF16),
            pltpu.VMEM((ff, d), BF16),
            pltpu.VMEM((n_mb, seq, d), BF16),
            pltpu.VMEM((7, n_mb, seq, d), BF16),
            pltpu.VMEM((8, n_mb, seq, d), BF16),
            pltpu.VMEM((n_mb, HEADS, seq, seq), BF16),
            pltpu.VMEM((n_mb, seq, d), BF16),
            pltpu.VMEM((n_mb, seq, d), BF16),
            pltpu.VMEM((seq, d), F32),
            pltpu.VMEM((seq, d), BF16),
            pltpu.VMEM((seq, seq), F32),
            dma((4,)),
            dma,
            dma,
            dma((n_mb,)),
            dma((n_mb,)),
            dma((7, n_mb)),
            dma((8, n_mb)),
            dma((n_mb,)),
            dma((n_mb,)),
            dma((n_mb,)),
            dma((n_mb,)),
        ],
        compiler_params=pltpu.CompilerParams(
            collective_id=0, has_side_effects=True, vmem_limit_bytes=62 * 2**20
        ),
        cost_estimate=pl.CostEstimate(flops=flops, bytes_accessed=40 * 2**20, transcendentals=0),
    )(lens, inputs, cot, g1, b1, wqkv, bqkv, wd, bd, g2, b2, wi, bi, wo, bo, tables)


PIECES = 4
SPLITS = 2


def a_index(b):
    g = b // 4
    return g * (2 - g) * (b - 3) + (g * (g - 1) // 2) * 5 + b // 11


def b_index(b):
    g = b // 4
    middle, late = g * (2 - g), g * (g - 1) // 2
    return (1 - middle - late) * b + middle * 4 + late * (b - 3) - (b // 11) * 4


def gradient_kernel(
    nb,
    a_hbm,
    b_hbm,
    small,
    out_all,
    out_vec,
    out_nrm,
    abuf,
    bbuf,
    own,
    csend,
    crecv,
    yred,
    leafy,
    leafz,
    midy,
    midz,
    yz,
    vec,
    vrecv,
    nrm,
    nrecv,
    absem,
    s_core,
    r_core,
    s_yred,
    r_yred,
    s_leafy,
    r_leafy,
    s_leafz,
    r_leafz,
    s_midy,
    r_midy,
    s_midz,
    r_midz,
    s_yz,
    r_yz,
    s_toty,
    r_toty,
    s_boty,
    r_boty,
    s_totz,
    r_totz,
    s_lz,
    r_lz,
    s_ag,
    r_ag,
    s_vec,
    r_vec,
    s_nrm,
    r_nrm,
):
    n_mb, seq, d = abuf.shape[1:]
    pipe = lax.axis_index("pipe")
    me = lax.axis_index("dp")
    group, inner = me // 16, me % 16
    z, y, core = inner // 4, (inner // 2) % 2, inner % 2
    mid = (z // 2 + z % 2) == 1
    leaf = jnp.logical_not(mid)

    def at(z_, y_, core_):
        return {"dp": group * 16 + (z_ * 2 + y_) * 2 + core_}

    core_peer = at(z, y, 1 - core)
    y_peer = at(z, 1 - y, core)
    near = at(z + 1 - 2 * (z % 2), y, core)
    across = at(3 - z, y, core)
    pipe_peer = {"pipe": 1 - pipe}
    zi = z // 2
    y_mine, y_other = y, 1 - y
    z_mine, z_other = 2 + zi, 3 - zi
    half = core * PIECES

    def remote(src, dst, send, recv, device):
        return pltpu.make_async_remote_copy(
            src_ref=src, dst_ref=dst, send_sem=send, recv_sem=recv, device_id=device, device_id_type=MESH
        )

    def c_core(b):
        return remote(csend.at[b % 2], crecv.at[b], s_core.at[b % 2], r_core.at[b], core_peer)

    def c_yred(b):
        return remote(own.at[b, y_other], yred.at[b], s_yred.at[b], r_yred.at[b], y_peer)

    def c_leafy(b):
        return remote(own.at[b, y_mine], leafy.at[b], s_leafy.at[b], r_leafy.at[b], near)

    def c_leafz(b):
        return remote(own.at[b, pl.ds(2, 2)], leafz.at[b], s_leafz.at[b], r_leafz.at[b], near)

    def c_midy(b):
        return remote(own.at[b, y_mine], midy.at[b], s_midy.at[b], r_midy.at[b], across)

    def c_midz(b):
        return remote(own.at[b, z_other], midz.at[b], s_midz.at[b], r_midz.at[b], across)

    def c_yz(b):
        return remote(own.at[b, z_mine], yz.at[b], s_yz.at[b], r_yz.at[b], y_peer)

    def piece(b, k):
        return out_all.at[b, half + k]

    def c_toty(b):
        return remote(piece(b, y_mine), piece(b, y_mine), s_toty.at[b], r_toty.at[b], near)

    def c_boty(b):
        return remote(piece(b, y_mine), piece(b, y_mine), s_boty.at[b], r_boty.at[b], y_peer)

    def c_totz(b):
        return remote(piece(b, z_mine), piece(b, z_mine), s_totz.at[b], r_totz.at[b], across)

    def c_lz(b, which):
        k = z_mine if which == 0 else z_other
        return remote(piece(b, k), piece(b, k), s_lz.at[which, b], r_lz.at[which, b], near)

    def c_ag(b, k):
        return remote(piece(b, k), piece(b, k), s_ag.at[k, b], r_ag.at[k, b], core_peer)

    def finish(b, k):
        c_ag(b, k).start()

    vec_to = (core_peer, y_peer, near, across, near)

    def c_vec(h):
        return remote(vec.at[h], vrecv.at[h], s_vec.at[h], r_vec.at[h], vec_to[h])

    def c_nrm():
        return remote(nrm, nrecv, s_nrm, r_nrm, pipe_peer)

    def c_load(w, which):
        slot = w % 2
        if which == 0:
            return pltpu.make_async_copy(a_hbm.at[a_index(w)], abuf.at[slot], absem.at[0, slot])
        return pltpu.make_async_copy(b_hbm.at[b_index(w)], bbuf.at[slot], absem.at[1, slot])

    def add(*values):
        total = values[0].astype(F32)
        for v in values[1:]:
            total = total + v.astype(F32)
        return total

    for which in range(2):
        c_load(0, which).start()

    barrier = pltpu.get_barrier_semaphore()
    for device in (core_peer, y_peer, near, pipe_peer):
        pl.semaphore_signal(barrier, inc=1, device_id=device, device_id_type=MESH)

    @pl.when(mid)
    def _():
        pl.semaphore_signal(barrier, inc=1, device_id=across, device_id_type=MESH)
        pl.semaphore_wait(barrier, 5)

    @pl.when(leaf)
    def _():
        pl.semaphore_wait(barrier, 4)

    row = lax.broadcasted_iota(jnp.int32, (16, d), 0)
    total = None
    for m in range(n_mb):
        value = jnp.where(row < 12, small[m], 0.0)
        squares = value * value * jnp.where(row == 7, 2.0, 1.0)
        folded = squares[:8] + squares[8:]
        nrm[m] = sum(folded[:, k * 128 : (k + 1) * 128] for k in range(d // 128))
        total = value if total is None else total + value
    vec[0] = total
    c_vec(0).start()

    def weight_block(b):
        slot = b % 2
        w, part = b // SPLITS, b % SPLITS
        wslot = w % 2

        @pl.when(part == 0)
        def _():
            for which in range(2):
                c_load(w, which).wait()

        @pl.when((part == 0) & (w + 1 < nb // SPLITS))
        def _():
            for which in range(2):
                c_load(w + 1, which).start()

        @pl.when(b >= 2)
        def _():
            c_core(b - 2).wait_send()

        step = 256
        lhs = pl.ds(pl.multiple_of(part * (d // SPLITS), 128), d // SPLITS)
        for c in range(d // step):
            cols = slice(c * step, (c + 1) * step)
            total = None
            for m in range(n_mb):
                grad = dot_tn(abuf[wslot, m, :, lhs], bbuf[wslot, m, :, cols])
                squares = jnp.sum((grad * grad).reshape(-1, 8, step), axis=0)
                nrm[m] += squares[:, :128] + squares[:, 128:]
                total = grad if total is None else total + grad
            total = total.astype(BF16).reshape(2, PIECES, -1, step)

            @pl.when(core == 0)
            def _():
                own[b, :, :, cols] = total[0]
                csend[slot, :, :, cols] = total[1]

            @pl.when(core == 1)
            def _():
                own[b, :, :, cols] = total[1]
                csend[slot, :, :, cols] = total[0]

        c_core(b).start()

    def lag1(b):
        c_core(b).wait_recv()
        for k in range(PIECES):
            own[b, k] = add(own[b, k], crecv[b, k]).astype(BF16)
        c_yred(b).start()

        @pl.when(leaf)
        def _():
            c_leafz(b).start()

    def lag2(b):
        @pl.when(mid)
        def _():
            c_leafz(b).wait_recv()
            for k in range(2):
                own[b, 2 + k] = add(own[b, 2 + k], leafz[b, k]).astype(BF16)
            c_midz(b).start()

        c_yred(b).wait_recv()
        own[b, y_mine] = add(own[b, y_mine], yred[b]).astype(BF16)

        @pl.when(leaf)
        def _():
            c_leafy(b).start()

    def lag3(b):
        @pl.when(mid)
        def _():
            c_midz(b).wait_recv()
            own[b, z_mine] = add(own[b, z_mine], midz[b]).astype(BF16)
            c_yz(b).start()
            c_leafy(b).wait_recv()
            own[b, y_mine] = add(own[b, y_mine], leafy[b]).astype(BF16)
            c_midy(b).start()

    def lag4(b):
        @pl.when(mid)
        def _():
            c_yz(b).wait_recv()
            out_all[b, half + z_mine] = add(own[b, z_mine], yz[b]).astype(BF16)
            c_totz(b).start()
            c_lz(b, 0).start()
            finish(b, z_mine)
            c_midy(b).wait_recv()
            out_all[b, half + y_mine] = add(own[b, y_mine], midy[b]).astype(BF16)
            c_toty(b).start()
            c_boty(b).start()
            finish(b, y_mine)

    def lag5(b):
        @pl.when(mid)
        def _():
            c_totz(b).wait_recv()
            c_lz(b, 1).start()
            finish(b, z_other)
            c_boty(b).wait_recv()
            finish(b, y_other)

        @pl.when(leaf)
        def _():
            c_toty(b).wait_recv()
            c_boty(b).start()
            finish(b, y_mine)
            c_lz(b, 0).wait_recv()
            finish(b, z_mine)

    def lag6(b):
        @pl.when(leaf)
        def _():
            c_boty(b).wait_recv()
            finish(b, y_other)
            c_lz(b, 1).wait_recv()
            finish(b, z_other)

    def vector_steps(t):
        @pl.when(t == 1)
        def _():
            c_vec(0).wait_recv()
            vec[1] = vec[0] + vrecv[0]
            c_vec(1).start()

        @pl.when(t == 2)
        def _():
            c_vec(1).wait_recv()
            vec[2] = vec[1] + vrecv[1]

            @pl.when(leaf)
            def _():
                c_vec(2).start()

        @pl.when((t == 3) & mid)
        def _():
            c_vec(2).wait_recv()
            vec[3] = vec[2] + vrecv[2]
            c_vec(3).start()

        @pl.when((t == 4) & mid)
        def _():
            c_vec(3).wait_recv()
            vec[4] = vec[3] + vrecv[3]
            c_vec(4).start()
            out_vec[...] = vec[4]

        @pl.when((t == 5) & leaf)
        def _():
            c_vec(4).wait_recv()
            out_vec[...] = vrecv[4]

        @pl.when(t == nb)
        def _():
            c_nrm().start()

    stages = (weight_block, lag1, lag2, lag3, lag4, lag5, lag6)

    def step(t, carry):
        for lag, stage in enumerate(stages):

            @pl.when((t >= lag) & (t - lag < nb))
            def _(lag=lag, stage=stage):
                stage(t - lag)

        vector_steps(t)
        return carry

    lax.fori_loop(0, nb + len(stages) - 1, step, 0)

    c_nrm().wait_recv()
    out_nrm[...] = nrm[...] + nrecv[...]
    c_nrm().wait_send()
    c_vec(0).wait_send()
    c_vec(1).wait_send()
    c_core(nb - 2).wait_send()
    c_core(nb - 1).wait_send()

    @pl.when(leaf)
    def _():
        c_vec(2).wait_send()

    @pl.when(mid)
    def _():
        c_vec(3).wait_send()
        c_vec(4).wait_send()

    def drain(b, carry):
        c_yred(b).wait_send()
        c_boty(b).wait_send()
        for k in range(PIECES):
            c_ag(b, k).wait()

        @pl.when(leaf)
        def _():
            c_leafy(b).wait_send()
            c_leafz(b).wait_send()

        @pl.when(mid)
        def _():
            c_midy(b).wait_send()
            c_midz(b).wait_send()
            c_yz(b).wait_send()
            c_toty(b).wait_send()
            c_totz(b).wait_send()
            c_lz(b, 0).wait_send()
            c_lz(b, 1).wait_send()

        return carry

    lax.fori_loop(0, nb, drain, 0)


def gradient_call(a, b, small, stay):
    n_mb, seq, d = a.shape[1:]
    nb = 12 * SPLITS
    rows = d // (2 * PIECES * SPLITS)
    summed = (nb, 2 * PIECES, rows, d)
    vmem = pl.BlockSpec(memory_space=pltpu.VMEM)
    hbm = pl.BlockSpec(memory_space=pl.ANY)
    dma = pltpu.SemaphoreType.DMA

    def slots(*lead):
        return pltpu.VMEM(lead + (rows, d), BF16)

    return pl.pallas_call(
        functools.partial(gradient_kernel, nb),
        out_shape=(
            pltpu.VMEM(summed, BF16) if stay else jax.ShapeDtypeStruct(summed, BF16),
            jax.ShapeDtypeStruct((16, d), F32),
            jax.ShapeDtypeStruct((n_mb, 8, 128), F32),
        ),
        in_specs=[hbm, hbm, vmem],
        out_specs=(vmem, vmem, vmem),
        scratch_shapes=[
            pltpu.VMEM((2, n_mb, seq, d), BF16),
            pltpu.VMEM((2, n_mb, seq, d), BF16),
            slots(nb, PIECES),
            slots(2, PIECES),
            slots(nb, PIECES),
            slots(nb),
            slots(nb),
            slots(nb, 2),
            slots(nb),
            slots(nb),
            slots(nb),
            pltpu.VMEM((5, 16, d), F32),
            pltpu.VMEM((5, 16, d), F32),
            pltpu.VMEM((n_mb, 8, 128), F32),
            pltpu.VMEM((n_mb, 8, 128), F32),
            dma((2, 2)),
            dma((2,)),
            dma((nb,)),
        ]
        + [dma((nb,)) for _ in range(18)]
        + [dma((2, nb)), dma((2, nb)), dma((PIECES, nb)), dma((PIECES, nb)), dma((5,)), dma((5,)), dma, dma],
        compiler_params=pltpu.CompilerParams(
            collective_id=1, has_side_effects=True, vmem_limit_bytes=(44 if stay else 60) * 2**20
        ),
        cost_estimate=pl.CostEstimate(
            flops=24 * n_mb * seq * d * d, bytes_accessed=64 * 2**20, transcendentals=0
        ),
    )(a, b, small)


def widen_kernel(
    blocks,
    y_in,
    dx_in,
    vec,
    nrm,
    out_y,
    out_dx,
    gain1,
    bias1,
    w_qkv,
    b_qkv,
    w_dense,
    b_dense,
    gain2,
    bias2,
    w_in,
    b_in,
    w_out,
    b_out,
    norms,
    narrow,
    wide,
    held,
    isem,
    osem,
    csem,
):
    d = wide.shape[2]
    reads = [
        pltpu.make_async_copy(blocks.at[pl.ds(w * SPLITS, SPLITS)], narrow.at[w % 4], isem.at[w % 4])
        for w in range(12)
    ]
    targets = [w_in.at[0, :, pl.ds(k * d, d)] for k in range(4)]
    targets += [w_out.at[0, pl.ds(k * d, d)] for k in range(4)]
    targets += [w_qkv.at[0, :, pl.ds(k * d, d)] for k in range(3)]
    targets += [w_dense.at[0]]
    writes = [pltpu.make_async_copy(wide.at[w], targets[w], osem.at[w]) for w in range(12)]
    copies = [
        pltpu.make_async_copy(held.at[0], out_y, csem.at[2]),
        pltpu.make_async_copy(held.at[1], out_dx, csem.at[3]),
    ]
    fetch = [
        pltpu.make_async_copy(y_in, held.at[0], csem.at[0]),
        pltpu.make_async_copy(dx_in, held.at[1], csem.at[1]),
    ]
    for c in fetch + reads[:3]:
        c.start()
    for row, refs in ((0, (gain1,)), (1, (bias1,)), (2, (gain2,)), (3, (bias2,)), (7, (b_dense, b_out))):
        for ref in refs:
            ref[...] = vec[row : row + 1, :]
    for k in range(3):
        b_qkv[:, k * d : (k + 1) * d] = vec[4 + k : 5 + k, :]
    for k in range(4):
        b_in[:, k * d : (k + 1) * d] = vec[8 + k : 9 + k, :]
    for m in range(nrm.shape[0]):
        norms[m] = jnp.sum(nrm[m])
    for w in range(12):
        if w + 3 < 12:
            reads[w + 3].start()
        reads[w].wait()
        wide[w] = narrow[w % 4].astype(F32).reshape(d, d)
        writes[w].start()
    for c in fetch:
        c.wait()
    for c in copies:
        c.start()
    for c in writes + copies:
        c.wait()


def widen_call(blocks, y, dx, vec, nrm):
    d = y.shape[3]
    vmem = pl.BlockSpec(memory_space=pltpu.VMEM)
    hbm = pl.BlockSpec(memory_space=pl.ANY)
    dma = pltpu.SemaphoreType.DMA

    def row(k):
        return jax.ShapeDtypeStruct((1, k * d), F32)

    def matrix(r, c):
        return jax.ShapeDtypeStruct((1, r * d, c * d), F32)

    same = jax.ShapeDtypeStruct(y.shape, BF16)
    return pl.pallas_call(
        widen_kernel,
        out_shape=(same, same, row(1), row(1), matrix(1, 3), row(3), matrix(1, 1), row(1))
        + (row(1), row(1), matrix(1, 4), row(4), matrix(4, 1), row(1))
        + (jax.ShapeDtypeStruct(nrm.shape[:1], F32),),
        in_specs=[hbm, hbm, hbm, vmem, vmem],
        out_specs=(hbm, hbm) + (vmem, vmem, hbm, vmem, hbm, vmem) * 2 + (pl.BlockSpec(memory_space=pltpu.SMEM),),
        scratch_shapes=[
            pltpu.VMEM((4, SPLITS) + blocks.shape[1:], BF16),
            pltpu.VMEM((12, d, d), F32),
            pltpu.VMEM((2,) + y.shape, BF16),
            dma((4,)),
            dma((12,)),
            dma((4,)),
        ],
        compiler_params=pltpu.CompilerParams(vmem_limit_bytes=42 * 2**20),
        cost_estimate=pl.CostEstimate(flops=12 * d * d, bytes_accessed=72 * d * d, transcendentals=0),
    )(blocks, y, dx, vec, nrm)


def on_device(size, inputs, cotangent, lengths, *params):
    n_mb, seq, d = inputs.shape
    tables = jnp.asarray(rotary_tables(seq))
    out_y, out_dx, a, b, small = section_call(lengths, inputs, cotangent, params, tables)
    stay = size == 16
    blocks, vectors, nrm = gradient_call(a, b, small, stay)
    if stay:
        blocks = pltpu.with_memory_space_constraint(blocks, pltpu.VMEM)
    else:
        groups = [[g * 16 + r for g in range(size // 16)] for r in range(16)]
        blocks, vectors = [lax.psum(v, "dp", axis_index_groups=groups) for v in (blocks, vectors)]
    return widen_call(blocks, out_y, out_dx, vectors, nrm)


def solution(mesh):
    matrix, vector = P("pipe", None, None), P("pipe", None)
    weights = (vector, vector, matrix, vector, matrix, vector) * 2
    tokens = P("dp", None, None)
    return jax.shard_map(
        functools.partial(on_device, mesh.shape["dp"]),
        mesh=mesh,
        in_specs=(tokens, tokens, P("dp")) + weights,
        out_specs=(P("pipe", "dp", None, None),) * 2 + weights + (P("dp"),),
        check_vma=False,
    )
```

```python
import functools

import jax
import jax.numpy as jnp
import numpy as np
from jax import lax
from jax.experimental import pallas as pl
from jax.experimental.pallas import tpu as pltpu
from jax.sharding import PartitionSpec as P

HEADS = 12
HEAD = 64
ROT = 16
EPSILON = 1e-05
NEG_FILL = -1e30
INV_ROOT_TWO = 0.7071067811865476
INV_ROOT_TWO_PI = 0.3989422804014327
MESH = pl.DeviceIdType.MESH
F32 = jnp.float32
BF16 = jnp.bfloat16


def dot_nn(a, b):
    return jnp.dot(a, b, preferred_element_type=F32)


def dot_nt(a, b):
    return lax.dot_general(a, b, (((1,), (1,)), ((), ())), preferred_element_type=F32)


def dot_tn(a, b):
    return lax.dot_general(a, b, (((0,), (0,)), ((), ())), preferred_element_type=F32)


def rotary_tables(seq):
    half = ROT // 2
    freq = 10000.0 ** (-2.0 * np.arange(half) / ROT)
    angle = np.arange(seq)[:, None] * freq[None, :]
    cosine, sine = np.cos(angle), np.sin(angle)
    own = np.ones((seq, HEAD))
    up = np.zeros((seq, HEAD))
    down = np.zeros((seq, HEAD))
    own[:, :half] = cosine
    own[:, half:ROT] = cosine
    up[:, half:ROT] = sine
    down[:, :half] = -sine
    tables = np.stack([np.concatenate([t, t], axis=1) for t in (own, up, down)])
    return tables.astype(np.float32)


def section_kernel(
    n_mb,
    lens,
    inputs,
    cot,
    g1,
    b1,
    wqkv,
    bqkv,
    wd,
    bd,
    g2,
    b2,
    wi,
    bi,
    wo,
    bo,
    tables,
    out_y,
    out_dx,
    a_hbm,
    b_hbm,
    small,
    wqkv_v,
    wd_v,
    wi_v,
    wo_v,
    xb,
    av,
    bv,
    pb,
    yb,
    dxb,
    acc,
    dctx_v,
    bias_v,
    wsem,
    insem,
    cotsem,
    ysem,
    dxsem,
    asem,
    bsem,
    fsend,
    frecv,
    bsend,
    brecv,
):
    section = lax.axis_index("pipe")
    first = section == 0
    last = section == 1
    peer = 1 - section
    seq, d = xb.shape[1], xb.shape[2]
    pairs = d // 128

    wcopies = [
        pltpu.make_async_copy(src.at[0], dst, wsem.at[k])
        for k, (src, dst) in enumerate(((wqkv, wqkv_v), (wd, wd_v), (wi, wi_v), (wo, wo_v)))
    ]

    @pl.when(first)
    def _():
        pltpu.make_async_copy(inputs.at[0], xb.at[0], insem.at[0]).start()

    for c in wcopies:
        c.start()

    @pl.when(first)
    def _():
        rest = pl.ds(1, n_mb - 1)
        pltpu.make_async_copy(inputs.at[rest], xb.at[rest], insem.at[1]).start()

    @pl.when(last)
    def _():
        pltpu.make_async_copy(cot, bv.at[4], cotsem).start()

    barrier = pltpu.get_barrier_semaphore()
    pl.semaphore_signal(barrier, inc=1, device_id={"pipe": peer}, device_id_type=MESH)
    pl.semaphore_wait(barrier, 1)

    def half_copy(k):
        rows = pl.ds(k * (seq // 2), seq // 2)
        return pltpu.make_async_remote_copy(
            src_ref=yb.at[0, rows],
            dst_ref=xb.at[0, rows],
            send_sem=fsend.at[k * n_mb],
            recv_sem=frecv.at[k * n_mb],
            device_id={"pipe": peer},
            device_id_type=MESH,
        )

    def fcopy(i):
        return pltpu.make_async_remote_copy(
            src_ref=yb.at[i],
            dst_ref=xb.at[i],
            send_sem=fsend.at[i],
            recv_sem=frecv.at[i],
            device_id={"pipe": peer},
            device_id_type=MESH,
        )

    def bcopy(i):
        return pltpu.make_async_remote_copy(
            src_ref=dxb.at[i],
            dst_ref=bv.at[4, i],
            send_sem=bsend.at[i],
            recv_sem=brecv.at[i],
            device_id={"pipe": peer},
            device_id_type=MESH,
        )

    def pick(value, a):
        lower = lax.broadcasted_iota(jnp.int32, value.shape, 1) < HEAD
        return jnp.where(lower if a == 0 else jnp.logical_not(lower), value, jnp.zeros_like(value))

    def rotate(w, sign, rows=slice(None)):
        up = pltpu.roll(w, ROT // 2, 1) * tables[1, rows]
        down = pltpu.roll(w, 128 - ROT // 2, 1) * tables[2, rows]
        return w * tables[0, rows] + sign * (up + down)

    def unit_of(i, rows=slice(None)):
        x = xb[i, rows].astype(F32)
        center = x - jnp.mean(x, axis=-1, keepdims=True)
        inverse = lax.rsqrt(jnp.mean(center * center, axis=-1, keepdims=True) + EPSILON)
        return x, center * inverse, inverse

    def pair_columns(h):
        return slice((h // 2) * 128, (h // 2 + 1) * 128)

    def pipelined(stages, count, extra):
        for t in range(count + max(lag for lag, _ in stages)):
            for run in extra.get(t, ()):
                run()
            for lag, stage in stages:
                if 0 <= t - lag < count:
                    stage(t - lag)

    def feed_slots(feed_in, feed_mid, feed_out):
        slots = {}
        for k in range(6):
            runs = []
            for lag, stage in ((2, feed_out), (1, feed_mid), (0, feed_in)):
                if 0 <= k - lag < 4:
                    runs.append(functools.partial(stage, k - lag))
            slots[(5 * k) // 2] = runs
        return slots

    def forward(i, start, count, ready):
        rows, keys = slice(start, start + count), slice(0, start + count)
        x, unit, inverse = unit_of(i, rows)
        a1 = (unit * g1[...] + b1[...]).astype(BF16)
        av[5, i, rows] = a1
        av[0, i, rows] = (unit * g2[...] + b2[...]).astype(BF16)
        acc[rows] = x + bd[...] + bo[...]
        if start == 0:
            key = lax.broadcasted_iota(jnp.int32, (seq, seq), 0)
            query = lax.broadcasted_iota(jnp.int32, (seq, seq), 1)
            bias_v[...] = jnp.where((key <= query) & (key < lens[i]), 0.0, NEG_FILL)
        mixed, scores, probs, parts, hidden = {}, {}, {}, {}, {}

        def project(t):
            mixed[t] = dot_nn(a1, wqkv_v[:, t * d : (t + 1) * d]) + bqkv[:, t * d : (t + 1) * d]

        def settle(t):
            if t == 2:
                bv[7, i, rows] = mixed[2].astype(BF16)
                return
            for hp in range(pairs):
                w = rotate(mixed[t][:, hp * 128 : (hp + 1) * 128], 1.0, rows)
                if t == 0:
                    w = w * HEAD ** (-0.5)
                bv[5 + t, i, rows, hp * 128 : (hp + 1) * 128] = w.astype(BF16)

        def head_scores(h):
            cols = pair_columns(h)
            scores[h] = dot_nt(pick(bv[6, i, keys, cols], h % 2), bv[5, i, rows, cols])

        def head_softmax(h):
            value = scores.pop(h) + bias_v[keys, rows]
            expo = jnp.exp(value - jnp.max(value, axis=0, keepdims=True))
            probs[h] = (expo * (1.0 / jnp.sum(expo, axis=0, keepdims=True))).astype(BF16)
            pb[i, h, keys, rows] = probs[h]
            if start + count < seq:
                pb[i, h, start + count :, rows] = jnp.zeros((seq - start - count, count), BF16)

        def head_context(h):
            cols = pair_columns(h)
            parts[h] = dot_tn(probs.pop(h), pick(bv[7, i, keys, cols], h % 2))
            if h % 2 == 1:
                av[6, i, rows, cols] = (parts.pop(h - 1) + parts.pop(h)).astype(BF16)

        def feed_in(j):
            cols = slice(j * d, (j + 1) * d)
            hidden[j] = dot_nn(av[0, i, rows], wi_v[:, cols]) + bi[:, cols]

        def feed_gate(j):
            value = hidden.pop(j)
            gate = 0.5 * (1.0 + lax.erf(value * INV_ROOT_TWO))
            av[1 + j, i, rows] = (value * gate).astype(BF16)
            bv[j, i, rows] = (gate + value * jnp.exp(-0.5 * value * value) * INV_ROOT_TWO_PI).astype(BF16)

        def feed_out(j):
            acc[rows] += dot_nn(av[1 + j, i, rows], wo_v[j * d : (j + 1) * d, :])

        ready(0)
        pipelined(((0, project), (1, settle)), 3, {})
        heads = ((0, head_scores), (4, head_softmax), (6, head_context))
        ready(1)
        pipelined(heads, HEADS, feed_slots(feed_in, feed_gate, feed_out))
        yb[i, rows] = (acc[rows] + dot_nn(av[6, i, rows], wd_v[...])).astype(BF16)

    def forward_done(i):
        pltpu.make_async_copy(yb.at[i], out_y.at[0, i], ysem.at[i]).start()
        for k in range(7):
            pltpu.make_async_copy(av.at[k, i], a_hbm.at[k, i], asem.at[k, i]).start()

    def forward_whole(i):
        @pl.when(last)
        def _():
            fcopy(i).wait_recv()

        forward(i, 0, seq, lambda k: None)

        @pl.when(first)
        def _():
            fcopy(i).start()

        forward_done(i)

    def forward_halves():
        def ready(k):
            for c in wcopies[:1] if k == 0 else wcopies[1:]:
                c.wait()

        for k in range(2):
            @pl.when(last)
            def _(k=k):
                half_copy(k).wait_recv()

            forward(0, k * (seq // 2), seq // 2, ready if k == 0 else lambda k: None)

            @pl.when(first)
            def _(k=k):
                half_copy(k).start()

        forward_done(0)

    def backward(i):
        @pl.when(first)
        def _():
            bcopy(i).wait_recv()

        @pl.when(last)
        def _():
            row = lax.broadcasted_iota(jnp.int32, (seq, d), 0)
            value = bv[4, i].astype(F32)
            bv[4, i] = jnp.where(row < lens[i], value, 0.0).astype(BF16)

        gy = bv[4, i]
        small[i, 7:8, :] = jnp.sum(gy.astype(F32), axis=0, keepdims=True)
        acc[...] = jnp.zeros_like(acc)

        dctx_v[...] = dot_nt(gy, wd_v[...]).astype(BF16)
        dact, dprob, ds, dmix = {}, {}, {}, {}

        def feed_in(j):
            dact[j] = dot_nt(bv[4, i], wo_v[j * d : (j + 1) * d, :])

        def feed_slope(j):
            dh = (dact.pop(j) * bv[j, i].astype(F32)).astype(BF16)
            bv[j, i] = dh
            small[i, 8 + j : 9 + j, :] = jnp.sum(dh.astype(F32), axis=0, keepdims=True)

        def feed_out(j):
            acc[...] += dot_nt(bv[j, i], wi_v[:, j * d : (j + 1) * d])

        def head_dprob(h):
            cols = pair_columns(h)
            dprob[h] = dot_nt(pick(bv[7, i, :, cols], h % 2), dctx_v[:, cols])

        def head_dscores(h):
            pf = pb[i, h].astype(F32)
            prod = dprob.pop(h) * pf
            ds[h] = (prod - pf * jnp.sum(prod, axis=0, keepdims=True)).astype(BF16)

        def head_products(h):
            cols = pair_columns(h)
            value = ds.pop(h)
            dv = dot_nn(pb[i, h], pick(dctx_v[:, cols], h % 2))
            dk = dot_nn(value, pick(bv[5, i, :, cols], h % 2))
            dq = dot_tn(value, pick(bv[6, i, :, cols], h % 2))
            dmix[h] = (dq, dk, dv)

        def pair_settle(h):
            if h % 2 == 0:
                return
            cols = pair_columns(h)
            dq, dk, dv = [p + q for p, q in zip(dmix.pop(h - 1), dmix.pop(h))]
            for t, w in ((0, rotate(dq * HEAD ** (-0.5), -1.0)), (1, rotate(dk, -1.0)), (2, dv)):
                w = w.astype(BF16)
                bv[5 + t, i, :, cols] = w
                small[i, 4 + t : 5 + t, cols] = jnp.sum(w.astype(F32), axis=0, keepdims=True)

        pipelined(
            ((0, head_dprob), (2, head_dscores), (3, head_products), (4, pair_settle)),
            HEADS,
            feed_slots(feed_in, feed_slope, feed_out),
        )
        dmixed = jnp.concatenate([bv[5, i], bv[6, i], bv[7, i]], axis=1)
        da1 = dot_nt(dmixed, wqkv_v[...])
        da2 = acc[...]
        x, unit, inverse = unit_of(i)
        small[i, 0:1, :] = jnp.sum(da1 * unit, axis=0, keepdims=True)
        small[i, 1:2, :] = jnp.sum(da1, axis=0, keepdims=True)
        small[i, 2:3, :] = jnp.sum(da2 * unit, axis=0, keepdims=True)
        small[i, 3:4, :] = jnp.sum(da2, axis=0, keepdims=True)
        scaled = da1 * g1[...] + da2 * g2[...]
        mean_g = jnp.mean(scaled, axis=-1, keepdims=True)
        mean_gn = jnp.mean(scaled * unit, axis=-1, keepdims=True)
        dx = bv[4, i].astype(F32) + inverse * (scaled - mean_g - unit * mean_gn)
        dxb[i] = dx.astype(BF16)

        @pl.when(last)
        def _():
            bcopy(i).start()

        pltpu.make_async_copy(dxb.at[i], out_dx.at[0, i], dxsem.at[i]).start()
        for k in range(8):
            pltpu.make_async_copy(bv.at[k, i], b_hbm.at[k, i], bsem.at[k, i]).start()

    @pl.when(first)
    def _():
        pltpu.make_async_copy(inputs.at[0], xb.at[0], insem.at[0]).wait()

    forward_halves()

    @pl.when(first)
    def _():
        rest = pl.ds(1, n_mb - 1)
        pltpu.make_async_copy(inputs.at[rest], xb.at[rest], insem.at[1]).wait()

    @pl.when(last)
    def _():
        pltpu.make_async_copy(cot, bv.at[4], cotsem).wait()

    def tick(step, carry):
        after = step + 1
        phase = section * (after % 2) + (1 - section) * (after // n_mb)
        mb = section * (after // 2) + (1 - section) * (after % n_mb)

        @pl.when(phase == 0)
        def _():
            forward_whole(mb)

        @pl.when(phase == 1)
        def _():
            backward(mb)

        return carry

    lax.fori_loop(0, 2 * n_mb - 1, tick, 0)

    def drain(i, carry):
        @pl.when(first & (i > 0))
        def _():
            fcopy(i).wait_send()

        @pl.when(last)
        def _():
            bcopy(i).wait_send()

        pltpu.make_async_copy(yb.at[i], out_y.at[0, i], ysem.at[i]).wait()
        pltpu.make_async_copy(dxb.at[i], out_dx.at[0, i], dxsem.at[i]).wait()
        for k in range(7):
            pltpu.make_async_copy(av.at[k, i], a_hbm.at[k, i], asem.at[k, i]).wait()
        for k in range(8):
            pltpu.make_async_copy(bv.at[k, i], b_hbm.at[k, i], bsem.at[k, i]).wait()
        return carry

    lax.fori_loop(0, n_mb, drain, 0)

    @pl.when(first)
    def _():
        half_copy(0).wait_send()
        half_copy(1).wait_send()


def section_call(lens, inputs, cot, params, tables):
    n_mb, seq, d = inputs.shape
    g1, b1, wqkv, bqkv, wd, bd, g2, b2, wi, bi, wo, bo = params
    ff = wi.shape[2]
    vmem = pl.BlockSpec(memory_space=pltpu.VMEM)
    smem = pl.BlockSpec(memory_space=pltpu.SMEM)
    hbm = pl.BlockSpec(memory_space=pl.ANY)
    dma = pltpu.SemaphoreType.DMA
    flops = n_mb * 2 * seq * (3 * d * d + d * d + 2 * d * ff) * 2
    return pl.pallas_call(
        functools.partial(section_kernel, n_mb),
        out_shape=(
            jax.ShapeDtypeStruct((1, n_mb, seq, d), BF16),
            jax.ShapeDtypeStruct((1, n_mb, seq, d), BF16),
            jax.ShapeDtypeStruct((7, n_mb, seq, d), BF16),
            jax.ShapeDtypeStruct((8, n_mb, seq, d), BF16),
            jax.ShapeDtypeStruct((n_mb, 16, d), F32),
        ),
        in_specs=[smem, hbm, hbm, vmem, vmem, hbm, vmem, hbm, vmem, vmem, vmem, hbm, vmem, hbm, vmem, vmem],
        out_specs=(hbm, hbm, hbm, hbm, vmem),
        scratch_shapes=[
            pltpu.VMEM((d, 3 * d), BF16),
            pltpu.VMEM((d, d), BF16),
            pltpu.VMEM((d, ff), BF16),
            pltpu.VMEM((ff, d), BF16),
            pltpu.VMEM((n_mb, seq, d), BF16),
            pltpu.VMEM((7, n_mb, seq, d), BF16),
            pltpu.VMEM((8, n_mb, seq, d), BF16),
            pltpu.VMEM((n_mb, HEADS, seq, seq), BF16),
            pltpu.VMEM((n_mb, seq, d), BF16),
            pltpu.VMEM((n_mb, seq, d), BF16),
            pltpu.VMEM((seq, d), F32),
            pltpu.VMEM((seq, d), BF16),
            pltpu.VMEM((seq, seq), F32),
            dma((4,)),
            dma((2,)),
            dma,
            dma((n_mb,)),
            dma((n_mb,)),
            dma((7, n_mb)),
            dma((8, n_mb)),
            dma((n_mb + 1,)),
            dma((n_mb + 1,)),
            dma((n_mb,)),
            dma((n_mb,)),
        ],
        compiler_params=pltpu.CompilerParams(
            collective_id=0, has_side_effects=True, vmem_limit_bytes=62 * 2**20
        ),
        cost_estimate=pl.CostEstimate(flops=flops, bytes_accessed=40 * 2**20, transcendentals=0),
    )(lens, inputs, cot, g1, b1, wqkv, bqkv, wd, bd, g2, b2, wi, bi, wo, bo, tables)


PIECES = 4
SPLITS = 2


def a_index(b):
    g = b // 4
    return g * (2 - g) * (b - 3) + (g * (g - 1) // 2) * 5 + b // 11


def b_index(b):
    g = b // 4
    middle, late = g * (2 - g), g * (g - 1) // 2
    return (1 - middle - late) * b + middle * 4 + late * (b - 3) - (b // 11) * 4


def gradient_kernel(
    nb,
    a_hbm,
    b_hbm,
    small,
    out_all,
    out_vec,
    out_nrm,
    abuf,
    bbuf,
    own,
    csend,
    crecv,
    yred,
    leafy,
    leafz,
    midy,
    midz,
    yz,
    vec,
    vrecv,
    nrm,
    nrecv,
    absem,
    s_core,
    r_core,
    s_yred,
    r_yred,
    s_leafy,
    r_leafy,
    s_leafz,
    r_leafz,
    s_midy,
    r_midy,
    s_midz,
    r_midz,
    s_yz,
    r_yz,
    s_toty,
    r_toty,
    s_boty,
    r_boty,
    s_totz,
    r_totz,
    s_lz,
    r_lz,
    s_ag,
    r_ag,
    s_vec,
    r_vec,
    s_nrm,
    r_nrm,
):
    n_mb, seq, d = abuf.shape[1:]
    pipe = lax.axis_index("pipe")
    me = lax.axis_index("dp")
    group, inner = me // 16, me % 16
    z, y, core = inner // 4, (inner // 2) % 2, inner % 2
    mid = (z // 2 + z % 2) == 1
    leaf = jnp.logical_not(mid)

    def at(z_, y_, core_):
        return {"dp": group * 16 + (z_ * 2 + y_) * 2 + core_}

    core_peer = at(z, y, 1 - core)
    y_peer = at(z, 1 - y, core)
    near = at(z + 1 - 2 * (z % 2), y, core)
    across = at(3 - z, y, core)
    pipe_peer = {"pipe": 1 - pipe}
    zi = z // 2
    y_mine, y_other = y, 1 - y
    z_mine, z_other = 2 + zi, 3 - zi
    half = core * PIECES

    def remote(src, dst, send, recv, device):
        return pltpu.make_async_remote_copy(
            src_ref=src, dst_ref=dst, send_sem=send, recv_sem=recv, device_id=device, device_id_type=MESH
        )

    def c_core(b):
        return remote(csend.at[b % 2], crecv.at[b], s_core.at[b % 2], r_core.at[b], core_peer)

    def c_yred(b):
        return remote(own.at[b, y_other], yred.at[b], s_yred.at[b], r_yred.at[b], y_peer)

    def c_leafy(b):
        return remote(own.at[b, y_mine], leafy.at[b], s_leafy.at[b], r_leafy.at[b], near)

    def c_leafz(b):
        return remote(own.at[b, pl.ds(2, 2)], leafz.at[b], s_leafz.at[b], r_leafz.at[b], near)

    def c_midy(b):
        return remote(own.at[b, y_mine], midy.at[b], s_midy.at[b], r_midy.at[b], across)

    def c_midz(b):
        return remote(own.at[b, z_other], midz.at[b], s_midz.at[b], r_midz.at[b], across)

    def c_yz(b):
        return remote(own.at[b, z_mine], yz.at[b], s_yz.at[b], r_yz.at[b], y_peer)

    def piece(b, k):
        return out_all.at[b, half + k]

    def c_toty(b):
        return remote(piece(b, y_mine), piece(b, y_mine), s_toty.at[b], r_toty.at[b], near)

    def c_boty(b):
        return remote(piece(b, y_mine), piece(b, y_mine), s_boty.at[b], r_boty.at[b], y_peer)

    def c_totz(b):
        return remote(piece(b, z_mine), piece(b, z_mine), s_totz.at[b], r_totz.at[b], across)

    def c_lz(b, which):
        k = z_mine if which == 0 else z_other
        return remote(piece(b, k), piece(b, k), s_lz.at[which, b], r_lz.at[which, b], near)

    def c_ag(b, k):
        return remote(piece(b, k), piece(b, k), s_ag.at[k, b], r_ag.at[k, b], core_peer)

    def finish(b, k):
        c_ag(b, k).start()

    vec_to = (core_peer, y_peer, near, across, near)

    def c_vec(h):
        return remote(vec.at[h], vrecv.at[h], s_vec.at[h], r_vec.at[h], vec_to[h])

    def c_nrm():
        return remote(nrm, nrecv, s_nrm, r_nrm, pipe_peer)

    def c_load(w, which):
        slot = w % 2
        if which == 0:
            return pltpu.make_async_copy(a_hbm.at[a_index(w)], abuf.at[slot], absem.at[0, slot])
        return pltpu.make_async_copy(b_hbm.at[b_index(w)], bbuf.at[slot], absem.at[1, slot])

    def add(*values):
        total = values[0].astype(F32)
        for v in values[1:]:
            total = total + v.astype(F32)
        return total

    for which in range(2):
        c_load(0, which).start()

    barrier = pltpu.get_barrier_semaphore()
    for device in (core_peer, y_peer, near, pipe_peer):
        pl.semaphore_signal(barrier, inc=1, device_id=device, device_id_type=MESH)

    @pl.when(mid)
    def _():
        pl.semaphore_signal(barrier, inc=1, device_id=across, device_id_type=MESH)
        pl.semaphore_wait(barrier, 5)

    @pl.when(leaf)
    def _():
        pl.semaphore_wait(barrier, 4)

    row = lax.broadcasted_iota(jnp.int32, (16, d), 0)
    total = None
    for m in range(n_mb):
        value = jnp.where(row < 12, small[m], 0.0)
        squares = value * value * jnp.where(row == 7, 2.0, 1.0)
        folded = squares[:8] + squares[8:]
        nrm[m] = sum(folded[:, k * 128 : (k + 1) * 128] for k in range(d // 128))
        total = value if total is None else total + value
    vec[0] = total
    c_vec(0).start()

    def weight_block(b):
        slot = b % 2
        w, part = b // SPLITS, b % SPLITS
        wslot = w % 2

        @pl.when(part == 0)
        def _():
            for which in range(2):
                c_load(w, which).wait()

        @pl.when((part == 0) & (w + 1 < nb // SPLITS))
        def _():
            for which in range(2):
                c_load(w + 1, which).start()

        @pl.when(b >= 2)
        def _():
            c_core(b - 2).wait_send()

        step = 256
        lhs = pl.ds(pl.multiple_of(part * (d // SPLITS), 128), d // SPLITS)
        for c in range(d // step):
            cols = slice(c * step, (c + 1) * step)
            total = None
            for m in range(n_mb):
                grad = dot_tn(abuf[wslot, m, :, lhs], bbuf[wslot, m, :, cols])
                squares = jnp.sum((grad * grad).reshape(-1, 8, step), axis=0)
                nrm[m] += squares[:, :128] + squares[:, 128:]
                total = grad if total is None else total + grad
            total = total.astype(BF16).reshape(2, PIECES, -1, step)

            @pl.when(core == 0)
            def _():
                own[b, :, :, cols] = total[0]
                csend[slot, :, :, cols] = total[1]

            @pl.when(core == 1)
            def _():
                own[b, :, :, cols] = total[1]
                csend[slot, :, :, cols] = total[0]

        c_core(b).start()

    def lag1(b):
        c_core(b).wait_recv()
        for k in range(PIECES):
            own[b, k] = add(own[b, k], crecv[b, k]).astype(BF16)
        c_yred(b).start()

        @pl.when(leaf)
        def _():
            c_leafz(b).start()

    def lag2(b):
        @pl.when(mid)
        def _():
            c_leafz(b).wait_recv()
            for k in range(2):
                own[b, 2 + k] = add(own[b, 2 + k], leafz[b, k]).astype(BF16)
            c_midz(b).start()

        c_yred(b).wait_recv()
        own[b, y_mine] = add(own[b, y_mine], yred[b]).astype(BF16)

        @pl.when(leaf)
        def _():
            c_leafy(b).start()

    def lag3(b):
        @pl.when(mid)
        def _():
            c_midz(b).wait_recv()
            own[b, z_mine] = add(own[b, z_mine], midz[b]).astype(BF16)
            c_yz(b).start()
            c_leafy(b).wait_recv()
            own[b, y_mine] = add(own[b, y_mine], leafy[b]).astype(BF16)
            c_midy(b).start()

    def lag4(b):
        @pl.when(mid)
        def _():
            c_yz(b).wait_recv()
            out_all[b, half + z_mine] = add(own[b, z_mine], yz[b]).astype(BF16)
            c_totz(b).start()
            c_lz(b, 0).start()
            finish(b, z_mine)
            c_midy(b).wait_recv()
            out_all[b, half + y_mine] = add(own[b, y_mine], midy[b]).astype(BF16)
            c_toty(b).start()
            c_boty(b).start()
            finish(b, y_mine)

    def lag5(b):
        @pl.when(mid)
        def _():
            c_totz(b).wait_recv()
            c_lz(b, 1).start()
            finish(b, z_other)
            c_boty(b).wait_recv()
            finish(b, y_other)

        @pl.when(leaf)
        def _():
            c_toty(b).wait_recv()
            c_boty(b).start()
            finish(b, y_mine)
            c_lz(b, 0).wait_recv()
            finish(b, z_mine)

    def lag6(b):
        @pl.when(leaf)
        def _():
            c_boty(b).wait_recv()
            finish(b, y_other)
            c_lz(b, 1).wait_recv()
            finish(b, z_other)

    def vector_steps(t):
        @pl.when(t == 1)
        def _():
            c_vec(0).wait_recv()
            vec[1] = vec[0] + vrecv[0]
            c_vec(1).start()

        @pl.when(t == 2)
        def _():
            c_vec(1).wait_recv()
            vec[2] = vec[1] + vrecv[1]

            @pl.when(leaf)
            def _():
                c_vec(2).start()

        @pl.when((t == 3) & mid)
        def _():
            c_vec(2).wait_recv()
            vec[3] = vec[2] + vrecv[2]
            c_vec(3).start()

        @pl.when((t == 4) & mid)
        def _():
            c_vec(3).wait_recv()
            vec[4] = vec[3] + vrecv[3]
            c_vec(4).start()
            out_vec[...] = vec[4]

        @pl.when((t == 5) & leaf)
        def _():
            c_vec(4).wait_recv()
            out_vec[...] = vrecv[4]

        @pl.when(t == nb)
        def _():
            c_nrm().start()

    stages = (weight_block, lag1, lag2, lag3, lag4, lag5, lag6)

    def step(t, carry):
        for lag in (1, 0, 2, 3, 4, 5, 6):
            stage = stages[lag]

            @pl.when((t >= lag) & (t - lag < nb))
            def _(lag=lag, stage=stage):
                stage(t - lag)

        vector_steps(t)
        return carry

    lax.fori_loop(0, nb + len(stages) - 1, step, 0)

    c_nrm().wait_recv()
    out_nrm[...] = nrm[...] + nrecv[...]
    c_nrm().wait_send()
    c_vec(0).wait_send()
    c_vec(1).wait_send()
    c_core(nb - 2).wait_send()
    c_core(nb - 1).wait_send()

    @pl.when(leaf)
    def _():
        c_vec(2).wait_send()

    @pl.when(mid)
    def _():
        c_vec(3).wait_send()
        c_vec(4).wait_send()

    def drain(b, carry):
        c_yred(b).wait_send()
        c_boty(b).wait_send()
        for k in range(PIECES):
            c_ag(b, k).wait()

        @pl.when(leaf)
        def _():
            c_leafy(b).wait_send()
            c_leafz(b).wait_send()

        @pl.when(mid)
        def _():
            c_midy(b).wait_send()
            c_midz(b).wait_send()
            c_yz(b).wait_send()
            c_toty(b).wait_send()
            c_totz(b).wait_send()
            c_lz(b, 0).wait_send()
            c_lz(b, 1).wait_send()

        return carry

    lax.fori_loop(0, nb, drain, 0)


def gradient_call(a, b, small, stay):
    n_mb, seq, d = a.shape[1:]
    nb = 12 * SPLITS
    rows = d // (2 * PIECES * SPLITS)
    summed = (nb, 2 * PIECES, rows, d)
    vmem = pl.BlockSpec(memory_space=pltpu.VMEM)
    hbm = pl.BlockSpec(memory_space=pl.ANY)
    dma = pltpu.SemaphoreType.DMA

    def slots(*lead):
        return pltpu.VMEM(lead + (rows, d), BF16)

    return pl.pallas_call(
        functools.partial(gradient_kernel, nb),
        out_shape=(
            pltpu.VMEM(summed, BF16) if stay else jax.ShapeDtypeStruct(summed, BF16),
            jax.ShapeDtypeStruct((16, d), F32),
            jax.ShapeDtypeStruct((n_mb, 8, 128), F32),
        ),
        in_specs=[hbm, hbm, vmem],
        out_specs=(vmem, vmem, vmem),
        scratch_shapes=[
            pltpu.VMEM((2, n_mb, seq, d), BF16),
            pltpu.VMEM((2, n_mb, seq, d), BF16),
            slots(nb, PIECES),
            slots(2, PIECES),
            slots(nb, PIECES),
            slots(nb),
            slots(nb),
            slots(nb, 2),
            slots(nb),
            slots(nb),
            slots(nb),
            pltpu.VMEM((5, 16, d), F32),
            pltpu.VMEM((5, 16, d), F32),
            pltpu.VMEM((n_mb, 8, 128), F32),
            pltpu.VMEM((n_mb, 8, 128), F32),
            dma((2, 2)),
            dma((2,)),
            dma((nb,)),
        ]
        + [dma((nb,)) for _ in range(18)]
        + [dma((2, nb)), dma((2, nb)), dma((PIECES, nb)), dma((PIECES, nb)), dma((5,)), dma((5,)), dma, dma],
        compiler_params=pltpu.CompilerParams(
            collective_id=1, has_side_effects=True, vmem_limit_bytes=(44 if stay else 60) * 2**20
        ),
        cost_estimate=pl.CostEstimate(
            flops=24 * n_mb * seq * d * d, bytes_accessed=64 * 2**20, transcendentals=0
        ),
    )(a, b, small)


def widen_kernel(
    stay,
    blocks,
    y_in,
    dx_in,
    vec,
    nrm,
    out_y,
    out_dx,
    gain1,
    bias1,
    w_qkv,
    b_qkv,
    w_dense,
    b_dense,
    gain2,
    bias2,
    w_in,
    b_in,
    w_out,
    b_out,
    norms,
    narrow,
    wide,
    held,
    isem,
    osem,
    csem,
):
    d = wide.shape[2]
    reads = [
        pltpu.make_async_copy(blocks.at[pl.ds(w * SPLITS, SPLITS)], narrow.at[w % 4], isem.at[w % 4])
        for w in range(12)
    ]
    targets = [w_in.at[0, :, pl.ds(k * d, d)] for k in range(4)]
    targets += [w_out.at[0, pl.ds(k * d, d)] for k in range(4)]
    targets += [w_qkv.at[0, :, pl.ds(k * d, d)] for k in range(3)]
    targets += [w_dense.at[0]]
    writes = [pltpu.make_async_copy(wide.at[w], targets[w], osem.at[w]) for w in range(12)]
    if stay:
        copies = [
            pltpu.make_async_copy(y_in, out_y, csem.at[2]),
            pltpu.make_async_copy(dx_in, out_dx, csem.at[3]),
        ]
        fetch = []
    else:
        copies = [
            pltpu.make_async_copy(held.at[0], out_y, csem.at[2]),
            pltpu.make_async_copy(held.at[1], out_dx, csem.at[3]),
        ]
        fetch = [
            pltpu.make_async_copy(y_in, held.at[0], csem.at[0]),
            pltpu.make_async_copy(dx_in, held.at[1], csem.at[1]),
        ]
    for c in (copies if stay else fetch) + reads[:3]:
        c.start()
    for row, refs in ((0, (gain1,)), (1, (bias1,)), (2, (gain2,)), (3, (bias2,)), (7, (b_dense, b_out))):
        for ref in refs:
            ref[...] = vec[row : row + 1, :]
    for k in range(3):
        b_qkv[:, k * d : (k + 1) * d] = vec[4 + k : 5 + k, :]
    for k in range(4):
        b_in[:, k * d : (k + 1) * d] = vec[8 + k : 9 + k, :]
    for m in range(nrm.shape[0]):
        norms[m] = jnp.sum(nrm[m])
    for w in range(12):
        if w + 3 < 12:
            reads[w + 3].start()
        reads[w].wait()
        wide[w] = narrow[w % 4].astype(F32).reshape(d, d)
        writes[w].start()
    for c in fetch:
        c.wait()
    for c in [] if stay else copies:
        c.start()
    for c in writes + copies:
        c.wait()


def widen_call(blocks, y, dx, vec, nrm, stay):
    d = y.shape[3]
    vmem = pl.BlockSpec(memory_space=pltpu.VMEM)
    hbm = pl.BlockSpec(memory_space=pl.ANY)
    dma = pltpu.SemaphoreType.DMA

    def row(k):
        return jax.ShapeDtypeStruct((1, k * d), F32)

    def matrix(r, c):
        return jax.ShapeDtypeStruct((1, r * d, c * d), F32)

    same = jax.ShapeDtypeStruct(y.shape, BF16)
    return pl.pallas_call(
        functools.partial(widen_kernel, stay),
        out_shape=(same, same, row(1), row(1), matrix(1, 3), row(3), matrix(1, 1), row(1))
        + (row(1), row(1), matrix(1, 4), row(4), matrix(4, 1), row(1))
        + (jax.ShapeDtypeStruct(nrm.shape[:1], F32),),
        in_specs=[hbm, hbm, hbm, vmem, vmem],
        out_specs=(hbm, hbm) + (vmem, vmem, hbm, vmem, hbm, vmem) * 2 + (pl.BlockSpec(memory_space=pltpu.SMEM),),
        scratch_shapes=[
            pltpu.VMEM((4, SPLITS) + blocks.shape[1:], BF16),
            pltpu.VMEM((12, d, d), F32),
            pltpu.VMEM((1, 8, 128) if stay else (2,) + y.shape, BF16),
            dma((4,)),
            dma((12,)),
            dma((4,)),
        ],
        compiler_params=pltpu.CompilerParams(vmem_limit_bytes=42 * 2**20),
        cost_estimate=pl.CostEstimate(flops=12 * d * d, bytes_accessed=72 * d * d, transcendentals=0),
    )(blocks, y, dx, vec, nrm)


def on_device(size, inputs, cotangent, lengths, *params):
    n_mb, seq, d = inputs.shape
    tables = jnp.asarray(rotary_tables(seq))
    out_y, out_dx, a, b, small = section_call(lengths, inputs, cotangent, params, tables)
    stay = size == 16
    blocks, vectors, nrm = gradient_call(a, b, small, stay)
    if stay:
        blocks, out_y, out_dx = [
            pltpu.with_memory_space_constraint(v, pltpu.VMEM) for v in (blocks, out_y, out_dx)
        ]
    else:
        groups = [[g * 16 + r for g in range(size // 16)] for r in range(16)]
        blocks, vectors = [lax.psum(v, "dp", axis_index_groups=groups) for v in (blocks, vectors)]
    return widen_call(blocks, out_y, out_dx, vectors, nrm, stay)


def solution(mesh):
    matrix, vector = P("pipe", None, None), P("pipe", None)
    weights = (vector, vector, matrix, vector, matrix, vector) * 2
    tokens = P("dp", None, None)
    return jax.shard_map(
        functools.partial(on_device, mesh.shape["dp"]),
        mesh=mesh,
        in_specs=(tokens, tokens, P("dp")) + weights,
        out_specs=(P("pipe", "dp", None, None),) * 2 + weights + (P("dp"),),
        check_vma=False,
    )
```

```python
import functools

import jax
import jax.numpy as jnp
import numpy as np
from jax import lax
from jax.experimental import pallas as pl
from jax.experimental.pallas import tpu as pltpu
from jax.sharding import PartitionSpec as P

HEADS = 12
HEAD = 64
ROT = 16
EPSILON = 1e-05
NEG_FILL = -1e30
INV_ROOT_TWO = 0.7071067811865476
INV_ROOT_TWO_PI = 0.3989422804014327
MESH = pl.DeviceIdType.MESH
F32 = jnp.float32
BF16 = jnp.bfloat16


def dot_nn(a, b):
    return jnp.dot(a, b, preferred_element_type=F32)


def dot_nt(a, b):
    return lax.dot_general(a, b, (((1,), (1,)), ((), ())), preferred_element_type=F32)


def dot_tn(a, b):
    return lax.dot_general(a, b, (((0,), (0,)), ((), ())), preferred_element_type=F32)


def rotary_tables(seq):
    half = ROT // 2
    freq = 10000.0 ** (-2.0 * np.arange(half) / ROT)
    angle = np.arange(seq)[:, None] * freq[None, :]
    cosine, sine = np.cos(angle), np.sin(angle)
    own = np.ones((seq, HEAD))
    up = np.zeros((seq, HEAD))
    down = np.zeros((seq, HEAD))
    own[:, :half] = cosine
    own[:, half:ROT] = cosine
    up[:, half:ROT] = sine
    down[:, :half] = -sine
    tables = np.stack([np.concatenate([t, t], axis=1) for t in (own, up, down)])
    return tables.astype(np.float32)


def section_kernel(
    n_mb,
    lens,
    inputs,
    cot,
    g1,
    b1,
    wqkv,
    bqkv,
    wd,
    bd,
    g2,
    b2,
    wi,
    bi,
    wo,
    bo,
    tables,
    out_y,
    out_dx,
    a_hbm,
    b_hbm,
    small,
    wqkv_v,
    wd_v,
    wi_v,
    wo_v,
    xb,
    av,
    bv,
    pb,
    yb,
    dxb,
    acc,
    dctx_v,
    bias_v,
    wsem,
    insem,
    cotsem,
    ysem,
    dxsem,
    asem,
    bsem,
    fsend,
    frecv,
    bsend,
    brecv,
):
    section = lax.axis_index("pipe")
    first = section == 0
    last = section == 1
    peer = 1 - section
    seq, d = xb.shape[1], xb.shape[2]
    pairs = d // 128

    wcopies = [
        pltpu.make_async_copy(src.at[0], dst, wsem.at[k])
        for k, (src, dst) in enumerate(((wd, wd_v), (wi, wi_v), (wo, wo_v)))
    ]
    wcopies = [
        pltpu.make_async_copy(
            wqkv.at[0, :, pl.ds(t * d, d)], wqkv_v.at[:, pl.ds(t * d, d)], wsem.at[3 + t]
        )
        for t in range(3)
    ] + wcopies

    @pl.when(first)
    def _():
        pltpu.make_async_copy(inputs.at[0], xb.at[0], insem.at[0]).start()

    for c in wcopies:
        c.start()

    @pl.when(first)
    def _():
        rest = pl.ds(1, n_mb - 1)
        pltpu.make_async_copy(inputs.at[rest], xb.at[rest], insem.at[1]).start()

    @pl.when(last)
    def _():
        pltpu.make_async_copy(cot, bv.at[4], cotsem).start()

    barrier = pltpu.get_barrier_semaphore()
    pl.semaphore_signal(barrier, inc=1, device_id={"pipe": peer}, device_id_type=MESH)
    pl.semaphore_wait(barrier, 1)

    def half_copy(k):
        rows = pl.ds(k * (seq // 2), seq // 2)
        return pltpu.make_async_remote_copy(
            src_ref=yb.at[0, rows],
            dst_ref=xb.at[0, rows],
            send_sem=fsend.at[k * n_mb],
            recv_sem=frecv.at[k * n_mb],
            device_id={"pipe": peer},
            device_id_type=MESH,
        )

    def fcopy(i):
        return pltpu.make_async_remote_copy(
            src_ref=yb.at[i],
            dst_ref=xb.at[i],
            send_sem=fsend.at[i],
            recv_sem=frecv.at[i],
            device_id={"pipe": peer},
            device_id_type=MESH,
        )

    def bcopy(i):
        return pltpu.make_async_remote_copy(
            src_ref=dxb.at[i],
            dst_ref=bv.at[4, i],
            send_sem=bsend.at[i],
            recv_sem=brecv.at[i],
            device_id={"pipe": peer},
            device_id_type=MESH,
        )

    def pick(value, a):
        lower = lax.broadcasted_iota(jnp.int32, value.shape, 1) < HEAD
        return jnp.where(lower if a == 0 else jnp.logical_not(lower), value, jnp.zeros_like(value))

    def rotate(w, sign, rows=slice(None)):
        up = pltpu.roll(w, ROT // 2, 1) * tables[1, rows]
        down = pltpu.roll(w, 128 - ROT // 2, 1) * tables[2, rows]
        return w * tables[0, rows] + sign * (up + down)

    def unit_of(i, rows=slice(None)):
        x = xb[i, rows].astype(F32)
        center = x - jnp.mean(x, axis=-1, keepdims=True)
        inverse = lax.rsqrt(jnp.mean(center * center, axis=-1, keepdims=True) + EPSILON)
        return x, center * inverse, inverse

    def pair_columns(h):
        return slice((h // 2) * 128, (h // 2 + 1) * 128)

    def pipelined(stages, count, extra):
        for t in range(count + max(lag for lag, _ in stages)):
            for run in extra.get(t, ()):
                run()
            for lag, stage in stages:
                if 0 <= t - lag < count:
                    stage(t - lag)

    def feed_slots(feed_in, feed_mid, feed_out, place):
        slots = {}
        for k in range(6):
            runs = []
            for lag, stage in ((2, feed_out), (1, feed_mid), (0, feed_in)):
                if 0 <= k - lag < 4:
                    runs.append(functools.partial(stage, k - lag))
            slots.setdefault(place(k), []).extend(runs)
        return slots

    def forward(i, start, count, ready):
        rows, keys = slice(start, start + count), slice(0, start + count)
        x, unit, inverse = unit_of(i, rows)
        a1 = (unit * g1[...] + b1[...]).astype(BF16)
        av[5, i, rows] = a1
        av[0, i, rows] = (unit * g2[...] + b2[...]).astype(BF16)
        acc[rows] = x + bd[...] + bo[...]
        if start == 0:
            key = lax.broadcasted_iota(jnp.int32, (seq, seq), 0)
            query = lax.broadcasted_iota(jnp.int32, (seq, seq), 1)
            bias_v[...] = jnp.where((key <= query) & (key < lens[i]), 0.0, NEG_FILL)
        mixed, scores, probs, parts, hidden = {}, {}, {}, {}, {}

        def project(t):
            ready(t)
            mixed[t] = dot_nn(a1, wqkv_v[:, t * d : (t + 1) * d]) + bqkv[:, t * d : (t + 1) * d]

        def settle(t):
            if t == 2:
                bv[7, i, rows] = mixed[2].astype(BF16)
                return
            for hp in range(pairs):
                w = rotate(mixed[t][:, hp * 128 : (hp + 1) * 128], 1.0, rows)
                if t == 0:
                    w = w * HEAD ** (-0.5)
                bv[5 + t, i, rows, hp * 128 : (hp + 1) * 128] = w.astype(BF16)

        def head_scores(h):
            cols = pair_columns(h)
            scores[h] = dot_nt(pick(bv[6, i, keys, cols], h % 2), bv[5, i, rows, cols])

        def head_softmax(h):
            value = scores.pop(h) + bias_v[keys, rows]
            expo = jnp.exp(value - jnp.max(value, axis=0, keepdims=True))
            probs[h] = (expo * (1.0 / jnp.sum(expo, axis=0, keepdims=True))).astype(BF16)
            pb[i, h, keys, rows] = probs[h]
            if start + count < seq:
                pb[i, h, start + count :, rows] = jnp.zeros((seq - start - count, count), BF16)

        def head_context(h):
            cols = pair_columns(h)
            parts[h] = dot_tn(probs.pop(h), pick(bv[7, i, keys, cols], h % 2))
            if h % 2 == 1:
                av[6, i, rows, cols] = (parts.pop(h - 1) + parts.pop(h)).astype(BF16)

        def feed_in(j):
            cols = slice(j * d, (j + 1) * d)
            hidden[j] = dot_nn(av[0, i, rows], wi_v[:, cols]) + bi[:, cols]

        def feed_gate(j):
            value = hidden.pop(j)
            gate = 0.5 * (1.0 + lax.erf(value * INV_ROOT_TWO))
            av[1 + j, i, rows] = (value * gate).astype(BF16)
            bv[j, i, rows] = (gate + value * jnp.exp(-0.5 * value * value) * INV_ROOT_TWO_PI).astype(BF16)

        def feed_out(j):
            acc[rows] += dot_nn(av[1 + j, i, rows], wo_v[j * d : (j + 1) * d, :])

        pipelined(((0, project), (1, settle)), 3, {})
        heads = ((0, head_scores), (4, head_softmax), (6, head_context))
        ready(3)
        pipelined(heads, HEADS, feed_slots(feed_in, feed_gate, feed_out, lambda k: 2 + 3 * k))
        yb[i, rows] = (acc[rows] + dot_nn(av[6, i, rows], wd_v[...])).astype(BF16)

    def forward_done(i):
        pltpu.make_async_copy(yb.at[i], out_y.at[0, i], ysem.at[i]).start()
        for k in range(7):
            pltpu.make_async_copy(av.at[k, i], a_hbm.at[k, i], asem.at[k, i]).start()

    def forward_whole(i):
        @pl.when(last)
        def _():
            fcopy(i).wait_recv()

        forward(i, 0, seq, lambda k: None)

        @pl.when(first)
        def _():
            fcopy(i).start()

        forward_done(i)

    def forward_halves():
        def ready(k):
            for c in wcopies[k : k + 1] if k < 3 else wcopies[3:]:
                c.wait()

        for k in range(2):
            @pl.when(last)
            def _(k=k):
                half_copy(k).wait_recv()

            forward(0, k * (seq // 2), seq // 2, ready if k == 0 else lambda k: None)

            @pl.when(first)
            def _(k=k):
                half_copy(k).start()

        forward_done(0)

    def backward(i):
        @pl.when(first)
        def _():
            bcopy(i).wait_recv()

        @pl.when(last)
        def _():
            row = lax.broadcasted_iota(jnp.int32, (seq, d), 0)
            value = bv[4, i].astype(F32)
            bv[4, i] = jnp.where(row < lens[i], value, 0.0).astype(BF16)

        gy = bv[4, i]
        small[i, 7:8, :] = jnp.sum(gy.astype(F32), axis=0, keepdims=True)
        dctx_v[...] = dot_nt(gy, wd_v[...]).astype(BF16)
        dact, dprob, ds, dmix = {}, {}, {}, {}

        def feed_in(j):
            dact[j] = dot_nt(bv[4, i], wo_v[j * d : (j + 1) * d, :])

        def feed_slope(j):
            dh = (dact.pop(j) * bv[j, i].astype(F32)).astype(BF16)
            bv[j, i] = dh
            small[i, 8 + j : 9 + j, :] = jnp.sum(dh.astype(F32), axis=0, keepdims=True)

        def feed_out(j):
            part = dot_nt(bv[j, i], wi_v[:, j * d : (j + 1) * d])
            acc[...] = part if j == 0 else acc[...] + part

        def head_dprob(h):
            cols = pair_columns(h)
            dprob[h] = dot_nt(pick(bv[7, i, :, cols], h % 2), dctx_v[:, cols])

        def head_dscores(h):
            pf = pb[i, h].astype(F32)
            prod = dprob.pop(h) * pf
            ds[h] = (prod - pf * jnp.sum(prod, axis=0, keepdims=True)).astype(BF16)

        def head_products(h):
            cols = pair_columns(h)
            value = ds.pop(h)
            dv = dot_nn(pb[i, h], pick(dctx_v[:, cols], h % 2))
            dk = dot_nn(value, pick(bv[5, i, :, cols], h % 2))
            dq = dot_tn(value, pick(bv[6, i, :, cols], h % 2))
            dmix[h] = (dq, dk, dv)

        def pair_settle(h):
            if h % 2 == 0:
                return
            cols = pair_columns(h)
            dq, dk, dv = [p + q for p, q in zip(dmix.pop(h - 1), dmix.pop(h))]
            for t, w in ((0, rotate(dq * HEAD ** (-0.5), -1.0)), (1, rotate(dk, -1.0)), (2, dv)):
                w = w.astype(BF16)
                bv[5 + t, i, :, cols] = w
                small[i, 4 + t : 5 + t, cols] = jnp.sum(w.astype(F32), axis=0, keepdims=True)

        pipelined(
            ((0, head_dprob), (2, head_dscores), (3, head_products), (4, pair_settle)),
            HEADS,
            feed_slots(feed_in, feed_slope, feed_out, lambda k: 2 + 2 * k),
        )
        for k in range(8):
            pltpu.make_async_copy(bv.at[k, i], b_hbm.at[k, i], bsem.at[k, i]).start()
        x, unit, inverse = unit_of(i)
        da2 = acc[...]
        small[i, 2:3, :] = jnp.sum(da2 * unit, axis=0, keepdims=True)
        small[i, 3:4, :] = jnp.sum(da2, axis=0, keepdims=True)
        dmixed = jnp.concatenate([bv[5, i], bv[6, i], bv[7, i]], axis=1)
        da1 = dot_nt(dmixed, wqkv_v[...])
        small[i, 0:1, :] = jnp.sum(da1 * unit, axis=0, keepdims=True)
        small[i, 1:2, :] = jnp.sum(da1, axis=0, keepdims=True)
        scaled = da1 * g1[...] + da2 * g2[...]
        mean_g = jnp.mean(scaled, axis=-1, keepdims=True)
        mean_gn = jnp.mean(scaled * unit, axis=-1, keepdims=True)
        dx = bv[4, i].astype(F32) + inverse * (scaled - mean_g - unit * mean_gn)
        dxb[i] = dx.astype(BF16)

        @pl.when(last)
        def _():
            bcopy(i).start()

        pltpu.make_async_copy(dxb.at[i], out_dx.at[0, i], dxsem.at[i]).start()

    @pl.when(first)
    def _():
        pltpu.make_async_copy(inputs.at[0], xb.at[0], insem.at[0]).wait()

    forward_halves()

    @pl.when(first)
    def _():
        rest = pl.ds(1, n_mb - 1)
        pltpu.make_async_copy(inputs.at[rest], xb.at[rest], insem.at[1]).wait()

    @pl.when(last)
    def _():
        pltpu.make_async_copy(cot, bv.at[4], cotsem).wait()

    def tick(step, carry):
        after = step + 1
        phase = section * (after % 2) + (1 - section) * (after // n_mb)
        mb = section * (after // 2) + (1 - section) * (after % n_mb)

        @pl.when(phase == 0)
        def _():
            forward_whole(mb)

        @pl.when(phase == 1)
        def _():
            backward(mb)

        return carry

    lax.fori_loop(0, 2 * n_mb - 1, tick, 0)

    def drain(i, carry):
        @pl.when(first & (i > 0))
        def _():
            fcopy(i).wait_send()

        @pl.when(last)
        def _():
            bcopy(i).wait_send()

        pltpu.make_async_copy(yb.at[i], out_y.at[0, i], ysem.at[i]).wait()
        pltpu.make_async_copy(dxb.at[i], out_dx.at[0, i], dxsem.at[i]).wait()
        for k in range(7):
            pltpu.make_async_copy(av.at[k, i], a_hbm.at[k, i], asem.at[k, i]).wait()
        for k in range(8):
            pltpu.make_async_copy(bv.at[k, i], b_hbm.at[k, i], bsem.at[k, i]).wait()
        return carry

    lax.fori_loop(0, n_mb, drain, 0)

    @pl.when(first)
    def _():
        half_copy(0).wait_send()
        half_copy(1).wait_send()


def section_call(lens, inputs, cot, params, tables):
    n_mb, seq, d = inputs.shape
    g1, b1, wqkv, bqkv, wd, bd, g2, b2, wi, bi, wo, bo = params
    ff = wi.shape[2]
    vmem = pl.BlockSpec(memory_space=pltpu.VMEM)
    smem = pl.BlockSpec(memory_space=pltpu.SMEM)
    hbm = pl.BlockSpec(memory_space=pl.ANY)
    dma = pltpu.SemaphoreType.DMA
    flops = n_mb * 2 * seq * (3 * d * d + d * d + 2 * d * ff) * 2
    return pl.pallas_call(
        functools.partial(section_kernel, n_mb),
        out_shape=(
            jax.ShapeDtypeStruct((1, n_mb, seq, d), BF16),
            jax.ShapeDtypeStruct((1, n_mb, seq, d), BF16),
            jax.ShapeDtypeStruct((7, n_mb, seq, d), BF16),
            jax.ShapeDtypeStruct((8, n_mb, seq, d), BF16),
            jax.ShapeDtypeStruct((n_mb, 16, d), F32),
        ),
        in_specs=[smem, hbm, hbm, vmem, vmem, hbm, vmem, hbm, vmem, vmem, vmem, hbm, vmem, hbm, vmem, vmem],
        out_specs=(hbm, hbm, hbm, hbm, vmem),
        scratch_shapes=[
            pltpu.VMEM((d, 3 * d), BF16),
            pltpu.VMEM((d, d), BF16),
            pltpu.VMEM((d, ff), BF16),
            pltpu.VMEM((ff, d), BF16),
            pltpu.VMEM((n_mb, seq, d), BF16),
            pltpu.VMEM((7, n_mb, seq, d), BF16),
            pltpu.VMEM((8, n_mb, seq, d), BF16),
            pltpu.VMEM((n_mb, HEADS, seq, seq), BF16),
            pltpu.VMEM((n_mb, seq, d), BF16),
            pltpu.VMEM((n_mb, seq, d), BF16),
            pltpu.VMEM((seq, d), F32),
            pltpu.VMEM((seq, d), BF16),
            pltpu.VMEM((seq, seq), F32),
            dma((6,)),
            dma((2,)),
            dma,
            dma((n_mb,)),
            dma((n_mb,)),
            dma((7, n_mb)),
            dma((8, n_mb)),
            dma((n_mb + 1,)),
            dma((n_mb + 1,)),
            dma((n_mb,)),
            dma((n_mb,)),
        ],
        compiler_params=pltpu.CompilerParams(
            collective_id=0, has_side_effects=True, vmem_limit_bytes=62 * 2**20
        ),
        cost_estimate=pl.CostEstimate(flops=flops, bytes_accessed=40 * 2**20, transcendentals=0),
    )(lens, inputs, cot, g1, b1, wqkv, bqkv, wd, bd, g2, b2, wi, bi, wo, bo, tables)


PIECES = 4
SPLITS = 2


def a_index(b):
    g = b // 4
    return g * (2 - g) * (b - 3) + (g * (g - 1) // 2) * 5 + b // 11


def b_index(b):
    g = b // 4
    middle, late = g * (2 - g), g * (g - 1) // 2
    return (1 - middle - late) * b + middle * 4 + late * (b - 3) - (b // 11) * 4


def gradient_kernel(
    nb,
    a_hbm,
    b_hbm,
    small,
    out_all,
    out_vec,
    out_nrm,
    abuf,
    bbuf,
    own,
    csend,
    crecv,
    yred,
    leafy,
    leafz,
    midy,
    midz,
    yz,
    vec,
    vrecv,
    nrm,
    nrecv,
    absem,
    s_core,
    r_core,
    s_yred,
    r_yred,
    s_leafy,
    r_leafy,
    s_leafz,
    r_leafz,
    s_midy,
    r_midy,
    s_midz,
    r_midz,
    s_yz,
    r_yz,
    s_toty,
    r_toty,
    s_boty,
    r_boty,
    s_totz,
    r_totz,
    s_lz,
    r_lz,
    s_ag,
    r_ag,
    s_vec,
    r_vec,
    s_nrm,
    r_nrm,
):
    n_mb, seq, d = abuf.shape[1:]
    pipe = lax.axis_index("pipe")
    me = lax.axis_index("dp")
    group, inner = me // 16, me % 16
    z, y, core = inner // 4, (inner // 2) % 2, inner % 2
    mid = (z // 2 + z % 2) == 1
    leaf = jnp.logical_not(mid)

    def at(z_, y_, core_):
        return {"dp": group * 16 + (z_ * 2 + y_) * 2 + core_}

    core_peer = at(z, y, 1 - core)
    y_peer = at(z, 1 - y, core)
    near = at(z + 1 - 2 * (z % 2), y, core)
    across = at(3 - z, y, core)
    pipe_peer = {"pipe": 1 - pipe}
    zi = z // 2
    y_mine, y_other = y, 1 - y
    z_mine, z_other = 2 + zi, 3 - zi
    half = core * PIECES

    def remote(src, dst, send, recv, device):
        return pltpu.make_async_remote_copy(
            src_ref=src, dst_ref=dst, send_sem=send, recv_sem=recv, device_id=device, device_id_type=MESH
        )

    def c_core(b):
        return remote(csend.at[b % 2], crecv.at[b], s_core.at[b % 2], r_core.at[b], core_peer)

    def c_yred(b):
        return remote(own.at[b, y_other], yred.at[b], s_yred.at[b], r_yred.at[b], y_peer)

    def c_leafy(b):
        return remote(own.at[b, y_mine], leafy.at[b], s_leafy.at[b], r_leafy.at[b], near)

    def c_leafz(b):
        return remote(own.at[b, pl.ds(2, 2)], leafz.at[b], s_leafz.at[b], r_leafz.at[b], near)

    def c_midy(b):
        return remote(own.at[b, y_mine], midy.at[b], s_midy.at[b], r_midy.at[b], across)

    def c_midz(b):
        return remote(own.at[b, z_other], midz.at[b], s_midz.at[b], r_midz.at[b], across)

    def c_yz(b):
        return remote(own.at[b, z_mine], yz.at[b], s_yz.at[b], r_yz.at[b], y_peer)

    def piece(b, k):
        return out_all.at[b, half + k]

    def c_toty(b):
        return remote(piece(b, y_mine), piece(b, y_mine), s_toty.at[b], r_toty.at[b], near)

    def c_boty(b):
        return remote(piece(b, y_mine), piece(b, y_mine), s_boty.at[b], r_boty.at[b], y_peer)

    def c_totz(b):
        return remote(piece(b, z_mine), piece(b, z_mine), s_totz.at[b], r_totz.at[b], across)

    def c_lz(b, which):
        k = z_mine if which == 0 else z_other
        return remote(piece(b, k), piece(b, k), s_lz.at[which, b], r_lz.at[which, b], near)

    def c_ag(b, k):
        return remote(piece(b, k), piece(b, k), s_ag.at[k, b], r_ag.at[k, b], core_peer)

    def finish(b, k):
        c_ag(b, k).start()

    vec_to = (core_peer, y_peer, near, across, near)

    def c_vec(h):
        return remote(vec.at[h], vrecv.at[h], s_vec.at[h], r_vec.at[h], vec_to[h])

    def c_nrm():
        return remote(nrm, nrecv, s_nrm, r_nrm, pipe_peer)

    def c_load(w, which):
        slot = w % 2
        if which == 0:
            return pltpu.make_async_copy(a_hbm.at[a_index(w)], abuf.at[slot], absem.at[0, slot])
        return pltpu.make_async_copy(b_hbm.at[b_index(w)], bbuf.at[slot], absem.at[1, slot])

    def add(*values):
        total = values[0].astype(F32)
        for v in values[1:]:
            total = total + v.astype(F32)
        return total

    for which in range(2):
        c_load(0, which).start()

    barrier = pltpu.get_barrier_semaphore()
    for device in (core_peer, y_peer, near, pipe_peer):
        pl.semaphore_signal(barrier, inc=1, device_id=device, device_id_type=MESH)

    @pl.when(mid)
    def _():
        pl.semaphore_signal(barrier, inc=1, device_id=across, device_id_type=MESH)
        pl.semaphore_wait(barrier, 5)

    @pl.when(leaf)
    def _():
        pl.semaphore_wait(barrier, 4)

    row = lax.broadcasted_iota(jnp.int32, (16, d), 0)
    total = None
    for m in range(n_mb):
        value = jnp.where(row < 12, small[m], 0.0)
        squares = value * value * jnp.where(row == 7, 2.0, 1.0)
        folded = squares[:8] + squares[8:]
        nrm[m] = sum(folded[:, k * 128 : (k + 1) * 128] for k in range(d // 128))
        total = value if total is None else total + value
    vec[0] = total
    c_vec(0).start()

    def weight_block(b):
        slot = b % 2
        w, part = b // SPLITS, b % SPLITS
        wslot = w % 2

        @pl.when(part == 0)
        def _():
            for which in range(2):
                c_load(w, which).wait()

        @pl.when((part == 0) & (w + 1 < nb // SPLITS))
        def _():
            for which in range(2):
                c_load(w + 1, which).start()

        @pl.when(b >= 2)
        def _():
            c_core(b - 2).wait_send()

        step = 256
        lhs = pl.ds(pl.multiple_of(part * (d // SPLITS), 128), d // SPLITS)
        for c in range(d // step):
            cols = slice(c * step, (c + 1) * step)
            total = None
            for m in range(n_mb):
                grad = dot_tn(abuf[wslot, m, :, lhs], bbuf[wslot, m, :, cols])
                squares = jnp.sum((grad * grad).reshape(-1, 8, step), axis=0)
                nrm[m] += squares[:, :128] + squares[:, 128:]
                total = grad if total is None else total + grad
            total = total.astype(BF16).reshape(2, PIECES, -1, step)

            @pl.when(core == 0)
            def _():
                own[b, :, :, cols] = total[0]
                csend[slot, :, :, cols] = total[1]

            @pl.when(core == 1)
            def _():
                own[b, :, :, cols] = total[1]
                csend[slot, :, :, cols] = total[0]

        c_core(b).start()

    def lag1(b):
        c_core(b).wait_recv()
        for k in range(PIECES):
            own[b, k] = add(own[b, k], crecv[b, k]).astype(BF16)
        c_yred(b).start()

        @pl.when(leaf)
        def _():
            c_leafz(b).start()

    def lag2(b):
        @pl.when(mid)
        def _():
            c_leafz(b).wait_recv()
            for k in range(2):
                own[b, 2 + k] = add(own[b, 2 + k], leafz[b, k]).astype(BF16)
            c_midz(b).start()

        c_yred(b).wait_recv()
        own[b, y_mine] = add(own[b, y_mine], yred[b]).astype(BF16)

        @pl.when(leaf)
        def _():
            c_leafy(b).start()

    def lag3(b):
        @pl.when(mid)
        def _():
            c_midz(b).wait_recv()
            own[b, z_mine] = add(own[b, z_mine], midz[b]).astype(BF16)
            c_yz(b).start()
            c_leafy(b).wait_recv()
            own[b, y_mine] = add(own[b, y_mine], leafy[b]).astype(BF16)
            c_midy(b).start()

    def lag4(b):
        @pl.when(mid)
        def _():
            c_yz(b).wait_recv()
            out_all[b, half + z_mine] = add(own[b, z_mine], yz[b]).astype(BF16)
            c_totz(b).start()
            c_lz(b, 0).start()
            finish(b, z_mine)
            c_midy(b).wait_recv()
            out_all[b, half + y_mine] = add(own[b, y_mine], midy[b]).astype(BF16)
            c_toty(b).start()
            c_boty(b).start()
            finish(b, y_mine)

    def lag5(b):
        @pl.when(mid)
        def _():
            c_totz(b).wait_recv()
            c_lz(b, 1).start()
            finish(b, z_other)
            c_boty(b).wait_recv()
            finish(b, y_other)

        @pl.when(leaf)
        def _():
            c_toty(b).wait_recv()
            c_boty(b).start()
            finish(b, y_mine)
            c_lz(b, 0).wait_recv()
            finish(b, z_mine)

    def lag6(b):
        @pl.when(leaf)
        def _():
            c_boty(b).wait_recv()
            finish(b, y_other)
            c_lz(b, 1).wait_recv()
            finish(b, z_other)

    def vector_steps(t):
        @pl.when(t == 1)
        def _():
            c_vec(0).wait_recv()
            vec[1] = vec[0] + vrecv[0]
            c_vec(1).start()

        @pl.when(t == 2)
        def _():
            c_vec(1).wait_recv()
            vec[2] = vec[1] + vrecv[1]

            @pl.when(leaf)
            def _():
                c_vec(2).start()

        @pl.when((t == 3) & mid)
        def _():
            c_vec(2).wait_recv()
            vec[3] = vec[2] + vrecv[2]
            c_vec(3).start()

        @pl.when((t == 4) & mid)
        def _():
            c_vec(3).wait_recv()
            vec[4] = vec[3] + vrecv[3]
            c_vec(4).start()
            out_vec[...] = vec[4]

        @pl.when((t == 5) & leaf)
        def _():
            c_vec(4).wait_recv()
            out_vec[...] = vrecv[4]

        @pl.when(t == nb)
        def _():
            c_nrm().start()

    stages = (weight_block, lag1, lag2, lag3, lag4, lag5, lag6)

    def step(t, carry):
        for lag in (1, 0, 2, 3, 4, 5, 6):
            stage = stages[lag]

            @pl.when((t >= lag) & (t - lag < nb))
            def _(lag=lag, stage=stage):
                stage(t - lag)

        vector_steps(t)
        return carry

    lax.fori_loop(0, nb + len(stages) - 1, step, 0)

    c_nrm().wait_recv()
    out_nrm[...] = nrm[...] + nrecv[...]
    c_nrm().wait_send()
    c_vec(0).wait_send()
    c_vec(1).wait_send()
    c_core(nb - 2).wait_send()
    c_core(nb - 1).wait_send()

    @pl.when(leaf)
    def _():
        c_vec(2).wait_send()

    @pl.when(mid)
    def _():
        c_vec(3).wait_send()
        c_vec(4).wait_send()

    def drain(b, carry):
        c_yred(b).wait_send()
        c_boty(b).wait_send()
        for k in range(PIECES):
            c_ag(b, k).wait()

        @pl.when(leaf)
        def _():
            c_leafy(b).wait_send()
            c_leafz(b).wait_send()

        @pl.when(mid)
        def _():
            c_midy(b).wait_send()
            c_midz(b).wait_send()
            c_yz(b).wait_send()
            c_toty(b).wait_send()
            c_totz(b).wait_send()
            c_lz(b, 0).wait_send()
            c_lz(b, 1).wait_send()

        return carry

    lax.fori_loop(0, nb, drain, 0)


def gradient_call(a, b, small, stay):
    n_mb, seq, d = a.shape[1:]
    nb = 12 * SPLITS
    rows = d // (2 * PIECES * SPLITS)
    summed = (nb, 2 * PIECES, rows, d)
    vmem = pl.BlockSpec(memory_space=pltpu.VMEM)
    hbm = pl.BlockSpec(memory_space=pl.ANY)
    dma = pltpu.SemaphoreType.DMA

    def slots(*lead):
        return pltpu.VMEM(lead + (rows, d), BF16)

    return pl.pallas_call(
        functools.partial(gradient_kernel, nb),
        out_shape=(
            pltpu.VMEM(summed, BF16) if stay else jax.ShapeDtypeStruct(summed, BF16),
            jax.ShapeDtypeStruct((16, d), F32),
            jax.ShapeDtypeStruct((n_mb, 8, 128), F32),
        ),
        in_specs=[hbm, hbm, vmem],
        out_specs=(vmem, vmem, vmem),
        scratch_shapes=[
            pltpu.VMEM((2, n_mb, seq, d), BF16),
            pltpu.VMEM((2, n_mb, seq, d), BF16),
            slots(nb, PIECES),
            slots(2, PIECES),
            slots(nb, PIECES),
            slots(nb),
            slots(nb),
            slots(nb, 2),
            slots(nb),
            slots(nb),
            slots(nb),
            pltpu.VMEM((5, 16, d), F32),
            pltpu.VMEM((5, 16, d), F32),
            pltpu.VMEM((n_mb, 8, 128), F32),
            pltpu.VMEM((n_mb, 8, 128), F32),
            dma((2, 2)),
            dma((2,)),
            dma((nb,)),
        ]
        + [dma((nb,)) for _ in range(18)]
        + [dma((2, nb)), dma((2, nb)), dma((PIECES, nb)), dma((PIECES, nb)), dma((5,)), dma((5,)), dma, dma],
        compiler_params=pltpu.CompilerParams(
            collective_id=1, has_side_effects=True, vmem_limit_bytes=(44 if stay else 60) * 2**20
        ),
        cost_estimate=pl.CostEstimate(
            flops=24 * n_mb * seq * d * d, bytes_accessed=64 * 2**20, transcendentals=0
        ),
    )(a, b, small)


def widen_kernel(
    stay,
    blocks,
    y_in,
    dx_in,
    vec,
    nrm,
    out_y,
    out_dx,
    gain1,
    bias1,
    w_qkv,
    b_qkv,
    w_dense,
    b_dense,
    gain2,
    bias2,
    w_in,
    b_in,
    w_out,
    b_out,
    norms,
    narrow,
    wide,
    held,
    isem,
    osem,
    csem,
):
    d = wide.shape[2]
    reads = [
        pltpu.make_async_copy(blocks.at[pl.ds(w * SPLITS, SPLITS)], narrow.at[w % 4], isem.at[w % 4])
        for w in range(12)
    ]
    targets = [w_in.at[0, :, pl.ds(k * d, d)] for k in range(4)]
    targets += [w_out.at[0, pl.ds(k * d, d)] for k in range(4)]
    targets += [w_qkv.at[0, :, pl.ds(k * d, d)] for k in range(3)]
    targets += [w_dense.at[0]]
    writes = [pltpu.make_async_copy(wide.at[w], targets[w], osem.at[w]) for w in range(12)]
    if stay:
        copies = [
            pltpu.make_async_copy(y_in, out_y, csem.at[2]),
            pltpu.make_async_copy(dx_in, out_dx, csem.at[3]),
        ]
        fetch = []
    else:
        copies = [
            pltpu.make_async_copy(held.at[0], out_y, csem.at[2]),
            pltpu.make_async_copy(held.at[1], out_dx, csem.at[3]),
        ]
        fetch = [
            pltpu.make_async_copy(y_in, held.at[0], csem.at[0]),
            pltpu.make_async_copy(dx_in, held.at[1], csem.at[1]),
        ]
    for c in (copies if stay else fetch) + reads[:3]:
        c.start()
    for row, refs in ((0, (gain1,)), (1, (bias1,)), (2, (gain2,)), (3, (bias2,)), (7, (b_dense, b_out))):
        for ref in refs:
            ref[...] = vec[row : row + 1, :]
    for k in range(3):
        b_qkv[:, k * d : (k + 1) * d] = vec[4 + k : 5 + k, :]
    for k in range(4):
        b_in[:, k * d : (k + 1) * d] = vec[8 + k : 9 + k, :]
    for m in range(nrm.shape[0]):
        norms[m] = jnp.sum(nrm[m])
    for w in range(12):
        if w + 3 < 12:
            reads[w + 3].start()
        reads[w].wait()
        wide[w] = narrow[w % 4].astype(F32).reshape(d, d)
        writes[w].start()
    for c in fetch:
        c.wait()
    for c in [] if stay else copies:
        c.start()
    for c in writes + copies:
        c.wait()


def widen_call(blocks, y, dx, vec, nrm, stay):
    d = y.shape[3]
    vmem = pl.BlockSpec(memory_space=pltpu.VMEM)
    hbm = pl.BlockSpec(memory_space=pl.ANY)
    dma = pltpu.SemaphoreType.DMA

    def row(k):
        return jax.ShapeDtypeStruct((1, k * d), F32)

    def matrix(r, c):
        return jax.ShapeDtypeStruct((1, r * d, c * d), F32)

    same = jax.ShapeDtypeStruct(y.shape, BF16)
    return pl.pallas_call(
        functools.partial(widen_kernel, stay),
        out_shape=(same, same, row(1), row(1), matrix(1, 3), row(3), matrix(1, 1), row(1))
        + (row(1), row(1), matrix(1, 4), row(4), matrix(4, 1), row(1))
        + (jax.ShapeDtypeStruct(nrm.shape[:1], F32),),
        in_specs=[hbm, hbm, hbm, vmem, vmem],
        out_specs=(hbm, hbm) + (vmem, vmem, hbm, vmem, hbm, vmem) * 2 + (pl.BlockSpec(memory_space=pltpu.SMEM),),
        scratch_shapes=[
            pltpu.VMEM((4, SPLITS) + blocks.shape[1:], BF16),
            pltpu.VMEM((12, d, d), F32),
            pltpu.VMEM((1, 8, 128) if stay else (2,) + y.shape, BF16),
            dma((4,)),
            dma((12,)),
            dma((4,)),
        ],
        compiler_params=pltpu.CompilerParams(vmem_limit_bytes=42 * 2**20),
        cost_estimate=pl.CostEstimate(flops=12 * d * d, bytes_accessed=72 * d * d, transcendentals=0),
    )(blocks, y, dx, vec, nrm)


def on_device(size, inputs, cotangent, lengths, *params):
    n_mb, seq, d = inputs.shape
    tables = jnp.asarray(rotary_tables(seq))
    out_y, out_dx, a, b, small = section_call(lengths, inputs, cotangent, params, tables)
    stay = size == 16
    blocks, vectors, nrm = gradient_call(a, b, small, stay)
    if stay:
        blocks, out_y, out_dx = [
            pltpu.with_memory_space_constraint(v, pltpu.VMEM) for v in (blocks, out_y, out_dx)
        ]
    else:
        groups = [[g * 16 + r for g in range(size // 16)] for r in range(16)]
        blocks, vectors = [lax.psum(v, "dp", axis_index_groups=groups) for v in (blocks, vectors)]
    return widen_call(blocks, out_y, out_dx, vectors, nrm, stay)


def solution(mesh):
    matrix, vector = P("pipe", None, None), P("pipe", None)
    weights = (vector, vector, matrix, vector, matrix, vector) * 2
    tokens = P("dp", None, None)
    return jax.shard_map(
        functools.partial(on_device, mesh.shape["dp"]),
        mesh=mesh,
        in_specs=(tokens, tokens, P("dp")) + weights,
        out_specs=(P("pipe", "dp", None, None),) * 2 + weights + (P("dp"),),
        check_vma=False,
    )
```

```python
import functools

import jax
import jax.numpy as jnp
import numpy as np
from jax import lax
from jax.experimental import pallas as pl
from jax.experimental.pallas import tpu as pltpu
from jax.sharding import PartitionSpec as P

HEADS = 12
HEAD = 64
ROT = 16
EPSILON = 1e-05
NEG_FILL = -1e30
INV_ROOT_TWO = 0.7071067811865476
INV_ROOT_TWO_PI = 0.3989422804014327
MESH = pl.DeviceIdType.MESH
F32 = jnp.float32
BF16 = jnp.bfloat16


def dot_nn(a, b):
    return jnp.dot(a, b, preferred_element_type=F32)


def dot_nt(a, b):
    return lax.dot_general(a, b, (((1,), (1,)), ((), ())), preferred_element_type=F32)


def dot_tn(a, b):
    return lax.dot_general(a, b, (((0,), (0,)), ((), ())), preferred_element_type=F32)


def rotary_tables(seq):
    half = ROT // 2
    freq = 10000.0 ** (-2.0 * np.arange(half) / ROT)
    angle = np.arange(seq)[:, None] * freq[None, :]
    cosine, sine = np.cos(angle), np.sin(angle)
    own = np.ones((seq, HEAD))
    up = np.zeros((seq, HEAD))
    down = np.zeros((seq, HEAD))
    own[:, :half] = cosine
    own[:, half:ROT] = cosine
    up[:, half:ROT] = sine
    down[:, :half] = -sine
    tables = np.stack([np.concatenate([t, t], axis=1) for t in (own, up, down)])
    return tables.astype(np.float32)


def section_kernel(
    n_mb,
    lens,
    inputs,
    cot,
    g1,
    b1,
    wqkv,
    bqkv,
    wd,
    bd,
    g2,
    b2,
    wi,
    bi,
    wo,
    bo,
    tables,
    out_y,
    out_dx,
    a_hbm,
    b_hbm,
    small,
    wqkv_v,
    wd_v,
    wi_v,
    wo_v,
    xb,
    av,
    bv,
    pb,
    yb,
    dxb,
    acc,
    dctx_v,
    bias_v,
    wsem,
    insem,
    cotsem,
    ysem,
    dxsem,
    asem,
    bsem,
    fsend,
    frecv,
    bsend,
    brecv,
):
    section = lax.axis_index("pipe")
    first = section == 0
    last = section == 1
    peer = 1 - section
    seq, d = xb.shape[1], xb.shape[2]
    pairs = d // 128

    wcopies = [
        pltpu.make_async_copy(src.at[0], dst, wsem.at[k])
        for k, (src, dst) in enumerate(((wd, wd_v), (wi, wi_v), (wo, wo_v)))
    ]
    wcopies = [
        pltpu.make_async_copy(
            wqkv.at[0, :, pl.ds(t * d, d)], wqkv_v.at[:, pl.ds(t * d, d)], wsem.at[3 + t]
        )
        for t in range(3)
    ] + wcopies

    @pl.when(first)
    def _():
        pltpu.make_async_copy(inputs.at[0], xb.at[0], insem.at[0]).start()

    for c in wcopies:
        c.start()

    @pl.when(first)
    def _():
        rest = pl.ds(1, n_mb - 1)
        pltpu.make_async_copy(inputs.at[rest], xb.at[rest], insem.at[1]).start()

    @pl.when(last)
    def _():
        pltpu.make_async_copy(cot, bv.at[4], cotsem).start()

    barrier = pltpu.get_barrier_semaphore()
    pl.semaphore_signal(barrier, inc=1, device_id={"pipe": peer}, device_id_type=MESH)
    pl.semaphore_wait(barrier, 1)

    def half_copy(k):
        rows = pl.ds(k * (seq // 2), seq // 2)
        return pltpu.make_async_remote_copy(
            src_ref=yb.at[0, rows],
            dst_ref=xb.at[0, rows],
            send_sem=fsend.at[k * n_mb],
            recv_sem=frecv.at[k * n_mb],
            device_id={"pipe": peer},
            device_id_type=MESH,
        )

    def fcopy(i):
        return pltpu.make_async_remote_copy(
            src_ref=yb.at[i],
            dst_ref=xb.at[i],
            send_sem=fsend.at[i],
            recv_sem=frecv.at[i],
            device_id={"pipe": peer},
            device_id_type=MESH,
        )

    def bcopy(i):
        return pltpu.make_async_remote_copy(
            src_ref=dxb.at[i],
            dst_ref=bv.at[4, i],
            send_sem=bsend.at[i],
            recv_sem=brecv.at[i],
            device_id={"pipe": peer},
            device_id_type=MESH,
        )

    def pick(value, a):
        lower = lax.broadcasted_iota(jnp.int32, value.shape, 1) < HEAD
        return jnp.where(lower if a == 0 else jnp.logical_not(lower), value, jnp.zeros_like(value))

    def rotate(w, sign, rows=slice(None)):
        up = pltpu.roll(w, ROT // 2, 1) * tables[1, rows]
        down = pltpu.roll(w, 128 - ROT // 2, 1) * tables[2, rows]
        return w * tables[0, rows] + sign * (up + down)

    def unit_of(i, rows=slice(None)):
        x = xb[i, rows].astype(F32)
        center = x - jnp.mean(x, axis=-1, keepdims=True)
        inverse = lax.rsqrt(jnp.mean(center * center, axis=-1, keepdims=True) + EPSILON)
        return x, center * inverse, inverse

    def pair_columns(h):
        return slice((h // 2) * 128, (h // 2 + 1) * 128)

    def pipelined(stages, count, extra):
        for t in range(count + max(lag for lag, _ in stages)):
            for run in extra.get(t, ()):
                run()
            for lag, stage in stages:
                if 0 <= t - lag < count:
                    stage(t - lag)

    def feed_slots(feed_in, feed_mid, feed_out, place):
        slots = {}
        for k in range(6):
            runs = []
            for lag, stage in ((2, feed_out), (1, feed_mid), (0, feed_in)):
                if 0 <= k - lag < 4:
                    runs.append(functools.partial(stage, k - lag))
            slots.setdefault(place(k), []).extend(runs)
        return slots

    def forward(i, start, count, ready):
        rows, keys = slice(start, start + count), slice(0, start + count)
        x, unit, inverse = unit_of(i, rows)
        a1 = (unit * g1[...] + b1[...]).astype(BF16)
        av[5, i, rows] = a1
        av[0, i, rows] = (unit * g2[...] + b2[...]).astype(BF16)
        acc[rows] = x + bd[...] + bo[...]
        if start == 0:
            key = lax.broadcasted_iota(jnp.int32, (seq, seq), 0)
            query = lax.broadcasted_iota(jnp.int32, (seq, seq), 1)
            bias_v[...] = jnp.where((key <= query) & (key < lens[i]), 0.0, NEG_FILL)
        mixed, scores, probs, parts, hidden = {}, {}, {}, {}, {}

        def project(t):
            ready(t)
            mixed[t] = dot_nn(a1, wqkv_v[:, t * d : (t + 1) * d]) + bqkv[:, t * d : (t + 1) * d]

        def settle(t):
            if t == 2:
                bv[7, i, rows] = mixed[2].astype(BF16)
                return
            for hp in range(pairs):
                w = rotate(mixed[t][:, hp * 128 : (hp + 1) * 128], 1.0, rows)
                if t == 0:
                    w = w * HEAD ** (-0.5)
                bv[5 + t, i, rows, hp * 128 : (hp + 1) * 128] = w.astype(BF16)

        def head_scores(h):
            cols = pair_columns(h)
            scores[h] = dot_nt(pick(bv[6, i, keys, cols], h % 2), bv[5, i, rows, cols])

        def head_softmax(h):
            value = scores.pop(h) + bias_v[keys, rows]
            expo = jnp.exp(value - jnp.max(value, axis=0, keepdims=True))
            probs[h] = (expo * (1.0 / jnp.sum(expo, axis=0, keepdims=True))).astype(BF16)
            pb[i, h, keys, rows] = probs[h]
            if start + count < seq:
                pb[i, h, start + count :, rows] = jnp.zeros((seq - start - count, count), BF16)

        def head_context(h):
            cols = pair_columns(h)
            parts[h] = dot_tn(probs.pop(h), pick(bv[7, i, keys, cols], h % 2))
            if h % 2 == 1:
                av[6, i, rows, cols] = (parts.pop(h - 1) + parts.pop(h)).astype(BF16)

        def feed_in(j):
            cols = slice(j * d, (j + 1) * d)
            hidden[j] = dot_nn(av[0, i, rows], wi_v[:, cols]) + bi[:, cols]

        def feed_gate(j):
            value = hidden.pop(j)
            gate = 0.5 * (1.0 + lax.erf(value * INV_ROOT_TWO))
            av[1 + j, i, rows] = (value * gate).astype(BF16)
            bv[j, i, rows] = (gate + value * jnp.exp(-0.5 * value * value) * INV_ROOT_TWO_PI).astype(BF16)

        def feed_out(j):
            acc[rows] += dot_nn(av[1 + j, i, rows], wo_v[j * d : (j + 1) * d, :])

        pipelined(((0, project), (1, settle)), 3, {})
        heads = ((0, head_scores), (4, head_softmax), (6, head_context))
        ready(3)
        pipelined(heads, HEADS, feed_slots(feed_in, feed_gate, feed_out, lambda k: 2 + 3 * k))
        yb[i, rows] = (acc[rows] + dot_nn(av[6, i, rows], wd_v[...])).astype(BF16)

    def forward_done(i):
        pltpu.make_async_copy(yb.at[i], out_y.at[0, i], ysem.at[i]).start()
        for k in range(7):
            pltpu.make_async_copy(av.at[k, i], a_hbm.at[k, i], asem.at[k, i]).start()

    def forward_whole(i):
        @pl.when(last)
        def _():
            fcopy(i).wait_recv()

        forward(i, 0, seq, lambda k: None)

        @pl.when(first)
        def _():
            fcopy(i).start()

        forward_done(i)

    def forward_halves():
        def ready(k):
            for c in wcopies[k : k + 1] if k < 3 else wcopies[3:]:
                c.wait()

        for k in range(2):
            @pl.when(last)
            def _(k=k):
                half_copy(k).wait_recv()

            forward(0, k * (seq // 2), seq // 2, ready if k == 0 else lambda k: None)

            @pl.when(first)
            def _(k=k):
                half_copy(k).start()

        forward_done(0)

    def backward(i):
        @pl.when(first)
        def _():
            bcopy(i).wait_recv()

        @pl.when(last)
        def _():
            row = lax.broadcasted_iota(jnp.int32, (seq, d), 0)
            value = bv[4, i].astype(F32)
            bv[4, i] = jnp.where(row < lens[i], value, 0.0).astype(BF16)

        gy = bv[4, i]
        small[i, 7:8, :] = jnp.sum(gy.astype(F32), axis=0, keepdims=True)
        dctx_v[...] = dot_nt(gy, wd_v[...]).astype(BF16)
        dact, dprob, ds, dmix = {}, {}, {}, {}

        def feed_in(j):
            dact[j] = dot_nt(bv[4, i], wo_v[j * d : (j + 1) * d, :])

        def feed_slope(j):
            dh = (dact.pop(j) * bv[j, i].astype(F32)).astype(BF16)
            bv[j, i] = dh
            small[i, 8 + j : 9 + j, :] = jnp.sum(dh.astype(F32), axis=0, keepdims=True)

        def feed_out(j):
            part = dot_nt(bv[j, i], wi_v[:, j * d : (j + 1) * d])
            acc[...] = part if j == 0 else acc[...] + part

        def head_dprob(h):
            cols = pair_columns(h)
            dprob[h] = dot_nt(pick(bv[7, i, :, cols], h % 2), dctx_v[:, cols])

        def head_dscores(h):
            pf = pb[i, h].astype(F32)
            prod = dprob.pop(h) * pf
            ds[h] = (prod - pf * jnp.sum(prod, axis=0, keepdims=True)).astype(BF16)

        def head_products(h):
            cols = pair_columns(h)
            value = ds.pop(h)
            dv = dot_nn(pb[i, h], pick(dctx_v[:, cols], h % 2))
            dk = dot_nn(value, pick(bv[5, i, :, cols], h % 2))
            dq = dot_tn(value, pick(bv[6, i, :, cols], h % 2))
            dmix[h] = (dq, dk, dv)

        def pair_settle(h):
            if h % 2 == 0:
                return
            cols = pair_columns(h)
            dq, dk, dv = [p + q for p, q in zip(dmix.pop(h - 1), dmix.pop(h))]
            for t, w in ((0, rotate(dq * HEAD ** (-0.5), -1.0)), (1, rotate(dk, -1.0)), (2, dv)):
                w = w.astype(BF16)
                bv[5 + t, i, :, cols] = w
                small[i, 4 + t : 5 + t, cols] = jnp.sum(w.astype(F32), axis=0, keepdims=True)

        pipelined(
            ((0, head_dprob), (2, head_dscores), (3, head_products), (4, pair_settle)),
            HEADS,
            feed_slots(feed_in, feed_slope, feed_out, lambda k: 4 + 2 * k),
        )
        for k in range(8):
            pltpu.make_async_copy(bv.at[k, i], b_hbm.at[k, i], bsem.at[k, i]).start()
        x, unit, inverse = unit_of(i)
        da2 = acc[...]
        small[i, 2:3, :] = jnp.sum(da2 * unit, axis=0, keepdims=True)
        small[i, 3:4, :] = jnp.sum(da2, axis=0, keepdims=True)
        dmixed = jnp.concatenate([bv[5, i], bv[6, i], bv[7, i]], axis=1)
        da1 = dot_nt(dmixed, wqkv_v[...])
        small[i, 0:1, :] = jnp.sum(da1 * unit, axis=0, keepdims=True)
        small[i, 1:2, :] = jnp.sum(da1, axis=0, keepdims=True)
        scaled = da1 * g1[...] + da2 * g2[...]
        mean_g = jnp.mean(scaled, axis=-1, keepdims=True)
        mean_gn = jnp.mean(scaled * unit, axis=-1, keepdims=True)
        dx = bv[4, i].astype(F32) + inverse * (scaled - mean_g - unit * mean_gn)
        dxb[i] = dx.astype(BF16)

        @pl.when(last)
        def _():
            bcopy(i).start()

        pltpu.make_async_copy(dxb.at[i], out_dx.at[0, i], dxsem.at[i]).start()

    @pl.when(first)
    def _():
        pltpu.make_async_copy(inputs.at[0], xb.at[0], insem.at[0]).wait()

    forward_halves()

    @pl.when(first)
    def _():
        rest = pl.ds(1, n_mb - 1)
        pltpu.make_async_copy(inputs.at[rest], xb.at[rest], insem.at[1]).wait()

    @pl.when(last)
    def _():
        pltpu.make_async_copy(cot, bv.at[4], cotsem).wait()

    def tick(step, carry):
        after = step + 1
        phase = section * (after % 2) + (1 - section) * (after // n_mb)
        mb = section * (after // 2) + (1 - section) * (after % n_mb)

        @pl.when(phase == 0)
        def _():
            forward_whole(mb)

        @pl.when(phase == 1)
        def _():
            backward(mb)

        return carry

    lax.fori_loop(0, 2 * n_mb - 1, tick, 0)

    def drain(i, carry):
        @pl.when(first & (i > 0))
        def _():
            fcopy(i).wait_send()

        @pl.when(last)
        def _():
            bcopy(i).wait_send()

        pltpu.make_async_copy(yb.at[i], out_y.at[0, i], ysem.at[i]).wait()
        pltpu.make_async_copy(dxb.at[i], out_dx.at[0, i], dxsem.at[i]).wait()
        for k in range(7):
            pltpu.make_async_copy(av.at[k, i], a_hbm.at[k, i], asem.at[k, i]).wait()
        for k in range(8):
            pltpu.make_async_copy(bv.at[k, i], b_hbm.at[k, i], bsem.at[k, i]).wait()
        return carry

    lax.fori_loop(0, n_mb, drain, 0)

    @pl.when(first)
    def _():
        half_copy(0).wait_send()
        half_copy(1).wait_send()


def section_call(lens, inputs, cot, params, tables):
    n_mb, seq, d = inputs.shape
    g1, b1, wqkv, bqkv, wd, bd, g2, b2, wi, bi, wo, bo = params
    ff = wi.shape[2]
    vmem = pl.BlockSpec(memory_space=pltpu.VMEM)
    smem = pl.BlockSpec(memory_space=pltpu.SMEM)
    hbm = pl.BlockSpec(memory_space=pl.ANY)
    dma = pltpu.SemaphoreType.DMA
    flops = n_mb * 2 * seq * (3 * d * d + d * d + 2 * d * ff) * 2
    return pl.pallas_call(
        functools.partial(section_kernel, n_mb),
        out_shape=(
            jax.ShapeDtypeStruct((1, n_mb, seq, d), BF16),
            jax.ShapeDtypeStruct((1, n_mb, seq, d), BF16),
            jax.ShapeDtypeStruct((7, n_mb, seq, d), BF16),
            jax.ShapeDtypeStruct((8, n_mb, seq, d), BF16),
            jax.ShapeDtypeStruct((n_mb, 16, d), F32),
        ),
        in_specs=[smem, hbm, hbm, vmem, vmem, hbm, vmem, hbm, vmem, vmem, vmem, hbm, vmem, hbm, vmem, vmem],
        out_specs=(hbm, hbm, hbm, hbm, vmem),
        scratch_shapes=[
            pltpu.VMEM((d, 3 * d), BF16),
            pltpu.VMEM((d, d), BF16),
            pltpu.VMEM((d, ff), BF16),
            pltpu.VMEM((ff, d), BF16),
            pltpu.VMEM((n_mb, seq, d), BF16),
            pltpu.VMEM((7, n_mb, seq, d), BF16),
            pltpu.VMEM((8, n_mb, seq, d), BF16),
            pltpu.VMEM((n_mb, HEADS, seq, seq), BF16),
            pltpu.VMEM((n_mb, seq, d), BF16),
            pltpu.VMEM((n_mb, seq, d), BF16),
            pltpu.VMEM((seq, d), F32),
            pltpu.VMEM((seq, d), BF16),
            pltpu.VMEM((seq, seq), F32),
            dma((6,)),
            dma((2,)),
            dma,
            dma((n_mb,)),
            dma((n_mb,)),
            dma((7, n_mb)),
            dma((8, n_mb)),
            dma((n_mb + 1,)),
            dma((n_mb + 1,)),
            dma((n_mb,)),
            dma((n_mb,)),
        ],
        compiler_params=pltpu.CompilerParams(
            collective_id=0, has_side_effects=True, vmem_limit_bytes=62 * 2**20
        ),
        cost_estimate=pl.CostEstimate(flops=flops, bytes_accessed=40 * 2**20, transcendentals=0),
    )(lens, inputs, cot, g1, b1, wqkv, bqkv, wd, bd, g2, b2, wi, bi, wo, bo, tables)


PIECES = 4
SPLITS = 2


def a_index(b):
    g = b // 4
    return g * (2 - g) * (b - 3) + (g * (g - 1) // 2) * 5 + b // 11


def b_index(b):
    g = b // 4
    middle, late = g * (2 - g), g * (g - 1) // 2
    return (1 - middle - late) * b + middle * 4 + late * (b - 3) - (b // 11) * 4


def gradient_kernel(
    nb,
    a_hbm,
    b_hbm,
    small,
    out_all,
    out_vec,
    out_nrm,
    abuf,
    bbuf,
    own,
    csend,
    crecv,
    yred,
    leafy,
    leafz,
    midy,
    midz,
    yz,
    vec,
    vrecv,
    nrm,
    nrecv,
    absem,
    s_core,
    r_core,
    s_yred,
    r_yred,
    s_leafy,
    r_leafy,
    s_leafz,
    r_leafz,
    s_midy,
    r_midy,
    s_midz,
    r_midz,
    s_yz,
    r_yz,
    s_toty,
    r_toty,
    s_boty,
    r_boty,
    s_totz,
    r_totz,
    s_lz,
    r_lz,
    s_ag,
    r_ag,
    s_vec,
    r_vec,
    s_nrm,
    r_nrm,
):
    n_mb, seq, d = abuf.shape[1:]
    pipe = lax.axis_index("pipe")
    me = lax.axis_index("dp")
    group, inner = me // 16, me % 16
    z, y, core = inner // 4, (inner // 2) % 2, inner % 2
    mid = (z // 2 + z % 2) == 1
    leaf = jnp.logical_not(mid)

    def at(z_, y_, core_):
        return {"dp": group * 16 + (z_ * 2 + y_) * 2 + core_}

    core_peer = at(z, y, 1 - core)
    y_peer = at(z, 1 - y, core)
    near = at(z + 1 - 2 * (z % 2), y, core)
    across = at(3 - z, y, core)
    pipe_peer = {"pipe": 1 - pipe}
    zi = z // 2
    y_mine, y_other = y, 1 - y
    z_mine, z_other = 2 + zi, 3 - zi
    half = core * PIECES

    def remote(src, dst, send, recv, device):
        return pltpu.make_async_remote_copy(
            src_ref=src, dst_ref=dst, send_sem=send, recv_sem=recv, device_id=device, device_id_type=MESH
        )

    def c_core(b):
        return remote(csend.at[b % 2], crecv.at[b], s_core.at[b % 2], r_core.at[b], core_peer)

    def c_yred(b):
        return remote(own.at[b, y_other], yred.at[b], s_yred.at[b], r_yred.at[b], y_peer)

    def c_leafy(b):
        return remote(own.at[b, y_mine], leafy.at[b], s_leafy.at[b], r_leafy.at[b], near)

    def c_leafz(b):
        return remote(own.at[b, pl.ds(2, 2)], leafz.at[b], s_leafz.at[b], r_leafz.at[b], near)

    def c_midy(b):
        return remote(own.at[b, y_mine], midy.at[b], s_midy.at[b], r_midy.at[b], across)

    def c_midz(b):
        return remote(own.at[b, z_other], midz.at[b], s_midz.at[b], r_midz.at[b], across)

    def c_yz(b):
        return remote(own.at[b, z_mine], yz.at[b], s_yz.at[b], r_yz.at[b], y_peer)

    def piece(b, k):
        return out_all.at[b, half + k]

    def c_toty(b):
        return remote(piece(b, y_mine), piece(b, y_mine), s_toty.at[b], r_toty.at[b], near)

    def c_boty(b):
        return remote(piece(b, y_mine), piece(b, y_mine), s_boty.at[b], r_boty.at[b], y_peer)

    def c_totz(b):
        return remote(piece(b, z_mine), piece(b, z_mine), s_totz.at[b], r_totz.at[b], across)

    def c_lz(b, which):
        k = z_mine if which == 0 else z_other
        return remote(piece(b, k), piece(b, k), s_lz.at[which, b], r_lz.at[which, b], near)

    def c_ag(b, k):
        return remote(piece(b, k), piece(b, k), s_ag.at[k, b], r_ag.at[k, b], core_peer)

    def finish(b, k):
        c_ag(b, k).start()

    vec_to = (core_peer, y_peer, near, across, near)

    def c_vec(h):
        return remote(vec.at[h], vrecv.at[h], s_vec.at[h], r_vec.at[h], vec_to[h])

    def c_nrm():
        return remote(nrm, nrecv, s_nrm, r_nrm, pipe_peer)

    def c_load(w, which):
        slot = w % 2
        if which == 0:
            return pltpu.make_async_copy(a_hbm.at[a_index(w)], abuf.at[slot], absem.at[0, slot])
        return pltpu.make_async_copy(b_hbm.at[b_index(w)], bbuf.at[slot], absem.at[1, slot])

    def add(*values):
        total = values[0].astype(F32)
        for v in values[1:]:
            total = total + v.astype(F32)
        return total

    for which in range(2):
        c_load(0, which).start()

    barrier = pltpu.get_barrier_semaphore()
    for device in (core_peer, y_peer, near, pipe_peer):
        pl.semaphore_signal(barrier, inc=1, device_id=device, device_id_type=MESH)

    @pl.when(mid)
    def _():
        pl.semaphore_signal(barrier, inc=1, device_id=across, device_id_type=MESH)
        pl.semaphore_wait(barrier, 5)

    @pl.when(leaf)
    def _():
        pl.semaphore_wait(barrier, 4)

    row = lax.broadcasted_iota(jnp.int32, (16, d), 0)
    total = None
    for m in range(n_mb):
        value = jnp.where(row < 12, small[m], 0.0)
        squares = value * value * jnp.where(row == 7, 2.0, 1.0)
        folded = squares[:8] + squares[8:]
        nrm[m] = sum(folded[:, k * 128 : (k + 1) * 128] for k in range(d // 128))
        total = value if total is None else total + value
    vec[0] = total
    c_vec(0).start()

    def weight_block(b):
        slot = b % 2
        w, part = b // SPLITS, b % SPLITS
        wslot = w % 2

        @pl.when(part == 0)
        def _():
            for which in range(2):
                c_load(w, which).wait()

        @pl.when((part == 0) & (w + 1 < nb // SPLITS))
        def _():
            for which in range(2):
                c_load(w + 1, which).start()

        @pl.when(b >= 2)
        def _():
            c_core(b - 2).wait_send()

        step = 256
        lhs = pl.ds(pl.multiple_of(part * (d // SPLITS), 128), d // SPLITS)
        for c in range(d // step):
            cols = slice(c * step, (c + 1) * step)
            total = None
            for m in range(n_mb):
                grad = dot_tn(abuf[wslot, m, :, lhs], bbuf[wslot, m, :, cols])
                squares = jnp.sum((grad * grad).reshape(-1, 8, step), axis=0)
                nrm[m] += squares[:, :128] + squares[:, 128:]
                total = grad if total is None else total + grad
            total = total.astype(BF16).reshape(2, PIECES, -1, step)

            @pl.when(core == 0)
            def _():
                own[b, :, :, cols] = total[0]
                csend[slot, :, :, cols] = total[1]

            @pl.when(core == 1)
            def _():
                own[b, :, :, cols] = total[1]
                csend[slot, :, :, cols] = total[0]

        c_core(b).start()

    def lag1(b):
        c_core(b).wait_recv()
        for k in range(PIECES):
            own[b, k] = add(own[b, k], crecv[b, k]).astype(BF16)
        c_yred(b).start()

        @pl.when(leaf)
        def _():
            c_leafz(b).start()

    def lag2(b):
        @pl.when(mid)
        def _():
            c_leafz(b).wait_recv()
            for k in range(2):
                own[b, 2 + k] = add(own[b, 2 + k], leafz[b, k]).astype(BF16)
            c_midz(b).start()

        c_yred(b).wait_recv()
        own[b, y_mine] = add(own[b, y_mine], yred[b]).astype(BF16)

        @pl.when(leaf)
        def _():
            c_leafy(b).start()

    def lag3(b):
        @pl.when(mid)
        def _():
            c_midz(b).wait_recv()
            own[b, z_mine] = add(own[b, z_mine], midz[b]).astype(BF16)
            c_yz(b).start()
            c_leafy(b).wait_recv()
            own[b, y_mine] = add(own[b, y_mine], leafy[b]).astype(BF16)
            c_midy(b).start()

    def lag4(b):
        @pl.when(mid)
        def _():
            c_yz(b).wait_recv()
            out_all[b, half + z_mine] = add(own[b, z_mine], yz[b]).astype(BF16)
            c_totz(b).start()
            c_lz(b, 0).start()
            finish(b, z_mine)
            c_midy(b).wait_recv()
            out_all[b, half + y_mine] = add(own[b, y_mine], midy[b]).astype(BF16)
            c_toty(b).start()
            c_boty(b).start()
            finish(b, y_mine)

    def lag5(b):
        @pl.when(mid)
        def _():
            c_totz(b).wait_recv()
            c_lz(b, 1).start()
            finish(b, z_other)
            c_boty(b).wait_recv()
            finish(b, y_other)

        @pl.when(leaf)
        def _():
            c_toty(b).wait_recv()
            c_boty(b).start()
            finish(b, y_mine)
            c_lz(b, 0).wait_recv()
            finish(b, z_mine)

    def lag6(b):
        @pl.when(leaf)
        def _():
            c_boty(b).wait_recv()
            finish(b, y_other)
            c_lz(b, 1).wait_recv()
            finish(b, z_other)

    def vector_steps(t):
        @pl.when(t == 1)
        def _():
            c_vec(0).wait_recv()
            vec[1] = vec[0] + vrecv[0]
            c_vec(1).start()

        @pl.when(t == 2)
        def _():
            c_vec(1).wait_recv()
            vec[2] = vec[1] + vrecv[1]

            @pl.when(leaf)
            def _():
                c_vec(2).start()

        @pl.when((t == 3) & mid)
        def _():
            c_vec(2).wait_recv()
            vec[3] = vec[2] + vrecv[2]
            c_vec(3).start()

        @pl.when((t == 4) & mid)
        def _():
            c_vec(3).wait_recv()
            vec[4] = vec[3] + vrecv[3]
            c_vec(4).start()
            out_vec[...] = vec[4]

        @pl.when((t == 5) & leaf)
        def _():
            c_vec(4).wait_recv()
            out_vec[...] = vrecv[4]

        @pl.when(t == nb)
        def _():
            c_nrm().start()

    stages = (weight_block, lag1, lag2, lag3, lag4, lag5, lag6)

    def step(t, carry):
        for lag in (1, 0, 2, 3, 4, 5, 6):
            stage = stages[lag]

            @pl.when((t >= lag) & (t - lag < nb))
            def _(lag=lag, stage=stage):
                stage(t - lag)

        vector_steps(t)
        return carry

    lax.fori_loop(0, nb + len(stages) - 1, step, 0)

    c_nrm().wait_recv()
    out_nrm[...] = nrm[...] + nrecv[...]
    c_nrm().wait_send()
    c_vec(0).wait_send()
    c_vec(1).wait_send()
    c_core(nb - 2).wait_send()
    c_core(nb - 1).wait_send()

    @pl.when(leaf)
    def _():
        c_vec(2).wait_send()

    @pl.when(mid)
    def _():
        c_vec(3).wait_send()
        c_vec(4).wait_send()

    def drain(b, carry):
        c_yred(b).wait_send()
        c_boty(b).wait_send()
        for k in range(PIECES):
            c_ag(b, k).wait()

        @pl.when(leaf)
        def _():
            c_leafy(b).wait_send()
            c_leafz(b).wait_send()

        @pl.when(mid)
        def _():
            c_midy(b).wait_send()
            c_midz(b).wait_send()
            c_yz(b).wait_send()
            c_toty(b).wait_send()
            c_totz(b).wait_send()
            c_lz(b, 0).wait_send()
            c_lz(b, 1).wait_send()

        return carry

    lax.fori_loop(0, nb, drain, 0)


def gradient_call(a, b, small, stay):
    n_mb, seq, d = a.shape[1:]
    nb = 12 * SPLITS
    rows = d // (2 * PIECES * SPLITS)
    summed = (nb, 2 * PIECES, rows, d)
    vmem = pl.BlockSpec(memory_space=pltpu.VMEM)
    hbm = pl.BlockSpec(memory_space=pl.ANY)
    dma = pltpu.SemaphoreType.DMA

    def slots(*lead):
        return pltpu.VMEM(lead + (rows, d), BF16)

    return pl.pallas_call(
        functools.partial(gradient_kernel, nb),
        out_shape=(
            pltpu.VMEM(summed, BF16) if stay else jax.ShapeDtypeStruct(summed, BF16),
            jax.ShapeDtypeStruct((16, d), F32),
            jax.ShapeDtypeStruct((n_mb, 8, 128), F32),
        ),
        in_specs=[hbm, hbm, vmem],
        out_specs=(vmem, vmem, vmem),
        scratch_shapes=[
            pltpu.VMEM((2, n_mb, seq, d), BF16),
            pltpu.VMEM((2, n_mb, seq, d), BF16),
            slots(nb, PIECES),
            slots(2, PIECES),
            slots(nb, PIECES),
            slots(nb),
            slots(nb),
            slots(nb, 2),
            slots(nb),
            slots(nb),
            slots(nb),
            pltpu.VMEM((5, 16, d), F32),
            pltpu.VMEM((5, 16, d), F32),
            pltpu.VMEM((n_mb, 8, 128), F32),
            pltpu.VMEM((n_mb, 8, 128), F32),
            dma((2, 2)),
            dma((2,)),
            dma((nb,)),
        ]
        + [dma((nb,)) for _ in range(18)]
        + [dma((2, nb)), dma((2, nb)), dma((PIECES, nb)), dma((PIECES, nb)), dma((5,)), dma((5,)), dma, dma],
        compiler_params=pltpu.CompilerParams(
            collective_id=1, has_side_effects=True, vmem_limit_bytes=(44 if stay else 60) * 2**20
        ),
        cost_estimate=pl.CostEstimate(
            flops=24 * n_mb * seq * d * d, bytes_accessed=64 * 2**20, transcendentals=0
        ),
    )(a, b, small)


def widen_kernel(
    stay,
    blocks,
    y_in,
    dx_in,
    vec,
    nrm,
    out_y,
    out_dx,
    gain1,
    bias1,
    w_qkv,
    b_qkv,
    w_dense,
    b_dense,
    gain2,
    bias2,
    w_in,
    b_in,
    w_out,
    b_out,
    norms,
    narrow,
    wide,
    held,
    isem,
    osem,
    csem,
):
    d = wide.shape[2]
    reads = [
        pltpu.make_async_copy(blocks.at[pl.ds(w * SPLITS, SPLITS)], narrow.at[w % 4], isem.at[w % 4])
        for w in range(12)
    ]
    targets = [w_in.at[0, :, pl.ds(k * d, d)] for k in range(4)]
    targets += [w_out.at[0, pl.ds(k * d, d)] for k in range(4)]
    targets += [w_qkv.at[0, :, pl.ds(k * d, d)] for k in range(3)]
    targets += [w_dense.at[0]]
    writes = [pltpu.make_async_copy(wide.at[w], targets[w], osem.at[w]) for w in range(12)]
    if stay:
        copies = [
            pltpu.make_async_copy(y_in, out_y, csem.at[2]),
            pltpu.make_async_copy(dx_in, out_dx, csem.at[3]),
        ]
        fetch = []
    else:
        copies = [
            pltpu.make_async_copy(held.at[0], out_y, csem.at[2]),
            pltpu.make_async_copy(held.at[1], out_dx, csem.at[3]),
        ]
        fetch = [
            pltpu.make_async_copy(y_in, held.at[0], csem.at[0]),
            pltpu.make_async_copy(dx_in, held.at[1], csem.at[1]),
        ]
    for c in (copies if stay else fetch) + reads[:3]:
        c.start()
    for row, refs in ((0, (gain1,)), (1, (bias1,)), (2, (gain2,)), (3, (bias2,)), (7, (b_dense, b_out))):
        for ref in refs:
            ref[...] = vec[row : row + 1, :]
    for k in range(3):
        b_qkv[:, k * d : (k + 1) * d] = vec[4 + k : 5 + k, :]
    for k in range(4):
        b_in[:, k * d : (k + 1) * d] = vec[8 + k : 9 + k, :]
    for m in range(nrm.shape[0]):
        norms[m] = jnp.sum(nrm[m])
    for w in range(12):
        if w + 3 < 12:
            reads[w + 3].start()
        reads[w].wait()
        wide[w] = narrow[w % 4].astype(F32).reshape(d, d)
        writes[w].start()
    for c in fetch:
        c.wait()
    for c in [] if stay else copies:
        c.start()
    for c in writes + copies:
        c.wait()


def widen_call(blocks, y, dx, vec, nrm, stay):
    d = y.shape[3]
    vmem = pl.BlockSpec(memory_space=pltpu.VMEM)
    hbm = pl.BlockSpec(memory_space=pl.ANY)
    dma = pltpu.SemaphoreType.DMA

    def row(k):
        return jax.ShapeDtypeStruct((1, k * d), F32)

    def matrix(r, c):
        return jax.ShapeDtypeStruct((1, r * d, c * d), F32)

    same = jax.ShapeDtypeStruct(y.shape, BF16)
    return pl.pallas_call(
        functools.partial(widen_kernel, stay),
        out_shape=(same, same, row(1), row(1), matrix(1, 3), row(3), matrix(1, 1), row(1))
        + (row(1), row(1), matrix(1, 4), row(4), matrix(4, 1), row(1))
        + (jax.ShapeDtypeStruct(nrm.shape[:1], F32),),
        in_specs=[hbm, hbm, hbm, vmem, vmem],
        out_specs=(hbm, hbm) + (vmem, vmem, hbm, vmem, hbm, vmem) * 2 + (pl.BlockSpec(memory_space=pltpu.SMEM),),
        scratch_shapes=[
            pltpu.VMEM((4, SPLITS) + blocks.shape[1:], BF16),
            pltpu.VMEM((12, d, d), F32),
            pltpu.VMEM((1, 8, 128) if stay else (2,) + y.shape, BF16),
            dma((4,)),
            dma((12,)),
            dma((4,)),
        ],
        compiler_params=pltpu.CompilerParams(vmem_limit_bytes=42 * 2**20),
        cost_estimate=pl.CostEstimate(flops=12 * d * d, bytes_accessed=72 * d * d, transcendentals=0),
    )(blocks, y, dx, vec, nrm)


def on_device(size, inputs, cotangent, lengths, *params):
    n_mb, seq, d = inputs.shape
    tables = jnp.asarray(rotary_tables(seq))
    out_y, out_dx, a, b, small = section_call(lengths, inputs, cotangent, params, tables)
    stay = size == 16
    blocks, vectors, nrm = gradient_call(a, b, small, stay)
    if stay:
        blocks, out_y, out_dx = [
            pltpu.with_memory_space_constraint(v, pltpu.VMEM) for v in (blocks, out_y, out_dx)
        ]
    else:
        groups = [[g * 16 + r for g in range(size // 16)] for r in range(16)]
        blocks, vectors = [lax.psum(v, "dp", axis_index_groups=groups) for v in (blocks, vectors)]
    return widen_call(blocks, out_y, out_dx, vectors, nrm, stay)


def solution(mesh):
    matrix, vector = P("pipe", None, None), P("pipe", None)
    weights = (vector, vector, matrix, vector, matrix, vector) * 2
    tokens = P("dp", None, None)
    return jax.shard_map(
        functools.partial(on_device, mesh.shape["dp"]),
        mesh=mesh,
        in_specs=(tokens, tokens, P("dp")) + weights,
        out_specs=(P("pipe", "dp", None, None),) * 2 + weights + (P("dp"),),
        check_vma=False,
    )
```
